32 devices in a mesh: seq: 16 (over z, x, core), tensor: 2 (over y).
Axes of the slice: x: 2, y: 2, z: 4, core: 2. Of those that a mesh axis runs over, the one named last changes fastest.
Arguments:
- keyval: bfloat16 [8192, 8192], P('seq', 'tensor'), may hold values from -6 to 6
- gating: bfloat16 [8192, 8192], P('seq', 'tensor'), may hold values from -6 to 6
- skip_gain: float32 [8192], P('tensor'), may hold values from -4 to 4
- filter_values: float32 [2, 32, 4, 16, 8192], P(None, None, None, 'seq', 'tensor'), may hold values from -12 to 12
- blocks: int32 [64, 32], P('tensor'), may hold values from 0 to 127, as said below
- out_weight: bfloat16 [8192, 8192], P('seq', 'tensor'), may hold values from -0.0625 to 0.0625
Outputs:
- mixed: bfloat16 [8192, 8192], P('seq', 'tensor')
The draws below stay inside these ranges and needn't reach their ends.
Inputs may be any that keep to these rules, and one draw needn't show every extreme that they name: Each row names 32 different blocks.
All inputs are finite; a program needn't handle non-finite values.
Results may differ from the reference program's by a relative error of at most 0.0063.
Values may be sent and summed in bfloat16 or wider, within the bound.
No kernel may reach another device: no remote copies, remote signals or barrier semaphores. Data moves between devices by JAX's collectives and lax.ppermute only.
A program may use at most 192 MiB of HBM per device.

```python
import math
import jax
import jax.numpy as jnp
from jax import lax

D = 8192
GROUP = 128
BLOCK = 64
TOK_DEV = 512
TOKENS = 8192
NBLK = 128
KEEP = 32
NGROUP = 64
N_SEQ = 16


def draw_blocks(key, part):
    row_keys = jax.random.split(jax.random.fold_in(key, 11), NGROUP)
    orders = jax.vmap(lambda row_key: jax.random.permutation(row_key, NBLK))(row_keys)
    chosen = orders[:, :KEEP].astype(jnp.int32)
    top_row = jax.random.randint(jax.random.fold_in(key, 12), (), 0, NGROUP)
    low_row = (top_row + 1) % NGROUP
    has_top = jnp.any(chosen == NBLK - 1, axis=1)
    has_low = jnp.any(chosen == 0, axis=1)
    row_index = jnp.arange(NGROUP, dtype=jnp.int32)
    force_top = jnp.logical_and(row_index == top_row, jnp.logical_not(has_top))
    force_low = jnp.logical_and(row_index == low_row, jnp.logical_not(has_low))
    first_column = jnp.where(force_top, NBLK - 1, jnp.where(force_low, 0, chosen[:, 0]))
    return chosen.at[:, 0].set(first_column.astype(jnp.int32))


def level_of(rng, extent, shards, least, top_value):
    factor_of, own = 1.0, jax.random.fold_in(rng, 6)
    for position, parts in shards:
        draws = jnp.exp(jax.random.uniform(jax.random.fold_in(own, position), (parts,), jnp.float32, least / len(shards), top_value / len(shards)))
        factor_of = factor_of * jnp.repeat(draws, extent[position] // parts).reshape([-1 if axis == position else 1 for axis in range(len(extent))])
    return factor_of


def centred(rng, dims, spread, bound, cuts=(), kind=jnp.bfloat16):
    loudness = level_of(rng, dims, cuts, -0.22, 0.18) if cuts else 1.0
    array = jax.random.normal(rng, dims, jnp.float32) * spread * loudness
    return jnp.minimum(jnp.maximum(array, -bound), bound).astype(kind)


def setup_inputs(seed: int = 0) -> dict:
    seeds = jax.random.split(jax.random.key(seed), 7)
    return {
        "keyval": centred(seeds[0], (TOKENS, D), 1.0, 6.0, ((0, 16), (1, 2))),
        "gating": centred(seeds[1], (TOKENS, D), 1.0, 6.0, ((0, 16), (1, 2))),
        "skip_gain": centred(seeds[2], (D,), 1.0, 4.0, ((0, 2),), jnp.float32),
        "filter_values": centred(seeds[3], (2, KEEP, BLOCK // N_SEQ, N_SEQ, D), 2.0, 12.0, ((3, 16), (4, 2)), jnp.float32),
        "blocks": draw_blocks(jax.random.fold_in(seeds[6], 71), 0),
        "out_weight": centred(seeds[5], (D, D), D ** -0.5, 0.0625, ((0, 16), (1, 2))),
    }


HIGHEST = lax.Precision.HIGHEST


def tables(first_index, second_index, length):
    phase = (first_index * second_index) % length
    angle = (2.0 * math.pi / length) * phase.astype(jnp.float32)
    return jnp.cos(angle), jnp.sin(angle)


def rounded(value):
    return lax.optimization_barrier(value.astype(jnp.bfloat16)).astype(jnp.float32)


def group_conv(keyval_group, block_list, filter_group):
    repeat = BLOCK // N_SEQ
    signal = keyval_group.astype(jnp.float32).reshape(N_SEQ, TOK_DEV, GROUP)
    cycle_index = jnp.arange(N_SEQ, dtype=jnp.int32)
    local_index = jnp.arange(TOK_DEV, dtype=jnp.int32)
    cosine_cycle, sine_cycle = tables(cycle_index[:, None], cycle_index[None, :], N_SEQ)
    first_real = jnp.einsum('pa,ajc->pjc', cosine_cycle, signal, precision=HIGHEST)
    first_imaginary = -jnp.einsum('pa,ajc->pjc', sine_cycle, signal, precision=HIGHEST)
    cosine_twist, sine_twist = tables(cycle_index[:, None], local_index[None, :], TOKENS)
    cosine_twist = cosine_twist[:, :, None]
    sine_twist = sine_twist[:, :, None]
    twist_real = rounded(first_real * cosine_twist + first_imaginary * sine_twist)
    twist_imaginary = rounded(first_imaginary * cosine_twist - first_real * sine_twist)
    kept_rows = (block_list[:, None] * repeat + jnp.arange(repeat, dtype=jnp.int32)[None, :]).reshape(-1)
    cosine_kept, sine_kept = tables(kept_rows[:, None], local_index[None, :], TOK_DEV)
    spectrum_real = (jnp.einsum('qj,pjc->pqc', cosine_kept, twist_real, precision=HIGHEST)
                     + jnp.einsum('qj,pjc->pqc', sine_kept, twist_imaginary, precision=HIGHEST))
    spectrum_imaginary = (jnp.einsum('qj,pjc->pqc', cosine_kept, twist_imaginary, precision=HIGHEST)
                          - jnp.einsum('qj,pjc->pqc', sine_kept, twist_real, precision=HIGHEST))
    filter_real = filter_group[0].reshape(KEEP * repeat, N_SEQ, GROUP).transpose(1, 0, 2)
    filter_imaginary = filter_group[1].reshape(KEEP * repeat, N_SEQ, GROUP).transpose(1, 0, 2)
    product_real = filter_real * spectrum_real - filter_imaginary * spectrum_imaginary
    product_imaginary = filter_real * spectrum_imaginary + filter_imaginary * spectrum_real
    back_real = (jnp.einsum('qj,pqc->pjc', cosine_kept, product_real, precision=HIGHEST)
                 - jnp.einsum('qj,pqc->pjc', sine_kept, product_imaginary, precision=HIGHEST))
    back_imaginary = (jnp.einsum('qj,pqc->pjc', sine_kept, product_real, precision=HIGHEST)
                      + jnp.einsum('qj,pqc->pjc', cosine_kept, product_imaginary, precision=HIGHEST))
    turned_real = rounded(back_real * cosine_twist - back_imaginary * sine_twist)
    turned_imaginary = rounded(back_real * sine_twist + back_imaginary * cosine_twist)
    convolved = (jnp.einsum('pa,pjc->ajc', cosine_cycle, turned_real, precision=HIGHEST)
                 - jnp.einsum('pa,pjc->ajc', sine_cycle, turned_imaginary, precision=HIGHEST)) / TOKENS
    return convolved.astype(jnp.bfloat16).reshape(TOKENS, GROUP)


def group_step(items):
    return group_conv(items[0], items[1], items[2])


def reference(keyval, gating, skip_gain, filter_values, blocks, out_weight):
    grouped = keyval.reshape(TOKENS, NGROUP, GROUP).transpose(1, 0, 2)
    filters = filter_values.reshape(2, KEEP, BLOCK // N_SEQ, N_SEQ, NGROUP, GROUP).transpose(4, 0, 1, 2, 3, 5)
    convolved = lax.map(group_step, (grouped, blocks, filters))
    convolved = convolved.transpose(1, 0, 2).reshape(TOKENS, D)
    hidden = (gating.astype(jnp.float32) * (convolved.astype(jnp.float32)
              + skip_gain[None, :] * keyval.astype(jnp.float32))).astype(jnp.bfloat16)
    return jnp.dot(hidden, out_weight, preferred_element_type=jnp.float32).astype(jnp.bfloat16)
```

```python
import functools
import math

import jax
import jax.numpy as jnp
from jax import lax
from jax.experimental import pallas as pl
from jax.experimental.pallas import tpu as pltpu
from jax.sharding import PartitionSpec as P

BLOCK = 64
ROWS = 16
VMEM = 48 * 2**20
F32 = jnp.float32
BF16 = jnp.bfloat16


def tables(first_index, second_index, length):
    phase = first_index * second_index % length
    angle = 2.0 * math.pi / length * phase.astype(F32)
    return (jnp.cos(angle), jnp.sin(angle))


def real_forward(values):
    n = len(values)
    if n == 2:
        return [(values[0] + values[1], None), (values[0] - values[1], None)]
    even, odd = real_forward(values[0::2]), real_forward(values[1::2])
    half = n // 2
    out = [None] * (half + 1)
    for p in range(half // 2 + 1):
        (er, ei), (dr, di) = even[p], odd[p]
        if p == 0:
            out[0], out[half] = (er + dr, None), (er - dr, None)
        elif 2 * p == half:
            out[p] = (er, -dr)
        else:
            c, s = math.cos(2 * math.pi * p / n), math.sin(2 * math.pi * p / n)
            tr, ti = dr * c + di * s, di * c - dr * s
            out[p], out[half - p] = (er + tr, ei + ti), (er - tr, ti - ei)
    return out


def real_inverse(freqs):
    half = len(freqs) - 1
    if half == 1:
        return [freqs[0][0] + freqs[1][0], freqs[0][0] - freqs[1][0]]
    n = 2 * half
    even, odd = [None] * (half // 2 + 1), [None] * (half // 2 + 1)
    for p in range(half // 2 + 1):
        (ar, ai), (br, bi) = freqs[p], freqs[half - p]
        if p == 0:
            even[0], odd[0] = (ar + br, None), (ar - br, None)
        elif 2 * p == half:
            even[p], odd[p] = (ar + ar, None), (-(ai + ai), None)
        else:
            c, s = math.cos(2 * math.pi * p / n), math.sin(2 * math.pi * p / n)
            dr, di = ar - br, ai + bi
            even[p], odd[p] = (ar + br, ai - bi), (dr * c - di * s, dr * s + di * c)
    out = [None] * n
    out[0::2], out[1::2] = real_inverse(even), real_inverse(odd)
    return out


def conv_kernel(twist_ref, ahead_ref, back_ref, x_ref, filter_ref, out_ref, first_ref, turned_ref):
    cycle, tokens, unit = x_ref.shape
    kept = filter_ref.shape[2] // 2
    per = max(1, 256 // unit)
    width = per * unit

    def twist(rows):
        block = twist_ref[rows, :]
        return [
            (block[:, p : p + 1], block[:, cycle + p : cycle + p + 1]) for p in range(cycle)
        ]

    def ahead(step, carry):
        start = pl.multiple_of(step * ROWS, ROWS)
        rows = pl.ds(start, ROWS)
        freqs = real_forward([x_ref[a, rows, :].astype(F32) for a in range(cycle)])
        for p, (c, s) in enumerate(twist(rows)):
            real, imaginary = freqs[min(p, cycle - p)]
            if imaginary is None:
                fr, fi = real * c, -(real * s)
            elif 2 * p > cycle:
                fr, fi = real * c - imaginary * s, -(imaginary * c + real * s)
            else:
                fr, fi = real * c + imaginary * s, imaginary * c - real * s
            lanes = slice(p * unit, (p + 1) * unit)
            first_ref[rows, lanes] = fr.astype(BF16)
            first_ref[pl.ds(tokens + start, ROWS), lanes] = fi.astype(BF16)
        return carry

    lax.fori_loop(0, tokens // ROWS, ahead, 0)

    def middle(step, carry):
        lanes = pl.ds(pl.multiple_of(step * width, width), width)
        spectrum = jnp.dot(ahead_ref[0], first_ref[:, lanes], preferred_element_type=F32)
        reals, imaginaries = [], []
        for u in range(per):
            part = filter_ref[step * per + u, 0].astype(F32)
            hr, hi = part[:kept], part[kept:]
            own = slice(u * unit, (u + 1) * unit)
            sr, si = spectrum[:kept, own], spectrum[kept:, own]
            reals.append(hr * sr - hi * si)
            imaginaries.append(hr * si + hi * sr)
        product = jnp.concatenate(
            [jnp.concatenate(reals, axis=1), jnp.concatenate(imaginaries, axis=1)], axis=0
        ).astype(BF16)
        turned_ref[:, lanes] = jnp.dot(back_ref[0], product, preferred_element_type=F32)
        return carry

    lax.fori_loop(0, cycle // per, middle, 0)

    def behind(step, carry):
        start = pl.multiple_of(step * ROWS, ROWS)
        rows = pl.ds(start, ROWS)
        parts = []
        for p, (c, s) in enumerate(twist(rows)):
            lanes = slice(p * unit, (p + 1) * unit)
            br = turned_ref[rows, lanes]
            bi = turned_ref[pl.ds(tokens + start, ROWS), lanes]
            parts.append(
                (
                    (br * c - bi * s).astype(BF16).astype(F32),
                    (br * s + bi * c).astype(BF16).astype(F32),
                )
            )
        half = cycle // 2
        freqs = [(parts[0][0] * 2.0, None)]
        for p in range(1, half):
            (ur, ui), (vr, vi) = parts[p], parts[cycle - p]
            freqs.append((ur + vr, ui - vi))
        freqs.append((parts[half][0] * 2.0, None))
        scale = 0.5 / (cycle * tokens)
        for a, value in enumerate(real_inverse(freqs)):
            out_ref[a, rows, :] = (value * scale).astype(BF16)
        return carry

    lax.fori_loop(0, tokens // ROWS, behind, 0)


def convolve(chunk, twist, ahead, back, signal, filters):
    cycle, tokens, unit = signal.shape
    kept = filters.shape[2] // 2
    flops = 4 * 2 * kept * 2 * tokens * cycle * unit
    return pl.pallas_call(
        conv_kernel,
        grid=(1,),
        out_shape=jax.ShapeDtypeStruct(signal.shape, BF16),
        in_specs=[
            pl.BlockSpec(twist.shape, lambda i: (0, 0)),
            pl.BlockSpec((1, *ahead.shape[1:]), lambda i: (chunk, 0, 0)),
            pl.BlockSpec((1, *back.shape[1:]), lambda i: (chunk, 0, 0)),
            pl.BlockSpec(signal.shape, lambda i: (0, 0, 0)),
            pl.BlockSpec((cycle, 1, 2 * kept, unit), lambda i: (0, chunk, 0, 0)),
        ],
        out_specs=pl.BlockSpec(signal.shape, lambda i: (0, 0, 0)),
        scratch_shapes=[
            pltpu.VMEM((2 * tokens, cycle * unit), BF16),
            pltpu.VMEM((2 * tokens, cycle * unit), F32),
        ],
        compiler_params=pltpu.CompilerParams(vmem_limit_bytes=VMEM),
        cost_estimate=pl.CostEstimate(
            flops=flops, bytes_accessed=16 * signal.size, transcendentals=0
        ),
        name="convolve",
    )(twist, ahead, back, signal, filters)


def pack_kernel(unit, x_ref, out_ref):
    for d in range(out_ref.shape[0]):
        out_ref[d] = x_ref[:, d * unit : (d + 1) * unit]


def pack_signal(keyval, chunk, cycle, unit):
    tokens = keyval.shape[0]
    wide = max(1, min(cycle, 512 // unit))
    steps = cycle // wide
    return pl.pallas_call(
        functools.partial(pack_kernel, unit),
        grid=(steps,),
        out_shape=jax.ShapeDtypeStruct((cycle, tokens, unit), BF16),
        in_specs=[pl.BlockSpec((tokens, wide * unit), lambda i: (0, chunk * steps + i))],
        out_specs=pl.BlockSpec((wide, tokens, unit), lambda i: (i, 0, 0)),
        compiler_params=pltpu.CompilerParams(vmem_limit_bytes=VMEM),
        cost_estimate=pl.CostEstimate(
            flops=0, bytes_accessed=4 * tokens * cycle * unit, transcendentals=0
        ),
        name="pack_signal",
    )(keyval)


def pack_filter_kernel(unit, f_ref, out_ref):
    for d in range(out_ref.shape[0]):
        out_ref[d, 0] = f_ref[:, 0, d * unit : (d + 1) * unit].astype(BF16)


def pack_filters(filter_values, cycle, chunks, unit):
    channels = filter_values.shape[-1]
    rows = filter_values.size // channels
    flat = filter_values.reshape(rows, 1, channels)
    wide = max(1, min(cycle, 512 // unit))
    steps = cycle // wide
    return pl.pallas_call(
        functools.partial(pack_filter_kernel, unit),
        grid=(chunks, steps),
        out_shape=jax.ShapeDtypeStruct((cycle, chunks, rows, unit), BF16),
        in_specs=[pl.BlockSpec((rows, 1, wide * unit), lambda g, i: (0, 0, g * steps + i))],
        out_specs=pl.BlockSpec((wide, 1, rows, unit), lambda g, i: (i, g, 0, 0)),
        compiler_params=pltpu.CompilerParams(vmem_limit_bytes=VMEM),
        cost_estimate=pl.CostEstimate(
            flops=0, bytes_accessed=6 * filter_values.size, transcendentals=0
        ),
        name="pack_filters",
    )(flat)


def gate_kernel(unit, c_ref, x_ref, g_ref, s_ref, out_ref):
    for d in range(c_ref.shape[0]):
        lanes = slice(d * unit, (d + 1) * unit)
        direct = s_ref[0:1, lanes] * x_ref[:, lanes].astype(F32)
        value = g_ref[:, lanes].astype(F32) * (c_ref[d].astype(F32) + direct)
        out_ref[:, lanes] = value.astype(BF16)


def gate(convolved, keyval, gating, skip_gain, chunk):
    cycle, tokens, unit = convolved.shape
    wide = max(1, min(cycle, 512 // unit))
    steps = cycle // wide
    lanes = wide * unit
    return pl.pallas_call(
        functools.partial(gate_kernel, unit),
        grid=(steps,),
        out_shape=jax.ShapeDtypeStruct((tokens, cycle * unit), BF16),
        in_specs=[
            pl.BlockSpec((wide, tokens, unit), lambda i: (i, 0, 0)),
            pl.BlockSpec((tokens, lanes), lambda i: (0, chunk * steps + i)),
            pl.BlockSpec((tokens, lanes), lambda i: (0, chunk * steps + i)),
            pl.BlockSpec((1, lanes), lambda i: (0, chunk * steps + i)),
        ],
        out_specs=pl.BlockSpec((tokens, lanes), lambda i: (0, i)),
        compiler_params=pltpu.CompilerParams(vmem_limit_bytes=VMEM),
        cost_estimate=pl.CostEstimate(
            flops=0, bytes_accessed=8 * convolved.size, transcendentals=0
        ),
        name="gate",
    )(convolved, keyval, gating, skip_gain.reshape(1, -1))


def mix_kernel(pieces, start_ref, *refs):
    w_ref, out_ref = refs[pieces], refs[pieces + 1]
    total = None
    for k in range(pieces):
        depth = refs[k].shape[1]
        start = pl.multiple_of(start_ref[k], depth)
        part = jnp.dot(
            refs[k][...], w_ref[pl.ds(start, depth), :], preferred_element_type=F32
        )
        total = part if total is None else total + part
    out_ref[...] = total.astype(BF16)


def mix(hidden, starts, weight):
    tokens = hidden[0].shape[0]
    depth, columns = weight.shape
    tile = min(256, columns)
    pieces = len(hidden)
    return pl.pallas_call(
        functools.partial(mix_kernel, pieces),
        grid=(columns // tile,),
        out_shape=jax.ShapeDtypeStruct((tokens, columns), BF16),
        in_specs=[pl.BlockSpec(memory_space=pltpu.SMEM)]
        + [pl.BlockSpec(h.shape, lambda i: (0, 0)) for h in hidden]
        + [pl.BlockSpec((depth, tile), lambda i: (0, i))],
        out_specs=pl.BlockSpec((tokens, tile), lambda i: (0, i)),
        compiler_params=pltpu.CompilerParams(vmem_limit_bytes=VMEM),
        cost_estimate=pl.CostEstimate(
            flops=2 * tokens * depth * columns,
            bytes_accessed=2 * depth * columns,
            transcendentals=0,
        ),
        name="mix",
    )(starts, *hidden, weight)


def body(keyval, gating, skip_gain, filter_values, blocks, out_weight):
    cycle = lax.axis_size("seq")
    place = lax.axis_index("seq")
    peers = lax.axis_size("tensor")
    side = lax.axis_index("tensor")
    tokens, channels = keyval.shape
    repeat = BLOCK // cycle
    groups_local = blocks.shape[0]
    group_width = channels // groups_local
    narrow = channels // cycle
    unit = min(narrow, group_width)
    chunks = narrow // unit

    weight = lax.all_gather(out_weight, "seq", axis=0, tiled=True)

    exchange = functools.partial(
        lax.all_to_all, axis_name="seq", split_axis=0, concat_axis=0, tiled=True
    )
    signals = [exchange(pack_signal(keyval, g, cycle, unit)) for g in range(chunks)]
    filters = exchange(pack_filters(filter_values, cycle, chunks, unit))

    group = (jnp.arange(chunks, dtype=jnp.int32) * cycle + place) * unit // group_width
    kept_blocks = jnp.take(blocks, group, axis=0)
    kept_rows = (
        kept_blocks[:, :, None] * repeat + jnp.arange(repeat, dtype=jnp.int32)
    ).reshape(chunks, -1)
    local_index = jnp.arange(tokens, dtype=jnp.int32)
    cosine, sine = tables(kept_rows[:, :, None], local_index[None, None, :], tokens)
    ahead = jnp.concatenate(
        [jnp.concatenate([cosine, sine], axis=2), jnp.concatenate([-sine, cosine], axis=2)],
        axis=1,
    ).astype(BF16)
    cosine, sine = tables(kept_rows[:, None, :], local_index[None, :, None], tokens)
    back = jnp.concatenate(
        [jnp.concatenate([cosine, -sine], axis=2), jnp.concatenate([sine, cosine], axis=2)],
        axis=1,
    ).astype(BF16)
    cycle_index = jnp.arange(cycle, dtype=jnp.int32)
    twist = jnp.concatenate(
        tables(local_index[:, None], cycle_index[None, :], cycle * tokens), axis=1
    )

    hidden, starts = [], []
    for g in range(chunks):
        done = exchange(convolve(g, twist, ahead, back, signals[g], filters))
        own = gate(done, keyval, gating, skip_gain, g)
        for shift in range(peers):
            if shift == 0:
                piece = own
            else:
                piece = lax.ppermute(
                    own, "tensor", [(t, (t + shift) % peers) for t in range(peers)]
                )
            hidden.append(piece)
            source = lax.rem(side + peers - shift, peers)
            starts.append(source * channels + g * cycle * unit)
    return mix(hidden, jnp.stack(starts).astype(jnp.int32), weight)


def solution(mesh):
    placed = (
        P("seq", "tensor"),
        P("seq", "tensor"),
        P("tensor"),
        P(None, None, None, "seq", "tensor"),
        P("tensor", None),
        P("seq", "tensor"),
    )
    return jax.shard_map(
        body, mesh=mesh, in_specs=placed, out_specs=P("seq", "tensor"), check_vma=False
    )
```

```python
import functools
import math

import jax
import jax.numpy as jnp
from jax import lax
from jax.experimental import pallas as pl
from jax.experimental.pallas import tpu as pltpu
from jax.sharding import PartitionSpec as P

BLOCK = 64
ROWS = 16
VMEM = 48 * 2**20
F32 = jnp.float32
BF16 = jnp.bfloat16


def tables(first_index, second_index, length):
    phase = first_index * second_index % length
    angle = 2.0 * math.pi / length * phase.astype(F32)
    return (jnp.cos(angle), jnp.sin(angle))


def real_forward(values):
    n = len(values)
    if n == 2:
        return [(values[0] + values[1], None), (values[0] - values[1], None)]
    even, odd = real_forward(values[0::2]), real_forward(values[1::2])
    half = n // 2
    out = [None] * (half + 1)
    for p in range(half // 2 + 1):
        (er, ei), (dr, di) = even[p], odd[p]
        if p == 0:
            out[0], out[half] = (er + dr, None), (er - dr, None)
        elif 2 * p == half:
            out[p] = (er, -dr)
        else:
            c, s = math.cos(2 * math.pi * p / n), math.sin(2 * math.pi * p / n)
            tr, ti = dr * c + di * s, di * c - dr * s
            out[p], out[half - p] = (er + tr, ei + ti), (er - tr, ti - ei)
    return out


def real_inverse(freqs):
    half = len(freqs) - 1
    if half == 1:
        return [freqs[0][0] + freqs[1][0], freqs[0][0] - freqs[1][0]]
    n = 2 * half
    even, odd = [None] * (half // 2 + 1), [None] * (half // 2 + 1)
    for p in range(half // 2 + 1):
        (ar, ai), (br, bi) = freqs[p], freqs[half - p]
        if p == 0:
            even[0], odd[0] = (ar + br, None), (ar - br, None)
        elif 2 * p == half:
            even[p], odd[p] = (ar + ar, None), (-(ai + ai), None)
        else:
            c, s = math.cos(2 * math.pi * p / n), math.sin(2 * math.pi * p / n)
            dr, di = ar - br, ai + bi
            even[p], odd[p] = (ar + br, ai - bi), (dr * c - di * s, dr * s + di * c)
    out = [None] * n
    out[0::2], out[1::2] = real_inverse(even), real_inverse(odd)
    return out


def conv_kernel(twist_ref, ahead_ref, back_ref, x_ref, filter_ref, out_ref, first_ref, turned_ref):
    cycle, tokens, unit = x_ref.shape
    kept = filter_ref.shape[2] // 2
    per = max(1, 256 // unit)
    width = per * unit

    def twist(rows):
        block = twist_ref[rows, :]
        return [
            (block[:, p : p + 1], block[:, cycle + p : cycle + p + 1]) for p in range(cycle)
        ]

    def ahead(step, carry):
        start = pl.multiple_of(step * ROWS, ROWS)
        rows = pl.ds(start, ROWS)
        freqs = real_forward([x_ref[a, rows, :].astype(F32) for a in range(cycle)])
        for p, (c, s) in enumerate(twist(rows)):
            real, imaginary = freqs[min(p, cycle - p)]
            if imaginary is None:
                fr, fi = real * c, -(real * s)
            elif 2 * p > cycle:
                fr, fi = real * c - imaginary * s, -(imaginary * c + real * s)
            else:
                fr, fi = real * c + imaginary * s, imaginary * c - real * s
            lanes = slice(p * unit, (p + 1) * unit)
            first_ref[rows, lanes] = fr.astype(BF16)
            first_ref[pl.ds(tokens + start, ROWS), lanes] = fi.astype(BF16)
        return carry

    lax.fori_loop(0, tokens // ROWS, ahead, 0)

    def middle(step, carry):
        lanes = pl.ds(pl.multiple_of(step * width, width), width)
        spectrum = jnp.dot(ahead_ref[0], first_ref[:, lanes], preferred_element_type=F32)
        reals, imaginaries = [], []
        for u in range(per):
            part = filter_ref[step * per + u, 0].astype(F32)
            hr, hi = part[:kept], part[kept:]
            own = slice(u * unit, (u + 1) * unit)
            sr, si = spectrum[:kept, own], spectrum[kept:, own]
            reals.append(hr * sr - hi * si)
            imaginaries.append(hr * si + hi * sr)
        product = jnp.concatenate(
            [jnp.concatenate(reals, axis=1), jnp.concatenate(imaginaries, axis=1)], axis=0
        ).astype(BF16)
        turned_ref[:, lanes] = jnp.dot(back_ref[0], product, preferred_element_type=F32)
        return carry

    lax.fori_loop(0, cycle // per, middle, 0)

    def behind(step, carry):
        start = pl.multiple_of(step * ROWS, ROWS)
        rows = pl.ds(start, ROWS)
        parts = []
        for p, (c, s) in enumerate(twist(rows)):
            lanes = slice(p * unit, (p + 1) * unit)
            br = turned_ref[rows, lanes]
            bi = turned_ref[pl.ds(tokens + start, ROWS), lanes]
            parts.append(
                (
                    (br * c - bi * s).astype(BF16).astype(F32),
                    (br * s + bi * c).astype(BF16).astype(F32),
                )
            )
        half = cycle // 2
        freqs = [(parts[0][0] * 2.0, None)]
        for p in range(1, half):
            (ur, ui), (vr, vi) = parts[p], parts[cycle - p]
            freqs.append((ur + vr, ui - vi))
        freqs.append((parts[half][0] * 2.0, None))
        scale = 0.5 / (cycle * tokens)
        for a, value in enumerate(real_inverse(freqs)):
            out_ref[a, rows, :] = (value * scale).astype(BF16)
        return carry

    lax.fori_loop(0, tokens // ROWS, behind, 0)


def convolve(chunk, twist, ahead, back, signal, filters):
    cycle, tokens, unit = signal.shape
    kept = filters.shape[2] // 2
    flops = 4 * 2 * kept * 2 * tokens * cycle * unit
    return pl.pallas_call(
        conv_kernel,
        grid=(1,),
        out_shape=jax.ShapeDtypeStruct(signal.shape, BF16),
        in_specs=[
            pl.BlockSpec(twist.shape, lambda i: (0, 0)),
            pl.BlockSpec((1, *ahead.shape[1:]), lambda i: (chunk, 0, 0)),
            pl.BlockSpec((1, *back.shape[1:]), lambda i: (chunk, 0, 0)),
            pl.BlockSpec(signal.shape, lambda i: (0, 0, 0)),
            pl.BlockSpec((cycle, 1, 2 * kept, unit), lambda i: (0, chunk, 0, 0)),
        ],
        out_specs=pl.BlockSpec(signal.shape, lambda i: (0, 0, 0)),
        scratch_shapes=[
            pltpu.VMEM((2 * tokens, cycle * unit), BF16),
            pltpu.VMEM((2 * tokens, cycle * unit), F32),
        ],
        compiler_params=pltpu.CompilerParams(vmem_limit_bytes=VMEM),
        cost_estimate=pl.CostEstimate(
            flops=flops, bytes_accessed=16 * signal.size, transcendentals=0
        ),
        name="convolve",
    )(twist, ahead, back, signal, filters)


def pack_kernel(unit, x_ref, out_ref):
    for d in range(out_ref.shape[0]):
        out_ref[d] = x_ref[:, d * unit : (d + 1) * unit]


def pack_signal(keyval, chunk, cycle, unit):
    tokens = keyval.shape[0]
    wide = max(1, min(cycle, 512 // unit))
    steps = cycle // wide
    return pl.pallas_call(
        functools.partial(pack_kernel, unit),
        grid=(steps,),
        out_shape=jax.ShapeDtypeStruct((cycle, tokens, unit), BF16),
        in_specs=[pl.BlockSpec((tokens, wide * unit), lambda i: (0, chunk * steps + i))],
        out_specs=pl.BlockSpec((wide, tokens, unit), lambda i: (i, 0, 0)),
        compiler_params=pltpu.CompilerParams(vmem_limit_bytes=VMEM),
        cost_estimate=pl.CostEstimate(
            flops=0, bytes_accessed=4 * tokens * cycle * unit, transcendentals=0
        ),
        name="pack_signal",
    )(keyval)


def pack_filter_kernel(unit, f_ref, out_ref):
    for d in range(out_ref.shape[0]):
        out_ref[d, 0] = f_ref[:, 0, d * unit : (d + 1) * unit].astype(BF16)


def pack_filters(filter_values, cycle, chunks, unit):
    channels = filter_values.shape[-1]
    rows = filter_values.size // channels
    flat = filter_values.reshape(rows, 1, channels)
    wide = max(1, min(cycle, 512 // unit))
    steps = cycle // wide
    return pl.pallas_call(
        functools.partial(pack_filter_kernel, unit),
        grid=(chunks, steps),
        out_shape=jax.ShapeDtypeStruct((cycle, chunks, rows, unit), BF16),
        in_specs=[pl.BlockSpec((rows, 1, wide * unit), lambda g, i: (0, 0, g * steps + i))],
        out_specs=pl.BlockSpec((wide, 1, rows, unit), lambda g, i: (i, g, 0, 0)),
        compiler_params=pltpu.CompilerParams(vmem_limit_bytes=VMEM),
        cost_estimate=pl.CostEstimate(
            flops=0, bytes_accessed=6 * filter_values.size, transcendentals=0
        ),
        name="pack_filters",
    )(flat)


def gate_kernel(unit, c_ref, x_ref, g_ref, s_ref, out_ref):
    for d in range(c_ref.shape[0]):
        lanes = slice(d * unit, (d + 1) * unit)
        direct = s_ref[0:1, lanes] * x_ref[:, lanes].astype(F32)
        value = g_ref[:, lanes].astype(F32) * (c_ref[d].astype(F32) + direct)
        out_ref[:, lanes] = value.astype(BF16)


def gate(convolved, keyval, gating, skip_gain, chunk):
    cycle, tokens, unit = convolved.shape
    wide = max(1, min(cycle, 512 // unit))
    steps = cycle // wide
    lanes = wide * unit
    return pl.pallas_call(
        functools.partial(gate_kernel, unit),
        grid=(steps,),
        out_shape=jax.ShapeDtypeStruct((tokens, cycle * unit), BF16),
        in_specs=[
            pl.BlockSpec((wide, tokens, unit), lambda i: (i, 0, 0)),
            pl.BlockSpec((tokens, lanes), lambda i: (0, chunk * steps + i)),
            pl.BlockSpec((tokens, lanes), lambda i: (0, chunk * steps + i)),
            pl.BlockSpec((1, lanes), lambda i: (0, chunk * steps + i)),
        ],
        out_specs=pl.BlockSpec((tokens, lanes), lambda i: (0, i)),
        compiler_params=pltpu.CompilerParams(vmem_limit_bytes=VMEM),
        cost_estimate=pl.CostEstimate(
            flops=0, bytes_accessed=8 * convolved.size, transcendentals=0
        ),
        name="gate",
    )(convolved, keyval, gating, skip_gain.reshape(1, -1))


def mix_kernel(shape, *refs):
    pieces, peers, halves = shape
    place_ref, refs = refs[0], refs[1:]
    h_refs, w_refs, out_refs = refs[: pieces * peers], refs[pieces * peers :][:halves], refs[-peers:]
    depth = w_refs[0].shape[2]
    per = h_refs[0].shape[1] // (halves * depth)
    totals = [None] * peers
    for k in range(pieces):
        for j in range(per):
            line = place_ref[2 + 2 * (k * per + j)]
            turn = place_ref[3 + 2 * (k * per + j)]
            for core in range(halves):
                at = j * halves + lax.rem(place_ref[0] + core, halves)
                lanes = pl.ds(pl.multiple_of(at * depth, depth), depth)
                w = w_refs[core][line, turn]
                for m in range(peers):
                    part = jnp.dot(
                        h_refs[k * peers + m][:, lanes], w, preferred_element_type=F32
                    )
                    totals[m] = part if totals[m] is None else totals[m] + part
    for m in range(peers):
        out_refs[m][...] = totals[m].astype(BF16)


def mix(hidden, weights, places):
    pieces, peers, halves = len(hidden), len(hidden[0]), len(weights)
    tokens = hidden[0][0].shape[0]
    line, turns, depth, columns = weights[0].shape
    tile = min(256, columns)
    flat = [h for piece in hidden for h in piece]
    return pl.pallas_call(
        functools.partial(mix_kernel, (pieces, peers, halves)),
        grid=(columns // tile,),
        out_shape=[jax.ShapeDtypeStruct((tokens, columns), BF16)] * peers,
        in_specs=[pl.BlockSpec(memory_space=pltpu.SMEM)]
        + [pl.BlockSpec(h.shape, lambda i: (0, 0)) for h in flat]
        + [pl.BlockSpec((line, turns, depth, tile), lambda i: (0, 0, 0, i))] * halves,
        out_specs=[pl.BlockSpec((tokens, tile), lambda i: (0, i))] * peers,
        compiler_params=pltpu.CompilerParams(vmem_limit_bytes=VMEM),
        cost_estimate=pl.CostEstimate(
            flops=2 * tokens * peers * halves * line * turns * depth * columns,
            bytes_accessed=2 * halves * line * turns * depth * columns,
            transcendentals=0,
        ),
        name="mix",
    )(places, *flat, *weights)


def body(keyval, gating, skip_gain, filter_values, blocks, out_weight):
    cycle = lax.axis_size("seq")
    place = lax.axis_index("seq")
    peers = lax.axis_size("tensor")
    side = lax.axis_index("tensor")
    tokens, channels = keyval.shape
    repeat = BLOCK // cycle
    groups_local = blocks.shape[0]
    group_width = channels // groups_local
    narrow = channels // cycle
    unit = min(narrow, group_width)
    chunks = narrow // unit

    cores = 2 if cycle % 2 == 0 else 1
    line = math.gcd(cycle // cores, 4)
    turns = cycle // (cores * line)
    core, turn = place % cores, place // cores % turns

    def index(i, m, c):
        return (i % line * turns + m % turns) * cores + c % cores

    def move(value, by_turn, by_core):
        pairs = [
            (index(i, m, c), index(i, m + by_turn, c + by_core))
            for i in range(line)
            for m in range(turns)
            for c in range(cores)
        ]
        return lax.ppermute(value, "seq", pairs)

    rows, columns = out_weight.shape[0], out_weight.shape[1] // turns
    shares = []
    for m in range(turns):
        target = (turn + m) % turns
        share = lax.dynamic_slice_in_dim(out_weight, target * columns, columns, axis=1)
        shares.append(move(share, m, 0) if m else share)
    stacked = jnp.concatenate(shares, axis=0)
    lines = [
        [index(i, m, c) for i in range(line)] for m in range(turns) for c in range(cores)
    ]
    bounds = [0, columns * 3 // 4, columns] if columns % 1024 == 0 else [0, columns]
    weights = []
    for low, high in zip(bounds[:-1], bounds[1:]):
        lined = lax.all_gather(
            stacked[:, low:high], "seq", axis=0, tiled=True, axis_index_groups=lines
        )
        weights.append(
            [
                (move(lined, 0, c) if c else lined).reshape(line, turns, rows, high - low)
                for c in range(cores)
            ]
        )

    exchange = functools.partial(
        lax.all_to_all, axis_name="seq", split_axis=0, concat_axis=0, tiled=True
    )
    signals = [exchange(pack_signal(keyval, g, cycle, unit)) for g in range(chunks)]
    filters = exchange(pack_filters(filter_values, cycle, chunks, unit))

    group = (jnp.arange(chunks, dtype=jnp.int32) * cycle + place) * unit // group_width
    kept_blocks = jnp.take(blocks, group, axis=0)
    kept_rows = (
        kept_blocks[:, :, None] * repeat + jnp.arange(repeat, dtype=jnp.int32)
    ).reshape(chunks, -1)
    local_index = jnp.arange(tokens, dtype=jnp.int32)
    cosine, sine = tables(kept_rows[:, :, None], local_index[None, None, :], tokens)
    ahead = jnp.concatenate(
        [jnp.concatenate([cosine, sine], axis=2), jnp.concatenate([-sine, cosine], axis=2)],
        axis=1,
    ).astype(BF16)
    cosine, sine = tables(kept_rows[:, None, :], local_index[None, :, None], tokens)
    back = jnp.concatenate(
        [jnp.concatenate([cosine, -sine], axis=2), jnp.concatenate([sine, cosine], axis=2)],
        axis=1,
    ).astype(BF16)
    cycle_index = jnp.arange(cycle, dtype=jnp.int32)
    twist = jnp.concatenate(
        tables(local_index[:, None], cycle_index[None, :], cycle * tokens), axis=1
    )

    hidden, places = [], [core, jnp.zeros_like(core)]
    width = cycle * unit
    for g in range(chunks):
        done = exchange(convolve(g, twist, ahead, back, signals[g], filters))
        own = gate(done, keyval, gating, skip_gain, g)
        for shift in range(peers):
            piece = own
            if shift:
                piece = lax.ppermute(
                    own, "tensor", [(t, (t + shift) % peers) for t in range(peers)]
                )
            hidden.append([move(piece, m, 0) if m else piece for m in range(turns)])
            start = (side + peers - shift) % peers * channels + g * width
            for j in range(width // (cores * rows)):
                at = start // rows + j * cores
                places += [at // (cores * turns), (turn + turns - at // cores % turns) % turns]
    places = jnp.stack(places).astype(jnp.int32)

    result = jnp.zeros((tokens, columns * turns), BF16)
    for low, weight in zip(bounds[:-1], weights):
        for m, part in enumerate(mix(hidden, weight, places)):
            part = move(part, -m, 0) if m else part
            source = (turn + m) % turns
            result = lax.dynamic_update_slice(result, part, (0, source * columns + low))
    return result


def solution(mesh):
    placed = (
        P("seq", "tensor"),
        P("seq", "tensor"),
        P("tensor"),
        P(None, None, None, "seq", "tensor"),
        P("tensor", None),
        P("seq", "tensor"),
    )
    return jax.shard_map(
        body, mesh=mesh, in_specs=placed, out_specs=P("seq", "tensor"), check_vma=False
    )
```

```python
import functools
import math

import jax
import jax.numpy as jnp
from jax import lax
from jax.experimental import pallas as pl
from jax.experimental.pallas import tpu as pltpu
from jax.sharding import PartitionSpec as P

BLOCK = 64
ROWS = 16
VMEM = 48 * 2**20
F32 = jnp.float32
BF16 = jnp.bfloat16


def tables(first_index, second_index, length):
    phase = first_index * second_index % length
    angle = 2.0 * math.pi / length * phase.astype(F32)
    return (jnp.cos(angle), jnp.sin(angle))


def real_forward(values):
    n = len(values)
    if n == 2:
        return [(values[0] + values[1], None), (values[0] - values[1], None)]
    even, odd = real_forward(values[0::2]), real_forward(values[1::2])
    half = n // 2
    out = [None] * (half + 1)
    for p in range(half // 2 + 1):
        (er, ei), (dr, di) = even[p], odd[p]
        if p == 0:
            out[0], out[half] = (er + dr, None), (er - dr, None)
        elif 2 * p == half:
            out[p] = (er, -dr)
        else:
            c, s = math.cos(2 * math.pi * p / n), math.sin(2 * math.pi * p / n)
            tr, ti = dr * c + di * s, di * c - dr * s
            out[p], out[half - p] = (er + tr, ei + ti), (er - tr, ti - ei)
    return out


def real_inverse(freqs):
    half = len(freqs) - 1
    if half == 1:
        return [freqs[0][0] + freqs[1][0], freqs[0][0] - freqs[1][0]]
    n = 2 * half
    even, odd = [None] * (half // 2 + 1), [None] * (half // 2 + 1)
    for p in range(half // 2 + 1):
        (ar, ai), (br, bi) = freqs[p], freqs[half - p]
        if p == 0:
            even[0], odd[0] = (ar + br, None), (ar - br, None)
        elif 2 * p == half:
            even[p], odd[p] = (ar + ar, None), (-(ai + ai), None)
        else:
            c, s = math.cos(2 * math.pi * p / n), math.sin(2 * math.pi * p / n)
            dr, di = ar - br, ai + bi
            even[p], odd[p] = (ar + br, ai - bi), (dr * c - di * s, dr * s + di * c)
    out = [None] * n
    out[0::2], out[1::2] = real_inverse(even), real_inverse(odd)
    return out


def conv_kernel(twist_ref, ahead_ref, back_ref, x_ref, filter_ref, out_ref, first_ref, turned_ref):
    cycle, tokens, unit = x_ref.shape
    kept = filter_ref.shape[2] // 2
    per = max(1, 256 // unit)
    width = per * unit

    def twist(rows):
        block = twist_ref[rows, :]
        return [
            (block[:, p : p + 1], block[:, cycle + p : cycle + p + 1]) for p in range(cycle)
        ]

    def ahead(step, carry):
        start = pl.multiple_of(step * ROWS, ROWS)
        rows = pl.ds(start, ROWS)
        freqs = real_forward([x_ref[a, rows, :].astype(F32) for a in range(cycle)])
        for p, (c, s) in enumerate(twist(rows)):
            real, imaginary = freqs[min(p, cycle - p)]
            if imaginary is None:
                fr, fi = real * c, -(real * s)
            elif 2 * p > cycle:
                fr, fi = real * c - imaginary * s, -(imaginary * c + real * s)
            else:
                fr, fi = real * c + imaginary * s, imaginary * c - real * s
            lanes = slice(p * unit, (p + 1) * unit)
            first_ref[rows, lanes] = fr.astype(BF16)
            first_ref[pl.ds(tokens + start, ROWS), lanes] = fi.astype(BF16)
        return carry

    lax.fori_loop(0, tokens // ROWS, ahead, 0)

    def middle(step, carry):
        lanes = pl.ds(pl.multiple_of(step * width, width), width)
        spectrum = jnp.dot(ahead_ref[0], first_ref[:, lanes], preferred_element_type=F32)
        reals, imaginaries = [], []
        for u in range(per):
            part = filter_ref[step * per + u, 0].astype(F32)
            hr, hi = part[:kept], part[kept:]
            own = slice(u * unit, (u + 1) * unit)
            sr, si = spectrum[:kept, own], spectrum[kept:, own]
            reals.append(hr * sr - hi * si)
            imaginaries.append(hr * si + hi * sr)
        product = jnp.concatenate(
            [jnp.concatenate(reals, axis=1), jnp.concatenate(imaginaries, axis=1)], axis=0
        ).astype(BF16)
        turned_ref[:, lanes] = jnp.dot(back_ref[0], product, preferred_element_type=F32)
        return carry

    lax.fori_loop(0, cycle // per, middle, 0)

    def behind(step, carry):
        start = pl.multiple_of(step * ROWS, ROWS)
        rows = pl.ds(start, ROWS)
        parts = []
        for p, (c, s) in enumerate(twist(rows)):
            lanes = slice(p * unit, (p + 1) * unit)
            br = turned_ref[rows, lanes]
            bi = turned_ref[pl.ds(tokens + start, ROWS), lanes]
            parts.append(
                (
                    (br * c - bi * s).astype(BF16).astype(F32),
                    (br * s + bi * c).astype(BF16).astype(F32),
                )
            )
        half = cycle // 2
        freqs = [(parts[0][0] * 2.0, None)]
        for p in range(1, half):
            (ur, ui), (vr, vi) = parts[p], parts[cycle - p]
            freqs.append((ur + vr, ui - vi))
        freqs.append((parts[half][0] * 2.0, None))
        scale = 0.5 / (cycle * tokens)
        for a, value in enumerate(real_inverse(freqs)):
            out_ref[a, rows, :] = (value * scale).astype(BF16)
        return carry

    lax.fori_loop(0, tokens // ROWS, behind, 0)


def convolve(chunk, twist, ahead, back, signal, filters):
    cycle, tokens, unit = signal.shape
    kept = filters.shape[2] // 2
    flops = 4 * 2 * kept * 2 * tokens * cycle * unit
    return pl.pallas_call(
        conv_kernel,
        grid=(1,),
        out_shape=jax.ShapeDtypeStruct(signal.shape, BF16),
        in_specs=[
            pl.BlockSpec(twist.shape, lambda i: (0, 0)),
            pl.BlockSpec((1, *ahead.shape[1:]), lambda i: (chunk, 0, 0)),
            pl.BlockSpec((1, *back.shape[1:]), lambda i: (chunk, 0, 0)),
            pl.BlockSpec(signal.shape, lambda i: (0, 0, 0)),
            pl.BlockSpec((cycle, 1, 2 * kept, unit), lambda i: (0, chunk, 0, 0)),
        ],
        out_specs=pl.BlockSpec(signal.shape, lambda i: (0, 0, 0)),
        scratch_shapes=[
            pltpu.VMEM((2 * tokens, cycle * unit), BF16),
            pltpu.VMEM((2 * tokens, cycle * unit), F32),
        ],
        compiler_params=pltpu.CompilerParams(vmem_limit_bytes=VMEM),
        cost_estimate=pl.CostEstimate(
            flops=flops, bytes_accessed=16 * signal.size, transcendentals=0
        ),
        name="convolve",
    )(twist, ahead, back, signal, filters)


def pack_kernel(unit, x_ref, out_ref):
    for d in range(out_ref.shape[0]):
        out_ref[d] = x_ref[:, d * unit : (d + 1) * unit]


def pack_signal(keyval, chunk, cycle, unit):
    tokens = keyval.shape[0]
    wide = max(1, min(cycle, 512 // unit))
    steps = cycle // wide
    return pl.pallas_call(
        functools.partial(pack_kernel, unit),
        grid=(steps,),
        out_shape=jax.ShapeDtypeStruct((cycle, tokens, unit), BF16),
        in_specs=[pl.BlockSpec((tokens, wide * unit), lambda i: (0, chunk * steps + i))],
        out_specs=pl.BlockSpec((wide, tokens, unit), lambda i: (i, 0, 0)),
        compiler_params=pltpu.CompilerParams(vmem_limit_bytes=VMEM),
        cost_estimate=pl.CostEstimate(
            flops=0, bytes_accessed=4 * tokens * cycle * unit, transcendentals=0
        ),
        name="pack_signal",
    )(keyval)


def pack_filter_kernel(unit, f_ref, out_ref):
    for d in range(out_ref.shape[0]):
        out_ref[d, 0] = f_ref[:, 0, d * unit : (d + 1) * unit].astype(BF16)


def pack_filters(filter_values, cycle, chunks, unit):
    channels = filter_values.shape[-1]
    rows = filter_values.size // channels
    flat = filter_values.reshape(rows, 1, channels)
    wide = max(1, min(cycle, 512 // unit))
    steps = cycle // wide
    return pl.pallas_call(
        functools.partial(pack_filter_kernel, unit),
        grid=(chunks, steps),
        out_shape=jax.ShapeDtypeStruct((cycle, chunks, rows, unit), BF16),
        in_specs=[pl.BlockSpec((rows, 1, wide * unit), lambda g, i: (0, 0, g * steps + i))],
        out_specs=pl.BlockSpec((wide, 1, rows, unit), lambda g, i: (i, g, 0, 0)),
        compiler_params=pltpu.CompilerParams(vmem_limit_bytes=VMEM),
        cost_estimate=pl.CostEstimate(
            flops=0, bytes_accessed=6 * filter_values.size, transcendentals=0
        ),
        name="pack_filters",
    )(flat)


def gate_kernel(unit, c_ref, x_ref, g_ref, s_ref, out_ref):
    for d in range(c_ref.shape[0]):
        lanes = slice(d * unit, (d + 1) * unit)
        direct = s_ref[0:1, lanes] * x_ref[:, lanes].astype(F32)
        value = g_ref[:, lanes].astype(F32) * (c_ref[d].astype(F32) + direct)
        out_ref[:, lanes] = value.astype(BF16)


def gate(convolved, keyval, gating, skip_gain, chunk):
    cycle, tokens, unit = convolved.shape
    wide = max(1, min(cycle, 512 // unit))
    steps = cycle // wide
    lanes = wide * unit
    return pl.pallas_call(
        functools.partial(gate_kernel, unit),
        grid=(steps,),
        out_shape=jax.ShapeDtypeStruct((tokens, cycle * unit), BF16),
        in_specs=[
            pl.BlockSpec((wide, tokens, unit), lambda i: (i, 0, 0)),
            pl.BlockSpec((tokens, lanes), lambda i: (0, chunk * steps + i)),
            pl.BlockSpec((tokens, lanes), lambda i: (0, chunk * steps + i)),
            pl.BlockSpec((1, lanes), lambda i: (0, chunk * steps + i)),
        ],
        out_specs=pl.BlockSpec((tokens, lanes), lambda i: (0, i)),
        compiler_params=pltpu.CompilerParams(vmem_limit_bytes=VMEM),
        cost_estimate=pl.CostEstimate(
            flops=0, bytes_accessed=8 * convolved.size, transcendentals=0
        ),
        name="gate",
    )(convolved, keyval, gating, skip_gain.reshape(1, -1))


def mix_kernel(pieces, start_ref, *refs):
    w_ref, out_ref = refs[pieces], refs[-1]
    total = None
    for k in range(pieces):
        depth = refs[k].shape[1]
        start = pl.multiple_of(start_ref[k], depth)
        part = jnp.dot(
            refs[k][...], w_ref[pl.ds(start, depth), :], preferred_element_type=F32
        )
        total = part if total is None else total + part
    out_ref[...] = total.astype(BF16)


def mix(hidden, starts, weight, low, columns, result):
    tokens = hidden[0].shape[0]
    depth, part = weight.shape
    tile = min(256, part)
    first = low // tile
    pieces = len(hidden)
    before = [] if result is None else [result]
    return pl.pallas_call(
        functools.partial(mix_kernel, pieces),
        grid=(part // tile,),
        out_shape=jax.ShapeDtypeStruct((tokens, columns), BF16),
        in_specs=[pl.BlockSpec(memory_space=pltpu.SMEM)]
        + [pl.BlockSpec(h.shape, lambda i: (0, 0)) for h in hidden]
        + [pl.BlockSpec((depth, tile), lambda i: (0, i))]
        + [pl.BlockSpec(memory_space=pl.ANY) for _ in before],
        out_specs=pl.BlockSpec((tokens, tile), lambda i: (0, first + i)),
        input_output_aliases={pieces + 2: 0} if before else {},
        compiler_params=pltpu.CompilerParams(vmem_limit_bytes=VMEM),
        cost_estimate=pl.CostEstimate(
            flops=2 * tokens * depth * part, bytes_accessed=2 * depth * part, transcendentals=0
        ),
        name="mix",
    )(starts, *hidden, weight, *before)


def body(keyval, gating, skip_gain, filter_values, blocks, out_weight):
    cycle = lax.axis_size("seq")
    place = lax.axis_index("seq")
    peers = lax.axis_size("tensor")
    side = lax.axis_index("tensor")
    tokens, channels = keyval.shape
    repeat = BLOCK // cycle
    groups_local = blocks.shape[0]
    group_width = channels // groups_local
    narrow = channels // cycle
    unit = min(narrow, group_width)
    chunks = narrow // unit

    columns = out_weight.shape[1]
    eighth = columns // 8
    bounds = [0, 4 * eighth, 7 * eighth, columns] if eighth % 256 == 0 else [0, columns]
    weights = [
        lax.all_gather(out_weight[:, low:high], "seq", axis=0, tiled=True)
        for low, high in zip(bounds[:-1], bounds[1:])
    ]

    exchange = functools.partial(
        lax.all_to_all, axis_name="seq", split_axis=0, concat_axis=0, tiled=True
    )
    signals = [exchange(pack_signal(keyval, g, cycle, unit)) for g in range(chunks)]
    filters = exchange(pack_filters(filter_values, cycle, chunks, unit))

    group = (jnp.arange(chunks, dtype=jnp.int32) * cycle + place) * unit // group_width
    kept_blocks = jnp.take(blocks, group, axis=0)
    kept_rows = (
        kept_blocks[:, :, None] * repeat + jnp.arange(repeat, dtype=jnp.int32)
    ).reshape(chunks, -1)
    local_index = jnp.arange(tokens, dtype=jnp.int32)
    cosine, sine = tables(kept_rows[:, :, None], local_index[None, None, :], tokens)
    ahead = jnp.concatenate(
        [jnp.concatenate([cosine, sine], axis=2), jnp.concatenate([-sine, cosine], axis=2)],
        axis=1,
    ).astype(BF16)
    cosine, sine = tables(kept_rows[:, None, :], local_index[None, :, None], tokens)
    back = jnp.concatenate(
        [jnp.concatenate([cosine, -sine], axis=2), jnp.concatenate([sine, cosine], axis=2)],
        axis=1,
    ).astype(BF16)
    cycle_index = jnp.arange(cycle, dtype=jnp.int32)
    twist = jnp.concatenate(
        tables(local_index[:, None], cycle_index[None, :], cycle * tokens), axis=1
    )

    hidden, starts = [], []
    for g in range(chunks):
        done = exchange(convolve(g, twist, ahead, back, signals[g], filters))
        own = gate(done, keyval, gating, skip_gain, g)
        for shift in range(peers):
            if shift == 0:
                piece = own
            else:
                piece = lax.ppermute(
                    own, "tensor", [(t, (t + shift) % peers) for t in range(peers)]
                )
            hidden.append(piece)
            source = lax.rem(side + peers - shift, peers)
            starts.append(source * channels + g * cycle * unit)
    starts = jnp.stack(starts).astype(jnp.int32)
    result = None
    for low, weight in zip(bounds[:-1], weights):
        result = mix(hidden, starts, weight, low, columns, result)
    return result


def solution(mesh):
    placed = (
        P("seq", "tensor"),
        P("seq", "tensor"),
        P("tensor"),
        P(None, None, None, "seq", "tensor"),
        P("tensor", None),
        P("seq", "tensor"),
    )
    return jax.shard_map(
        body, mesh=mesh, in_specs=placed, out_specs=P("seq", "tensor"), check_vma=False
    )
```

```python
import functools
import math

import jax
import jax.numpy as jnp
from jax import lax
from jax.experimental import pallas as pl
from jax.experimental.pallas import tpu as pltpu
from jax.sharding import PartitionSpec as P

BLOCK = 64
ROWS = 16
VMEM = 48 * 2**20
F32 = jnp.float32
BF16 = jnp.bfloat16


def tables(first_index, second_index, length):
    phase = first_index * second_index % length
    angle = 2.0 * math.pi / length * phase.astype(F32)
    return (jnp.cos(angle), jnp.sin(angle))


def real_forward(values):
    n = len(values)
    if n == 2:
        return [(values[0] + values[1], None), (values[0] - values[1], None)]
    even, odd = real_forward(values[0::2]), real_forward(values[1::2])
    half = n // 2
    out = [None] * (half + 1)
    for p in range(half // 2 + 1):
        (er, ei), (dr, di) = even[p], odd[p]
        if p == 0:
            out[0], out[half] = (er + dr, None), (er - dr, None)
        elif 2 * p == half:
            out[p] = (er, -dr)
        else:
            c, s = math.cos(2 * math.pi * p / n), math.sin(2 * math.pi * p / n)
            tr, ti = dr * c + di * s, di * c - dr * s
            out[p], out[half - p] = (er + tr, ei + ti), (er - tr, ti - ei)
    return out


def real_inverse(freqs):
    half = len(freqs) - 1
    if half == 1:
        return [freqs[0][0] + freqs[1][0], freqs[0][0] - freqs[1][0]]
    n = 2 * half
    even, odd = [None] * (half // 2 + 1), [None] * (half // 2 + 1)
    for p in range(half // 2 + 1):
        (ar, ai), (br, bi) = freqs[p], freqs[half - p]
        if p == 0:
            even[0], odd[0] = (ar + br, None), (ar - br, None)
        elif 2 * p == half:
            even[p], odd[p] = (ar + ar, None), (-(ai + ai), None)
        else:
            c, s = math.cos(2 * math.pi * p / n), math.sin(2 * math.pi * p / n)
            dr, di = ar - br, ai + bi
            even[p], odd[p] = (ar + br, ai - bi), (dr * c - di * s, dr * s + di * c)
    out = [None] * n
    out[0::2], out[1::2] = real_inverse(even), real_inverse(odd)
    return out


def conv_kernel(twist_ref, ahead_ref, back_ref, x_ref, filter_ref, out_ref, first_ref, turned_ref):
    cycle, tokens, unit = x_ref.shape
    kept = filter_ref.shape[2] // 2
    per = max(1, 256 // unit)
    width = per * unit

    def twist(rows):
        block = twist_ref[rows, :]
        return [
            (block[:, p : p + 1], block[:, cycle + p : cycle + p + 1]) for p in range(cycle)
        ]

    def ahead(step, carry):
        start = pl.multiple_of(step * ROWS, ROWS)
        rows = pl.ds(start, ROWS)
        freqs = real_forward([x_ref[a, rows, :].astype(F32) for a in range(cycle)])
        for p, (c, s) in enumerate(twist(rows)):
            real, imaginary = freqs[min(p, cycle - p)]
            if imaginary is None:
                fr, fi = real * c, -(real * s)
            elif 2 * p > cycle:
                fr, fi = real * c - imaginary * s, -(imaginary * c + real * s)
            else:
                fr, fi = real * c + imaginary * s, imaginary * c - real * s
            lanes = slice(p * unit, (p + 1) * unit)
            first_ref[rows, lanes] = fr.astype(BF16)
            first_ref[pl.ds(tokens + start, ROWS), lanes] = fi.astype(BF16)
        return carry

    lax.fori_loop(0, tokens // ROWS, ahead, 0)

    def middle(step, carry):
        lanes = pl.ds(pl.multiple_of(step * width, width), width)
        spectrum = jnp.dot(ahead_ref[0], first_ref[:, lanes], preferred_element_type=F32)
        reals, imaginaries = [], []
        for u in range(per):
            part = filter_ref[step * per + u, 0].astype(F32)
            hr, hi = part[:kept], part[kept:]
            own = slice(u * unit, (u + 1) * unit)
            sr, si = spectrum[:kept, own], spectrum[kept:, own]
            reals.append(hr * sr - hi * si)
            imaginaries.append(hr * si + hi * sr)
        product = jnp.concatenate(
            [jnp.concatenate(reals, axis=1), jnp.concatenate(imaginaries, axis=1)], axis=0
        ).astype(BF16)
        turned_ref[:, lanes] = jnp.dot(back_ref[0], product, preferred_element_type=F32)
        return carry

    lax.fori_loop(0, cycle // per, middle, 0)

    def behind(step, carry):
        start = pl.multiple_of(step * ROWS, ROWS)
        rows = pl.ds(start, ROWS)
        parts = []
        for p, (c, s) in enumerate(twist(rows)):
            lanes = slice(p * unit, (p + 1) * unit)
            br = turned_ref[rows, lanes]
            bi = turned_ref[pl.ds(tokens + start, ROWS), lanes]
            parts.append(
                (
                    (br * c - bi * s).astype(BF16).astype(F32),
                    (br * s + bi * c).astype(BF16).astype(F32),
                )
            )
        half = cycle // 2
        freqs = [(parts[0][0] * 2.0, None)]
        for p in range(1, half):
            (ur, ui), (vr, vi) = parts[p], parts[cycle - p]
            freqs.append((ur + vr, ui - vi))
        freqs.append((parts[half][0] * 2.0, None))
        scale = 0.5 / (cycle * tokens)
        for a, value in enumerate(real_inverse(freqs)):
            out_ref[a, rows, :] = (value * scale).astype(BF16)
        return carry

    lax.fori_loop(0, tokens // ROWS, behind, 0)


def convolve(chunk, twist, ahead, back, signal, filters):
    cycle, tokens, unit = signal.shape
    kept = filters.shape[2] // 2
    flops = 4 * 2 * kept * 2 * tokens * cycle * unit
    return pl.pallas_call(
        conv_kernel,
        grid=(1,),
        out_shape=jax.ShapeDtypeStruct(signal.shape, BF16),
        in_specs=[
            pl.BlockSpec(twist.shape, lambda i: (0, 0)),
            pl.BlockSpec((1, *ahead.shape[1:]), lambda i: (chunk, 0, 0)),
            pl.BlockSpec((1, *back.shape[1:]), lambda i: (chunk, 0, 0)),
            pl.BlockSpec(signal.shape, lambda i: (0, 0, 0)),
            pl.BlockSpec((cycle, 1, 2 * kept, unit), lambda i: (0, chunk, 0, 0)),
        ],
        out_specs=pl.BlockSpec(signal.shape, lambda i: (0, 0, 0)),
        scratch_shapes=[
            pltpu.VMEM((2 * tokens, cycle * unit), BF16),
            pltpu.VMEM((2 * tokens, cycle * unit), F32),
        ],
        compiler_params=pltpu.CompilerParams(vmem_limit_bytes=VMEM),
        cost_estimate=pl.CostEstimate(
            flops=flops, bytes_accessed=16 * signal.size, transcendentals=0
        ),
        name="convolve",
    )(twist, ahead, back, signal, filters)


def pack_kernel(unit, x_ref, out_ref):
    for d in range(out_ref.shape[0]):
        out_ref[d] = x_ref[:, d * unit : (d + 1) * unit]


def pack_signal(keyval, chunk, cycle, unit):
    tokens = keyval.shape[0]
    wide = max(1, min(cycle, 512 // unit))
    steps = cycle // wide
    return pl.pallas_call(
        functools.partial(pack_kernel, unit),
        grid=(steps,),
        out_shape=jax.ShapeDtypeStruct((cycle, tokens, unit), BF16),
        in_specs=[pl.BlockSpec((tokens, wide * unit), lambda i: (0, chunk * steps + i))],
        out_specs=pl.BlockSpec((wide, tokens, unit), lambda i: (i, 0, 0)),
        compiler_params=pltpu.CompilerParams(vmem_limit_bytes=VMEM),
        cost_estimate=pl.CostEstimate(
            flops=0, bytes_accessed=4 * tokens * cycle * unit, transcendentals=0
        ),
        name="pack_signal",
    )(keyval)


def pack_filter_kernel(unit, f_ref, out_ref):
    for d in range(out_ref.shape[0]):
        out_ref[d, 0] = f_ref[:, 0, d * unit : (d + 1) * unit].astype(BF16)


def pack_filters(filter_values, cycle, chunks, unit):
    channels = filter_values.shape[-1]
    rows = filter_values.size // channels
    flat = filter_values.reshape(rows, 1, channels)
    wide = max(1, min(cycle, 512 // unit))
    steps = cycle // wide
    return pl.pallas_call(
        functools.partial(pack_filter_kernel, unit),
        grid=(chunks, steps),
        out_shape=jax.ShapeDtypeStruct((cycle, chunks, rows, unit), BF16),
        in_specs=[pl.BlockSpec((rows, 1, wide * unit), lambda g, i: (0, 0, g * steps + i))],
        out_specs=pl.BlockSpec((wide, 1, rows, unit), lambda g, i: (i, g, 0, 0)),
        compiler_params=pltpu.CompilerParams(vmem_limit_bytes=VMEM),
        cost_estimate=pl.CostEstimate(
            flops=0, bytes_accessed=6 * filter_values.size, transcendentals=0
        ),
        name="pack_filters",
    )(flat)


def gate_kernel(unit, c_ref, x_ref, g_ref, s_ref, out_ref):
    for d in range(c_ref.shape[0]):
        lanes = slice(d * unit, (d + 1) * unit)
        direct = s_ref[0:1, lanes] * x_ref[:, lanes].astype(F32)
        value = g_ref[:, lanes].astype(F32) * (c_ref[d].astype(F32) + direct)
        out_ref[:, lanes] = value.astype(BF16)


def gate(convolved, keyval, gating, skip_gain, chunk):
    cycle, tokens, unit = convolved.shape
    wide = max(1, min(cycle, 512 // unit))
    steps = cycle // wide
    lanes = wide * unit
    return pl.pallas_call(
        functools.partial(gate_kernel, unit),
        grid=(steps,),
        out_shape=jax.ShapeDtypeStruct((tokens, cycle * unit), BF16),
        in_specs=[
            pl.BlockSpec((wide, tokens, unit), lambda i: (i, 0, 0)),
            pl.BlockSpec((tokens, lanes), lambda i: (0, chunk * steps + i)),
            pl.BlockSpec((tokens, lanes), lambda i: (0, chunk * steps + i)),
            pl.BlockSpec((1, lanes), lambda i: (0, chunk * steps + i)),
        ],
        out_specs=pl.BlockSpec((tokens, lanes), lambda i: (0, i)),
        compiler_params=pltpu.CompilerParams(vmem_limit_bytes=VMEM),
        cost_estimate=pl.CostEstimate(
            flops=0, bytes_accessed=8 * convolved.size, transcendentals=0
        ),
        name="gate",
    )(convolved, keyval, gating, skip_gain.reshape(1, -1))


def mix_kernel(pieces, start_ref, *refs):
    w_ref, out_ref = refs[pieces], refs[-1]
    total = None
    for k in range(pieces):
        depth = refs[k].shape[1]
        start = pl.multiple_of(start_ref[k], depth)
        part = jnp.dot(
            refs[k][...], w_ref[pl.ds(start, depth), :], preferred_element_type=F32
        )
        total = part if total is None else total + part
    out_ref[...] = total.astype(BF16)


def mix(hidden, starts, weight, low, columns, result):
    tokens = hidden[0].shape[0]
    depth, part = weight.shape
    tile = min(256, part)
    first = low // tile
    pieces = len(hidden)
    before = [] if result is None else [result]
    return pl.pallas_call(
        functools.partial(mix_kernel, pieces),
        grid=(part // tile,),
        out_shape=jax.ShapeDtypeStruct((tokens, columns), BF16),
        in_specs=[pl.BlockSpec(memory_space=pltpu.SMEM)]
        + [pl.BlockSpec(h.shape, lambda i: (0, 0)) for h in hidden]
        + [pl.BlockSpec((depth, tile), lambda i: (0, i))]
        + [pl.BlockSpec(memory_space=pl.ANY) for _ in before],
        out_specs=pl.BlockSpec((tokens, tile), lambda i: (0, first + i)),
        input_output_aliases={pieces + 2: 0} if before else {},
        compiler_params=pltpu.CompilerParams(vmem_limit_bytes=VMEM),
        cost_estimate=pl.CostEstimate(
            flops=2 * tokens * depth * part, bytes_accessed=2 * depth * part, transcendentals=0
        ),
        name="mix",
    )(starts, *hidden, weight, *before)


def line_kernel(pieces, blocks, place_ref, *refs):
    w_refs, out_ref = refs[pieces : pieces + blocks], refs[-1]
    depth = w_refs[0].shape[1]
    total = None
    for k in range(pieces):
        for b in range(blocks):
            lanes = pl.ds(pl.multiple_of(place_ref[pieces + b], depth), depth)
            part = jnp.dot(
                refs[k][:, lanes], w_refs[b][place_ref[k]], preferred_element_type=F32
            )
            total = part if total is None else total + part
    out_ref[...] = total.astype(BF16)


def mix_line(hidden, places, weights, columns):
    tokens = hidden[0].shape[0]
    line, depth, part = weights[0].shape
    tile = min(256, part)
    pieces, blocks = len(hidden), len(weights)
    return pl.pallas_call(
        functools.partial(line_kernel, pieces, blocks),
        grid=(part // tile,),
        out_shape=jax.ShapeDtypeStruct((tokens, columns), BF16),
        in_specs=[pl.BlockSpec(memory_space=pltpu.SMEM)]
        + [pl.BlockSpec(h.shape, lambda i: (0, 0)) for h in hidden]
        + [pl.BlockSpec((line, depth, tile), lambda i: (0, 0, i))] * blocks,
        out_specs=pl.BlockSpec((tokens, tile), lambda i: (0, i)),
        compiler_params=pltpu.CompilerParams(vmem_limit_bytes=VMEM),
        cost_estimate=pl.CostEstimate(
            flops=2 * tokens * blocks * line * depth * part,
            bytes_accessed=2 * blocks * line * depth * part,
            transcendentals=0,
        ),
        name="mix_line",
    )(places, *hidden, *weights)


def body(keyval, gating, skip_gain, filter_values, blocks, out_weight):
    cycle = lax.axis_size("seq")
    place = lax.axis_index("seq")
    peers = lax.axis_size("tensor")
    side = lax.axis_index("tensor")
    tokens, channels = keyval.shape
    repeat = BLOCK // cycle
    groups_local = blocks.shape[0]
    group_width = channels // groups_local
    narrow = channels // cycle
    unit = min(narrow, group_width)
    chunks = narrow // unit

    rows, columns = out_weight.shape
    cores = 2
    line = math.gcd(cycle // cores, 4)
    turns = cycle // (cores * line)
    z, turn, core = place // (turns * cores), place // cores % turns, place % cores

    def move(value, by_line, by_turn, by_core, held=None):
        held = range(line) if held is None else held
        pairs = [
            (
                (i * turns + m) * cores + c,
                ((i + by_line) * turns + (m + by_turn) % turns) * cores + (c + by_core) % cores,
            )
            for i in held
            for m in range(turns)
            for c in range(cores)
        ]
        return lax.ppermute(value, "seq", pairs)

    eighth = columns // 8
    fits = eighth % 256 == 0 and unit * cycle == rows * cores * turns
    cut = 3 * eighth if fits else 0
    weight = lax.all_gather(out_weight[:, cut:], "seq", axis=0, tiled=True)
    if cut:
        ups, downs = [out_weight[:, :cut]], [out_weight[:, :cut]]
        for r in range(1, line):
            ups.append(move(ups[-1], 1, 0, 0, range(r - 1, line - 1)))
            downs.append(move(downs[-1], -1, 0, 0, range(1, line - r + 1)))
        lined = jnp.stack(
            [ups[0]] + [jnp.where(z >= r, ups[r], downs[line - r]) for r in range(1, line)]
        )
        lined = [move(lined, 0, m, 0) if m else lined for m in range(turns)]
        lined = [move(w, 0, 0, c) if c else w for c in range(cores) for w in lined]

    exchange = functools.partial(
        lax.all_to_all, axis_name="seq", split_axis=0, concat_axis=0, tiled=True
    )
    signals = [exchange(pack_signal(keyval, g, cycle, unit)) for g in range(chunks)]
    filters = exchange(pack_filters(filter_values, cycle, chunks, unit))

    group = (jnp.arange(chunks, dtype=jnp.int32) * cycle + place) * unit // group_width
    kept_blocks = jnp.take(blocks, group, axis=0)
    kept_rows = (
        kept_blocks[:, :, None] * repeat + jnp.arange(repeat, dtype=jnp.int32)
    ).reshape(chunks, -1)
    local_index = jnp.arange(tokens, dtype=jnp.int32)
    cosine, sine = tables(kept_rows[:, :, None], local_index[None, None, :], tokens)
    ahead = jnp.concatenate(
        [jnp.concatenate([cosine, sine], axis=2), jnp.concatenate([-sine, cosine], axis=2)],
        axis=1,
    ).astype(BF16)
    cosine, sine = tables(kept_rows[:, None, :], local_index[None, :, None], tokens)
    back = jnp.concatenate(
        [jnp.concatenate([cosine, -sine], axis=2), jnp.concatenate([sine, cosine], axis=2)],
        axis=1,
    ).astype(BF16)
    cycle_index = jnp.arange(cycle, dtype=jnp.int32)
    twist = jnp.concatenate(
        tables(local_index[:, None], cycle_index[None, :], cycle * tokens), axis=1
    )

    hidden, starts = [], []
    for g in range(chunks):
        done = exchange(convolve(g, twist, ahead, back, signals[g], filters))
        own = gate(done, keyval, gating, skip_gain, g)
        for shift in range(peers):
            if shift == 0:
                piece = own
            else:
                piece = lax.ppermute(
                    own, "tensor", [(t, (t + shift) % peers) for t in range(peers)]
                )
            hidden.append(piece)
            source = lax.rem(side + peers - shift, peers)
            starts.append(source * channels + g * cycle * unit)
    result = None
    if cut:
        places = [lax.rem(z + line - start // (rows * cores * turns), line) for start in starts]
        places += [
            (lax.rem(turn + turns - m, turns) * cores + lax.rem(core + c, cores)) * rows
            for c in range(cores)
            for m in range(turns)
        ]
        places = jnp.stack(places).astype(jnp.int32)
        result = mix_line(hidden, places, lined, columns)
    starts = jnp.stack(starts).astype(jnp.int32)
    return mix(hidden, starts, weight, cut, columns, result)


def solution(mesh):
    placed = (
        P("seq", "tensor"),
        P("seq", "tensor"),
        P("tensor"),
        P(None, None, None, "seq", "tensor"),
        P("tensor", None),
        P("seq", "tensor"),
    )
    return jax.shard_map(
        body, mesh=mesh, in_specs=placed, out_specs=P("seq", "tensor"), check_vma=False
    )
```

```python
import functools
import math

import jax
import jax.numpy as jnp
from jax import lax
from jax.experimental import pallas as pl
from jax.experimental.pallas import tpu as pltpu
from jax.sharding import PartitionSpec as P

BLOCK = 64
ROWS = 16
VMEM = 48 * 2**20
F32 = jnp.float32
BF16 = jnp.bfloat16


def tables(first_index, second_index, length):
    phase = first_index * second_index % length
    angle = 2.0 * math.pi / length * phase.astype(F32)
    return (jnp.cos(angle), jnp.sin(angle))


def real_forward(values):
    n = len(values)
    if n == 2:
        return [(values[0] + values[1], None), (values[0] - values[1], None)]
    even, odd = real_forward(values[0::2]), real_forward(values[1::2])
    half = n // 2
    out = [None] * (half + 1)
    for p in range(half // 2 + 1):
        (er, ei), (dr, di) = even[p], odd[p]
        if p == 0:
            out[0], out[half] = (er + dr, None), (er - dr, None)
        elif 2 * p == half:
            out[p] = (er, -dr)
        else:
            c, s = math.cos(2 * math.pi * p / n), math.sin(2 * math.pi * p / n)
            tr, ti = dr * c + di * s, di * c - dr * s
            out[p], out[half - p] = (er + tr, ei + ti), (er - tr, ti - ei)
    return out


def real_inverse(freqs):
    half = len(freqs) - 1
    if half == 1:
        return [freqs[0][0] + freqs[1][0], freqs[0][0] - freqs[1][0]]
    n = 2 * half
    even, odd = [None] * (half // 2 + 1), [None] * (half // 2 + 1)
    for p in range(half // 2 + 1):
        (ar, ai), (br, bi) = freqs[p], freqs[half - p]
        if p == 0:
            even[0], odd[0] = (ar + br, None), (ar - br, None)
        elif 2 * p == half:
            even[p], odd[p] = (ar + ar, None), (-(ai + ai), None)
        else:
            c, s = math.cos(2 * math.pi * p / n), math.sin(2 * math.pi * p / n)
            dr, di = ar - br, ai + bi
            even[p], odd[p] = (ar + br, ai - bi), (dr * c - di * s, dr * s + di * c)
    out = [None] * n
    out[0::2], out[1::2] = real_inverse(even), real_inverse(odd)
    return out


def conv_kernel(twist_ref, ahead_ref, back_ref, x_ref, filter_ref, out_ref, first_ref, turned_ref):
    cycle, tokens, unit = x_ref.shape
    kept = filter_ref.shape[2] // 2
    per = max(1, 256 // unit)
    width = per * unit

    def twist(rows):
        block = twist_ref[rows, :]
        return [
            (block[:, p : p + 1], block[:, cycle + p : cycle + p + 1]) for p in range(cycle)
        ]

    def ahead(step, carry):
        start = pl.multiple_of(step * ROWS, ROWS)
        rows = pl.ds(start, ROWS)
        freqs = real_forward([x_ref[a, rows, :].astype(F32) for a in range(cycle)])
        for p, (c, s) in enumerate(twist(rows)):
            real, imaginary = freqs[min(p, cycle - p)]
            if imaginary is None:
                fr, fi = real * c, -(real * s)
            elif 2 * p > cycle:
                fr, fi = real * c - imaginary * s, -(imaginary * c + real * s)
            else:
                fr, fi = real * c + imaginary * s, imaginary * c - real * s
            lanes = slice(p * unit, (p + 1) * unit)
            first_ref[rows, lanes] = fr.astype(BF16)
            first_ref[pl.ds(tokens + start, ROWS), lanes] = fi.astype(BF16)
        return carry

    lax.fori_loop(0, tokens // ROWS, ahead, 0)

    def middle(step, carry):
        lanes = pl.ds(pl.multiple_of(step * width, width), width)
        spectrum = jnp.dot(ahead_ref[0], first_ref[:, lanes], preferred_element_type=F32)
        reals, imaginaries = [], []
        for u in range(per):
            part = filter_ref[step * per + u, 0].astype(F32)
            hr, hi = part[:kept], part[kept:]
            own = slice(u * unit, (u + 1) * unit)
            sr, si = spectrum[:kept, own], spectrum[kept:, own]
            reals.append(hr * sr - hi * si)
            imaginaries.append(hr * si + hi * sr)
        product = jnp.concatenate(
            [jnp.concatenate(reals, axis=1), jnp.concatenate(imaginaries, axis=1)], axis=0
        ).astype(BF16)
        turned_ref[:, lanes] = jnp.dot(back_ref[0], product, preferred_element_type=F32)
        return carry

    lax.fori_loop(0, cycle // per, middle, 0)

    def behind(step, carry):
        start = pl.multiple_of(step * ROWS, ROWS)
        rows = pl.ds(start, ROWS)
        parts = []
        for p, (c, s) in enumerate(twist(rows)):
            lanes = slice(p * unit, (p + 1) * unit)
            br = turned_ref[rows, lanes]
            bi = turned_ref[pl.ds(tokens + start, ROWS), lanes]
            parts.append(
                (
                    (br * c - bi * s).astype(BF16).astype(F32),
                    (br * s + bi * c).astype(BF16).astype(F32),
                )
            )
        half = cycle // 2
        freqs = [(parts[0][0] * 2.0, None)]
        for p in range(1, half):
            (ur, ui), (vr, vi) = parts[p], parts[cycle - p]
            freqs.append((ur + vr, ui - vi))
        freqs.append((parts[half][0] * 2.0, None))
        scale = 0.5 / (cycle * tokens)
        for a, value in enumerate(real_inverse(freqs)):
            out_ref[a, rows, :] = (value * scale).astype(BF16)
        return carry

    lax.fori_loop(0, tokens // ROWS, behind, 0)


def convolve(chunk, twist, ahead, back, signal, filters):
    cycle, tokens, unit = signal.shape
    kept = filters.shape[2] // 2
    flops = 4 * 2 * kept * 2 * tokens * cycle * unit
    return pl.pallas_call(
        conv_kernel,
        grid=(1,),
        out_shape=jax.ShapeDtypeStruct(signal.shape, BF16),
        in_specs=[
            pl.BlockSpec(twist.shape, lambda i: (0, 0)),
            pl.BlockSpec((1, *ahead.shape[1:]), lambda i: (chunk, 0, 0)),
            pl.BlockSpec((1, *back.shape[1:]), lambda i: (chunk, 0, 0)),
            pl.BlockSpec(signal.shape, lambda i: (0, 0, 0)),
            pl.BlockSpec((cycle, 1, 2 * kept, unit), lambda i: (0, chunk, 0, 0)),
        ],
        out_specs=pl.BlockSpec(signal.shape, lambda i: (0, 0, 0)),
        scratch_shapes=[
            pltpu.VMEM((2 * tokens, cycle * unit), BF16),
            pltpu.VMEM((2 * tokens, cycle * unit), F32),
        ],
        compiler_params=pltpu.CompilerParams(vmem_limit_bytes=VMEM),
        cost_estimate=pl.CostEstimate(
            flops=flops, bytes_accessed=16 * signal.size, transcendentals=0
        ),
        name="convolve",
    )(twist, ahead, back, signal, filters)


def pack_kernel(unit, x_ref, out_ref):
    for d in range(out_ref.shape[0]):
        out_ref[d] = x_ref[:, d * unit : (d + 1) * unit]


def pack_signal(keyval, chunk, cycle, unit):
    tokens = keyval.shape[0]
    wide = max(1, min(cycle, 512 // unit))
    steps = cycle // wide
    return pl.pallas_call(
        functools.partial(pack_kernel, unit),
        grid=(steps,),
        out_shape=jax.ShapeDtypeStruct((cycle, tokens, unit), BF16),
        in_specs=[pl.BlockSpec((tokens, wide * unit), lambda i: (0, chunk * steps + i))],
        out_specs=pl.BlockSpec((wide, tokens, unit), lambda i: (i, 0, 0)),
        compiler_params=pltpu.CompilerParams(vmem_limit_bytes=VMEM),
        cost_estimate=pl.CostEstimate(
            flops=0, bytes_accessed=4 * tokens * cycle * unit, transcendentals=0
        ),
        name="pack_signal",
    )(keyval)


def pack_filter_kernel(unit, f_ref, out_ref):
    for d in range(out_ref.shape[0]):
        out_ref[d, 0] = f_ref[:, 0, d * unit : (d + 1) * unit].astype(BF16)


def pack_filters(filter_values, cycle, chunks, unit):
    channels = filter_values.shape[-1]
    rows = filter_values.size // channels
    flat = filter_values.reshape(rows, 1, channels)
    wide = max(1, min(cycle, 512 // unit))
    steps = cycle // wide
    return pl.pallas_call(
        functools.partial(pack_filter_kernel, unit),
        grid=(chunks, steps),
        out_shape=jax.ShapeDtypeStruct((cycle, chunks, rows, unit), BF16),
        in_specs=[pl.BlockSpec((rows, 1, wide * unit), lambda g, i: (0, 0, g * steps + i))],
        out_specs=pl.BlockSpec((wide, 1, rows, unit), lambda g, i: (i, g, 0, 0)),
        compiler_params=pltpu.CompilerParams(vmem_limit_bytes=VMEM),
        cost_estimate=pl.CostEstimate(
            flops=0, bytes_accessed=6 * filter_values.size, transcendentals=0
        ),
        name="pack_filters",
    )(flat)


def gate_kernel(unit, c_ref, x_ref, g_ref, s_ref, out_ref):
    for d in range(c_ref.shape[0]):
        lanes = slice(d * unit, (d + 1) * unit)
        direct = s_ref[0:1, lanes] * x_ref[:, lanes].astype(F32)
        value = g_ref[:, lanes].astype(F32) * (c_ref[d].astype(F32) + direct)
        out_ref[:, lanes] = value.astype(BF16)


def gate(convolved, keyval, gating, skip_gain, chunk):
    cycle, tokens, unit = convolved.shape
    wide = max(1, min(cycle, 512 // unit))
    steps = cycle // wide
    lanes = wide * unit
    return pl.pallas_call(
        functools.partial(gate_kernel, unit),
        grid=(steps,),
        out_shape=jax.ShapeDtypeStruct((tokens, cycle * unit), BF16),
        in_specs=[
            pl.BlockSpec((wide, tokens, unit), lambda i: (i, 0, 0)),
            pl.BlockSpec((tokens, lanes), lambda i: (0, chunk * steps + i)),
            pl.BlockSpec((tokens, lanes), lambda i: (0, chunk * steps + i)),
            pl.BlockSpec((1, lanes), lambda i: (0, chunk * steps + i)),
        ],
        out_specs=pl.BlockSpec((tokens, lanes), lambda i: (0, i)),
        compiler_params=pltpu.CompilerParams(vmem_limit_bytes=VMEM),
        cost_estimate=pl.CostEstimate(
            flops=0, bytes_accessed=8 * convolved.size, transcendentals=0
        ),
        name="gate",
    )(convolved, keyval, gating, skip_gain.reshape(1, -1))


def mix_kernel(pieces, start_ref, *refs):
    w_ref, out_ref = refs[pieces], refs[-1]
    total = None
    for k in range(pieces):
        depth = refs[k].shape[1]
        start = pl.multiple_of(start_ref[k], depth)
        part = jnp.dot(
            refs[k][...], w_ref[pl.ds(start, depth), :], preferred_element_type=F32
        )
        total = part if total is None else total + part
    out_ref[...] = total.astype(BF16)


def mix(hidden, starts, weight, low, columns, result):
    tokens = hidden[0].shape[0]
    depth, part = weight.shape
    tile = min(256, part)
    first = low // tile
    pieces = len(hidden)
    before = [] if result is None else [result]
    return pl.pallas_call(
        functools.partial(mix_kernel, pieces),
        grid=(part // tile,),
        out_shape=jax.ShapeDtypeStruct((tokens, columns), BF16),
        in_specs=[pl.BlockSpec(memory_space=pltpu.SMEM)]
        + [pl.BlockSpec(h.shape, lambda i: (0, 0)) for h in hidden]
        + [pl.BlockSpec((depth, tile), lambda i: (0, i))]
        + [pl.BlockSpec(memory_space=pl.ANY) for _ in before],
        out_specs=pl.BlockSpec((tokens, tile), lambda i: (0, first + i)),
        input_output_aliases={pieces + 2: 0} if before else {},
        compiler_params=pltpu.CompilerParams(vmem_limit_bytes=VMEM),
        cost_estimate=pl.CostEstimate(
            flops=2 * tokens * depth * part, bytes_accessed=2 * depth * part, transcendentals=0
        ),
        name="mix",
    )(starts, *hidden, weight, *before)


def line_kernel(pieces, steps, place_ref, *refs):
    w_refs, out_ref, held_ref = refs[pieces:-2], refs[-2], refs[-1]
    depth = w_refs[0].shape[1]

    @pl.when(pl.program_id(0) == 0)
    def _():
        for k in range(pieces):
            held_ref[place_ref[k]] = refs[k][...]

    blocks = len(w_refs) // len(steps)
    total = None
    for g, near in enumerate(steps):
        for b in range(blocks):
            lanes = pl.ds(pl.multiple_of(place_ref[2 * pieces + b], depth), depth)
            for n, j in enumerate(near):
                left = held_ref[place_ref[pieces + j], :, lanes]
                part = jnp.dot(left, w_refs[g * blocks + b][n], preferred_element_type=F32)
                total = part if total is None else total + part
    out_ref[...] = total.astype(BF16)


def mix_line(hidden, places, weights, steps, columns):
    tokens, width = hidden[0].shape
    depth, part = weights[0].shape[1:]
    tile = min(256, part)
    pieces = len(hidden)
    return pl.pallas_call(
        functools.partial(line_kernel, pieces, steps),
        grid=(part // tile,),
        out_shape=jax.ShapeDtypeStruct((tokens, columns), BF16),
        in_specs=[pl.BlockSpec(memory_space=pltpu.SMEM)]
        + [pl.BlockSpec(h.shape, lambda i: (0, 0)) for h in hidden]
        + [pl.BlockSpec((w.shape[0], depth, tile), lambda i: (0, 0, i)) for w in weights],
        out_specs=pl.BlockSpec((tokens, tile), lambda i: (0, i)),
        scratch_shapes=[pltpu.VMEM((pieces, tokens, width), BF16)],
        compiler_params=pltpu.CompilerParams(vmem_limit_bytes=VMEM),
        cost_estimate=pl.CostEstimate(
            flops=2 * tokens * pieces * width * part,
            bytes_accessed=2 * pieces * width * part,
            transcendentals=0,
        ),
        name="mix_line",
    )(places, *hidden, *weights)


def body(keyval, gating, skip_gain, filter_values, blocks, out_weight):
    cycle = lax.axis_size("seq")
    place = lax.axis_index("seq")
    peers = lax.axis_size("tensor")
    side = lax.axis_index("tensor")
    tokens, channels = keyval.shape
    repeat = BLOCK // cycle
    groups_local = blocks.shape[0]
    group_width = channels // groups_local
    narrow = channels // cycle
    unit = min(narrow, group_width)
    chunks = narrow // unit

    rows, columns = out_weight.shape
    cores = 2
    line = math.gcd(cycle // cores, 4)
    turns = cycle // (cores * line)
    z, turn, core = place // (turns * cores), place // cores % turns, place % cores

    def move(value, by_line, by_turn, by_core, held=None):
        held = range(line) if held is None else held
        pairs = [
            (
                (i * turns + m) * cores + c,
                ((i + by_line) * turns + (m + by_turn) % turns) * cores + (c + by_core) % cores,
            )
            for i in held
            for m in range(turns)
            for c in range(cores)
        ]
        return lax.ppermute(value, "seq", pairs)

    eighth = columns // 8
    fits = (
        eighth % 256 == 0
        and unit * cycle == rows * cores * turns
        and line == 4
        and chunks == 2
        and turns == 2
    )
    cut = 3 * eighth if fits else 0
    weight = lax.all_gather(out_weight[:, cut:], "seq", axis=0, tiled=True)

    exchange = functools.partial(
        lax.all_to_all, axis_name="seq", split_axis=0, concat_axis=0, tiled=True
    )
    filters = exchange(pack_filters(filter_values, cycle, chunks, unit))
    signals = []
    for g in range(chunks):
        signals.append(exchange(pack_signal(keyval, g, cycle, unit)))

    after = lax.optimization_barrier
    if cut:
        own = out_weight[:, :cut]
        up, down = move(own, 1, 0, 0, range(0, 3)), move(own, -1, 0, 0, range(1, 4))
        up, down, own, _ = after((up, down, own, signals[0]))
        near = [jnp.stack([own, jnp.where(z == 0, down, up)])]
        far = [move(near[0], 0, 1, 0)]
        up2, down2 = move(up, 1, 0, 0, range(1, 3)), move(down, -1, 0, 0, range(1, 3))
        up2, down2, _ = after((up2, down2, signals[1]))
        near.append(jnp.where(z == 0, down2, jnp.where(z == 3, up2, down))[None])
        far.append(move(near[1], 0, 1, 0))
        up3, down3 = move(up2, 1, 0, 0, range(2, 3)), move(down2, -1, 0, 0, range(1, 2))

    group = (jnp.arange(chunks, dtype=jnp.int32) * cycle + place) * unit // group_width
    kept_blocks = jnp.take(blocks, group, axis=0)
    kept_rows = (
        kept_blocks[:, :, None] * repeat + jnp.arange(repeat, dtype=jnp.int32)
    ).reshape(chunks, -1)
    local_index = jnp.arange(tokens, dtype=jnp.int32)
    cosine, sine = tables(kept_rows[:, :, None], local_index[None, None, :], tokens)
    ahead = jnp.concatenate(
        [jnp.concatenate([cosine, sine], axis=2), jnp.concatenate([-sine, cosine], axis=2)],
        axis=1,
    ).astype(BF16)
    cosine, sine = tables(kept_rows[:, None, :], local_index[None, :, None], tokens)
    back = jnp.concatenate(
        [jnp.concatenate([cosine, -sine], axis=2), jnp.concatenate([sine, cosine], axis=2)],
        axis=1,
    ).astype(BF16)
    cycle_index = jnp.arange(cycle, dtype=jnp.int32)
    twist = jnp.concatenate(
        tables(local_index[:, None], cycle_index[None, :], cycle * tokens), axis=1
    )

    hidden, starts, dones = [], [], []
    for g in range(chunks):
        dones.append(exchange(convolve(g, twist, ahead, back, signals[g], filters)))
    if cut:
        up3, down3, _ = after((up3, down3, dones[0]))
        near.append(
            jnp.where(
                z == 0, down3, jnp.where(z == 1, down2, jnp.where(z == 2, up2, up3))
            )[None]
        )
        far.append(move(near[2], 0, 1, 0))
        near[0], far[0], near[1], far[1], near[2], _ = after(
            (near[0], far[0], near[1], far[1], near[2], dones[1])
        )
        lined = []
        for n, f in zip(near, far):
            lined += [n, f, move(n, 0, 0, 1), move(f, 0, 0, 1)]
    for g in range(chunks):
        own = gate(dones[g], keyval, gating, skip_gain, g)
        for shift in range(peers):
            piece = own
            if shift:
                piece = lax.ppermute(
                    own, "tensor", [(t, (t + shift) % peers) for t in range(peers)]
                )
            hidden.append(piece)
            source = lax.rem(side + peers - shift, peers)
            starts.append(source * channels + g * cycle * unit)
    result = None
    if cut:
        order = ((0, 1, 2, 3), (1, 0, 2, 3), (2, 1, 3, 0), (3, 2, 1, 0))
        places = [start // (rows * cores * turns) for start in starts]
        places += [sum(jnp.where(z == i, order[i][j], 0) for i in range(4)) for j in range(4)]
        places += [
            (lax.rem(turn + m, turns) * cores + lax.rem(core + c, cores)) * rows
            for c in range(cores)
            for m in range(turns)
        ]
        places = jnp.stack(places).astype(jnp.int32)
        result = mix_line(hidden, places, lined, ((0, 1), (2,), (3,)), columns)
    starts = jnp.stack(starts).astype(jnp.int32)
    return mix(hidden, starts, weight, cut, columns, result)


def solution(mesh):
    placed = (
        P("seq", "tensor"),
        P("seq", "tensor"),
        P("tensor"),
        P(None, None, None, "seq", "tensor"),
        P("tensor", None),
        P("seq", "tensor"),
    )
    return jax.shard_map(
        body, mesh=mesh, in_specs=placed, out_specs=P("seq", "tensor"), check_vma=False
    )
```

```python
import functools
import math

import jax
import jax.numpy as jnp
from jax import lax
from jax.experimental import pallas as pl
from jax.experimental.pallas import tpu as pltpu
from jax.sharding import PartitionSpec as P

BLOCK = 64
ROWS = 16
VMEM = 48 * 2**20
F32 = jnp.float32
BF16 = jnp.bfloat16


def tables(first_index, second_index, length):
    phase = first_index * second_index % length
    angle = 2.0 * math.pi / length * phase.astype(F32)
    return (jnp.cos(angle), jnp.sin(angle))


def real_forward(values):
    n = len(values)
    if n == 2:
        return [(values[0] + values[1], None), (values[0] - values[1], None)]
    even, odd = real_forward(values[0::2]), real_forward(values[1::2])
    half = n // 2
    out = [None] * (half + 1)
    for p in range(half // 2 + 1):
        (er, ei), (dr, di) = even[p], odd[p]
        if p == 0:
            out[0], out[half] = (er + dr, None), (er - dr, None)
        elif 2 * p == half:
            out[p] = (er, -dr)
        else:
            c, s = math.cos(2 * math.pi * p / n), math.sin(2 * math.pi * p / n)
            tr, ti = dr * c + di * s, di * c - dr * s
            out[p], out[half - p] = (er + tr, ei + ti), (er - tr, ti - ei)
    return out


def real_inverse(freqs):
    half = len(freqs) - 1
    if half == 1:
        return [freqs[0][0] + freqs[1][0], freqs[0][0] - freqs[1][0]]
    n = 2 * half
    even, odd = [None] * (half // 2 + 1), [None] * (half // 2 + 1)
    for p in range(half // 2 + 1):
        (ar, ai), (br, bi) = freqs[p], freqs[half - p]
        if p == 0:
            even[0], odd[0] = (ar + br, None), (ar - br, None)
        elif 2 * p == half:
            even[p], odd[p] = (ar + ar, None), (-(ai + ai), None)
        else:
            c, s = math.cos(2 * math.pi * p / n), math.sin(2 * math.pi * p / n)
            dr, di = ar - br, ai + bi
            even[p], odd[p] = (ar + br, ai - bi), (dr * c - di * s, dr * s + di * c)
    out = [None] * n
    out[0::2], out[1::2] = real_inverse(even), real_inverse(odd)
    return out


def conv_kernel(twist_ref, ahead_ref, back_ref, x_ref, filter_ref, out_ref, first_ref, turned_ref):
    cycle, tokens, unit = x_ref.shape
    kept = filter_ref.shape[2] // 2
    per = max(1, 256 // unit)
    width = per * unit

    def twist(rows):
        block = twist_ref[rows, :]
        return [
            (block[:, p : p + 1], block[:, cycle + p : cycle + p + 1]) for p in range(cycle)
        ]

    def ahead(step, carry):
        start = pl.multiple_of(step * ROWS, ROWS)
        rows = pl.ds(start, ROWS)
        freqs = real_forward([x_ref[a, rows, :].astype(F32) for a in range(cycle)])
        for p, (c, s) in enumerate(twist(rows)):
            real, imaginary = freqs[min(p, cycle - p)]
            if imaginary is None:
                fr, fi = real * c, -(real * s)
            elif 2 * p > cycle:
                fr, fi = real * c - imaginary * s, -(imaginary * c + real * s)
            else:
                fr, fi = real * c + imaginary * s, imaginary * c - real * s
            lanes = slice(p * unit, (p + 1) * unit)
            first_ref[rows, lanes] = fr.astype(BF16)
            first_ref[pl.ds(tokens + start, ROWS), lanes] = fi.astype(BF16)
        return carry

    lax.fori_loop(0, tokens // ROWS, ahead, 0)

    def middle(step, carry):
        lanes = pl.ds(pl.multiple_of(step * width, width), width)
        spectrum = jnp.dot(ahead_ref[0], first_ref[:, lanes], preferred_element_type=F32)
        reals, imaginaries = [], []
        for u in range(per):
            part = filter_ref[step * per + u, 0].astype(F32)
            hr, hi = part[:kept], part[kept:]
            own = slice(u * unit, (u + 1) * unit)
            sr, si = spectrum[:kept, own], spectrum[kept:, own]
            reals.append(hr * sr - hi * si)
            imaginaries.append(hr * si + hi * sr)
        product = jnp.concatenate(
            [jnp.concatenate(reals, axis=1), jnp.concatenate(imaginaries, axis=1)], axis=0
        ).astype(BF16)
        turned_ref[:, lanes] = jnp.dot(back_ref[0], product, preferred_element_type=F32)
        return carry

    lax.fori_loop(0, cycle // per, middle, 0)

    def behind(step, carry):
        start = pl.multiple_of(step * ROWS, ROWS)
        rows = pl.ds(start, ROWS)
        parts = []
        for p, (c, s) in enumerate(twist(rows)):
            lanes = slice(p * unit, (p + 1) * unit)
            br = turned_ref[rows, lanes]
            bi = turned_ref[pl.ds(tokens + start, ROWS), lanes]
            parts.append(
                (
                    (br * c - bi * s).astype(BF16).astype(F32),
                    (br * s + bi * c).astype(BF16).astype(F32),
                )
            )
        half = cycle // 2
        freqs = [(parts[0][0] * 2.0, None)]
        for p in range(1, half):
            (ur, ui), (vr, vi) = parts[p], parts[cycle - p]
            freqs.append((ur + vr, ui - vi))
        freqs.append((parts[half][0] * 2.0, None))
        scale = 0.5 / (cycle * tokens)
        for a, value in enumerate(real_inverse(freqs)):
            out_ref[a, rows, :] = (value * scale).astype(BF16)
        return carry

    lax.fori_loop(0, tokens // ROWS, behind, 0)


def convolve(chunk, twist, ahead, back, signal, filters):
    cycle, tokens, unit = signal.shape
    kept = filters.shape[2] // 2
    flops = 4 * 2 * kept * 2 * tokens * cycle * unit
    return pl.pallas_call(
        conv_kernel,
        grid=(1,),
        out_shape=jax.ShapeDtypeStruct(signal.shape, BF16),
        in_specs=[
            pl.BlockSpec(twist.shape, lambda i: (0, 0)),
            pl.BlockSpec((1, *ahead.shape[1:]), lambda i: (chunk, 0, 0)),
            pl.BlockSpec((1, *back.shape[1:]), lambda i: (chunk, 0, 0)),
            pl.BlockSpec(signal.shape, lambda i: (0, 0, 0)),
            pl.BlockSpec((cycle, 1, 2 * kept, unit), lambda i: (0, chunk, 0, 0)),
        ],
        out_specs=pl.BlockSpec(signal.shape, lambda i: (0, 0, 0)),
        scratch_shapes=[
            pltpu.VMEM((2 * tokens, cycle * unit), BF16),
            pltpu.VMEM((2 * tokens, cycle * unit), F32),
        ],
        compiler_params=pltpu.CompilerParams(vmem_limit_bytes=VMEM),
        cost_estimate=pl.CostEstimate(
            flops=flops, bytes_accessed=16 * signal.size, transcendentals=0
        ),
        name="convolve",
    )(twist, ahead, back, signal, filters)


def pack_kernel(unit, x_ref, out_ref):
    for d in range(out_ref.shape[0]):
        out_ref[d] = x_ref[:, d * unit : (d + 1) * unit]


def pack_signal(keyval, chunk, cycle, unit):
    tokens = keyval.shape[0]
    wide = max(1, min(cycle, 512 // unit))
    steps = cycle // wide
    return pl.pallas_call(
        functools.partial(pack_kernel, unit),
        grid=(steps,),
        out_shape=jax.ShapeDtypeStruct((cycle, tokens, unit), BF16),
        in_specs=[pl.BlockSpec((tokens, wide * unit), lambda i: (0, chunk * steps + i))],
        out_specs=pl.BlockSpec((wide, tokens, unit), lambda i: (i, 0, 0)),
        compiler_params=pltpu.CompilerParams(vmem_limit_bytes=VMEM),
        cost_estimate=pl.CostEstimate(
            flops=0, bytes_accessed=4 * tokens * cycle * unit, transcendentals=0
        ),
        name="pack_signal",
    )(keyval)


def pack_filter_kernel(unit, f_ref, out_ref):
    for d in range(out_ref.shape[0]):
        out_ref[d, 0] = f_ref[:, 0, d * unit : (d + 1) * unit].astype(BF16)


def pack_filters(filter_values, cycle, chunks, unit):
    channels = filter_values.shape[-1]
    rows = filter_values.size // channels
    flat = filter_values.reshape(rows, 1, channels)
    wide = max(1, min(cycle, 512 // unit))
    steps = cycle // wide
    return pl.pallas_call(
        functools.partial(pack_filter_kernel, unit),
        grid=(chunks, steps),
        out_shape=jax.ShapeDtypeStruct((cycle, chunks, rows, unit), BF16),
        in_specs=[pl.BlockSpec((rows, 1, wide * unit), lambda g, i: (0, 0, g * steps + i))],
        out_specs=pl.BlockSpec((wide, 1, rows, unit), lambda g, i: (i, g, 0, 0)),
        compiler_params=pltpu.CompilerParams(vmem_limit_bytes=VMEM),
        cost_estimate=pl.CostEstimate(
            flops=0, bytes_accessed=6 * filter_values.size, transcendentals=0
        ),
        name="pack_filters",
    )(flat)


def gate_kernel(unit, c_ref, x_ref, g_ref, s_ref, out_ref):
    for d in range(c_ref.shape[0]):
        lanes = slice(d * unit, (d + 1) * unit)
        direct = s_ref[0:1, lanes] * x_ref[:, lanes].astype(F32)
        value = g_ref[:, lanes].astype(F32) * (c_ref[d].astype(F32) + direct)
        out_ref[:, lanes] = value.astype(BF16)


def gate(convolved, keyval, gating, skip_gain, chunk):
    cycle, tokens, unit = convolved.shape
    wide = max(1, min(cycle, 512 // unit))
    steps = cycle // wide
    lanes = wide * unit
    return pl.pallas_call(
        functools.partial(gate_kernel, unit),
        grid=(steps,),
        out_shape=jax.ShapeDtypeStruct((tokens, cycle * unit), BF16),
        in_specs=[
            pl.BlockSpec((wide, tokens, unit), lambda i: (i, 0, 0)),
            pl.BlockSpec((tokens, lanes), lambda i: (0, chunk * steps + i)),
            pl.BlockSpec((tokens, lanes), lambda i: (0, chunk * steps + i)),
            pl.BlockSpec((1, lanes), lambda i: (0, chunk * steps + i)),
        ],
        out_specs=pl.BlockSpec((tokens, lanes), lambda i: (0, i)),
        compiler_params=pltpu.CompilerParams(vmem_limit_bytes=VMEM),
        cost_estimate=pl.CostEstimate(
            flops=0, bytes_accessed=8 * convolved.size, transcendentals=0
        ),
        name="gate",
    )(convolved, keyval, gating, skip_gain.reshape(1, -1))


def mix_kernel(pieces, start_ref, *refs):
    w_ref, out_ref = refs[pieces], refs[-1]
    total = None
    for k in range(pieces):
        depth = refs[k].shape[1]
        start = pl.multiple_of(start_ref[k], depth)
        part = jnp.dot(
            refs[k][...], w_ref[pl.ds(start, depth), :], preferred_element_type=F32
        )
        total = part if total is None else total + part
    out_ref[...] = total.astype(BF16)


def mix(hidden, starts, weight, low, columns, result):
    tokens = hidden[0].shape[0]
    depth, part = weight.shape
    tile = min(256, part)
    first = low // tile
    pieces = len(hidden)
    before = [] if result is None else [result]
    return pl.pallas_call(
        functools.partial(mix_kernel, pieces),
        grid=(part // tile,),
        out_shape=jax.ShapeDtypeStruct((tokens, columns), BF16),
        in_specs=[pl.BlockSpec(memory_space=pltpu.SMEM)]
        + [pl.BlockSpec(h.shape, lambda i: (0, 0)) for h in hidden]
        + [pl.BlockSpec((depth, tile), lambda i: (0, i))]
        + [pl.BlockSpec(memory_space=pl.ANY) for _ in before],
        out_specs=pl.BlockSpec((tokens, tile), lambda i: (0, first + i)),
        input_output_aliases={pieces + 2: 0} if before else {},
        compiler_params=pltpu.CompilerParams(vmem_limit_bytes=VMEM),
        cost_estimate=pl.CostEstimate(
            flops=2 * tokens * depth * part, bytes_accessed=2 * depth * part, transcendentals=0
        ),
        name="mix",
    )(starts, *hidden, weight, *before)


def line_kernel(pieces, steps, place_ref, *refs):
    w_refs, out_ref, held_ref = refs[pieces:-2], refs[-2], refs[-1]
    depth = w_refs[0].shape[1]

    @pl.when(pl.program_id(0) == 0)
    def _():
        for k in range(pieces):
            held_ref[place_ref[k]] = refs[k][...]

    blocks = len(w_refs) // len(steps)
    total = None
    for g, near in enumerate(steps):
        for b in range(blocks):
            lanes = pl.ds(pl.multiple_of(place_ref[2 * pieces + b], depth), depth)
            for n, j in enumerate(near):
                left = held_ref[place_ref[pieces + j], :, lanes]
                part = jnp.dot(left, w_refs[g * blocks + b][n], preferred_element_type=F32)
                total = part if total is None else total + part
    out_ref[...] = total.astype(BF16)


def mix_line(hidden, places, weights, steps, columns):
    tokens, width = hidden[0].shape
    depth, part = weights[0].shape[1:]
    tile = min(256, part)
    pieces = len(hidden)
    return pl.pallas_call(
        functools.partial(line_kernel, pieces, steps),
        grid=(part // tile,),
        out_shape=jax.ShapeDtypeStruct((tokens, columns), BF16),
        in_specs=[pl.BlockSpec(memory_space=pltpu.SMEM)]
        + [pl.BlockSpec(h.shape, lambda i: (0, 0)) for h in hidden]
        + [pl.BlockSpec((w.shape[0], depth, tile), lambda i: (0, 0, i)) for w in weights],
        out_specs=pl.BlockSpec((tokens, tile), lambda i: (0, i)),
        scratch_shapes=[pltpu.VMEM((pieces, tokens, width), BF16)],
        compiler_params=pltpu.CompilerParams(vmem_limit_bytes=VMEM),
        cost_estimate=pl.CostEstimate(
            flops=2 * tokens * pieces * width * part,
            bytes_accessed=2 * pieces * width * part,
            transcendentals=0,
        ),
        name="mix_line",
    )(places, *hidden, *weights)


def body(keyval, gating, skip_gain, filter_values, blocks, out_weight):
    cycle = lax.axis_size("seq")
    place = lax.axis_index("seq")
    peers = lax.axis_size("tensor")
    side = lax.axis_index("tensor")
    tokens, channels = keyval.shape
    repeat = BLOCK // cycle
    groups_local = blocks.shape[0]
    group_width = channels // groups_local
    narrow = channels // cycle
    unit = min(narrow, group_width)
    chunks = narrow // unit

    rows, columns = out_weight.shape
    cores = 2
    line = math.gcd(cycle // cores, 4)
    turns = cycle // (cores * line)
    z, turn, core = place // (turns * cores), place // cores % turns, place % cores

    def move(value, by_line, by_turn, by_core, held=None):
        held = range(line) if held is None else held
        pairs = [
            (
                (i * turns + m) * cores + c,
                ((i + by_line) * turns + (m + by_turn) % turns) * cores + (c + by_core) % cores,
            )
            for i in held
            for m in range(turns)
            for c in range(cores)
        ]
        return lax.ppermute(value, "seq", pairs)

    eighth = columns // 8
    fits = (
        eighth % 256 == 0
        and unit * cycle == rows * cores * turns
        and line == 4
        and chunks == 2
        and turns == 2
    )
    cut = 3 * eighth if fits else 0
    weight = lax.all_gather(out_weight[:, cut:], "seq", axis=0, tiled=True)

    exchange = functools.partial(
        lax.all_to_all, axis_name="seq", split_axis=0, concat_axis=0, tiled=True
    )
    filters = exchange(pack_filters(filter_values, cycle, chunks, unit))
    packed = [pack_signal(keyval, g, cycle, unit) for g in range(chunks)]
    signals = [exchange(packed[0])]
    after = lax.optimization_barrier
    if cut:
        own = out_weight[:, :cut]
        up, down = move(own, 1, 0, 0, range(0, 3)), move(own, -1, 0, 0, range(1, 4))
        up, down, own, filters, signals[0], packed[1] = after(
            (up, down, own, filters, signals[0], packed[1])
        )
        near = [jnp.stack([own, jnp.where(z == 0, down, up)])]
        far = [move(near[0], 0, 1, 0)]
        up2, down2 = move(up, 1, 0, 0, range(1, 3)), move(down, -1, 0, 0, range(1, 3))
    for g in range(1, chunks):
        signals.append(exchange(packed[g]))

    group = (jnp.arange(chunks, dtype=jnp.int32) * cycle + place) * unit // group_width
    kept_blocks = jnp.take(blocks, group, axis=0)
    kept_rows = (
        kept_blocks[:, :, None] * repeat + jnp.arange(repeat, dtype=jnp.int32)
    ).reshape(chunks, -1)
    local_index = jnp.arange(tokens, dtype=jnp.int32)
    cosine, sine = tables(kept_rows[:, :, None], local_index[None, None, :], tokens)
    ahead = jnp.concatenate(
        [jnp.concatenate([cosine, sine], axis=2), jnp.concatenate([-sine, cosine], axis=2)],
        axis=1,
    ).astype(BF16)
    cosine, sine = tables(kept_rows[:, None, :], local_index[None, :, None], tokens)
    back = jnp.concatenate(
        [jnp.concatenate([cosine, -sine], axis=2), jnp.concatenate([sine, cosine], axis=2)],
        axis=1,
    ).astype(BF16)
    cycle_index = jnp.arange(cycle, dtype=jnp.int32)
    twist = jnp.concatenate(
        tables(local_index[:, None], cycle_index[None, :], cycle * tokens), axis=1
    )

    hidden, starts = [], []

    def finish(g, done):
        own = gate(done, keyval, gating, skip_gain, g)
        for shift in range(peers):
            piece = own
            if shift:
                piece = lax.ppermute(
                    own, "tensor", [(t, (t + shift) % peers) for t in range(peers)]
                )
            hidden.append(piece)
            source = lax.rem(side + peers - shift, peers)
            starts.append(source * channels + g * cycle * unit)

    lined = []
    if cut:
        done = exchange(convolve(0, twist, ahead, back, signals[0], filters))
        last = convolve(1, twist, ahead, back, signals[1], filters)
        up2, down2, done, last, down = after((up2, down2, done, last, down))
        near.append(jnp.where(z == 0, down2, jnp.where(z == 3, up2, down))[None])
        far.append(move(near[1], 0, 1, 0))
        up3, down3 = move(up2, 1, 0, 0, range(2, 3)), move(down2, -1, 0, 0, range(1, 2))
        finish(0, done)
        done = exchange(last)
        up3, down3, done, near[0], far[0], near[1], far[1] = after(
            (up3, down3, done, near[0], far[0], near[1], far[1])
        )
        near.append(
            jnp.where(
                z == 0, down3, jnp.where(z == 1, down2, jnp.where(z == 2, up2, up3))
            )[None]
        )
        far.append(move(near[2], 0, 1, 0))
        for n, f in zip(near, far):
            lined += [n, f, move(n, 0, 0, 1), move(f, 0, 0, 1)]
        finish(1, done)
    else:
        for g in range(chunks):
            finish(g, exchange(convolve(g, twist, ahead, back, signals[g], filters)))
    result = None
    if cut:
        order = ((0, 1, 2, 3), (1, 0, 2, 3), (2, 1, 3, 0), (3, 2, 1, 0))
        places = [start // (rows * cores * turns) for start in starts]
        places += [sum(jnp.where(z == i, order[i][j], 0) for i in range(4)) for j in range(4)]
        places += [
            (lax.rem(turn + m, turns) * cores + lax.rem(core + c, cores)) * rows
            for c in range(cores)
            for m in range(turns)
        ]
        places = jnp.stack(places).astype(jnp.int32)
        result = mix_line(hidden, places, lined, ((0, 1), (2,), (3,)), columns)
    starts = jnp.stack(starts).astype(jnp.int32)
    return mix(hidden, starts, weight, cut, columns, result)


def solution(mesh):
    placed = (
        P("seq", "tensor"),
        P("seq", "tensor"),
        P("tensor"),
        P(None, None, None, "seq", "tensor"),
        P("tensor", None),
        P("seq", "tensor"),
    )
    return jax.shard_map(
        body, mesh=mesh, in_specs=placed, out_specs=P("seq", "tensor"), check_vma=False
    )
```

```python
import functools
import math

import jax
import jax.numpy as jnp
from jax import lax
from jax.experimental import pallas as pl
from jax.experimental.pallas import tpu as pltpu
from jax.sharding import PartitionSpec as P

BLOCK = 64
ROWS = 16
VMEM = 48 * 2**20
F32 = jnp.float32
BF16 = jnp.bfloat16


def tables(first_index, second_index, length):
    phase = first_index * second_index % length
    angle = 2.0 * math.pi / length * phase.astype(F32)
    return (jnp.cos(angle), jnp.sin(angle))


def real_forward(values):
    n = len(values)
    if n == 2:
        return [(values[0] + values[1], None), (values[0] - values[1], None)]
    even, odd = real_forward(values[0::2]), real_forward(values[1::2])
    half = n // 2
    out = [None] * (half + 1)
    for p in range(half // 2 + 1):
        (er, ei), (dr, di) = even[p], odd[p]
        if p == 0:
            out[0], out[half] = (er + dr, None), (er - dr, None)
        elif 2 * p == half:
            out[p] = (er, -dr)
        else:
            c, s = math.cos(2 * math.pi * p / n), math.sin(2 * math.pi * p / n)
            tr, ti = dr * c + di * s, di * c - dr * s
            out[p], out[half - p] = (er + tr, ei + ti), (er - tr, ti - ei)
    return out


def real_inverse(freqs):
    half = len(freqs) - 1
    if half == 1:
        return [freqs[0][0] + freqs[1][0], freqs[0][0] - freqs[1][0]]
    n = 2 * half
    even, odd = [None] * (half // 2 + 1), [None] * (half // 2 + 1)
    for p in range(half // 2 + 1):
        (ar, ai), (br, bi) = freqs[p], freqs[half - p]
        if p == 0:
            even[0], odd[0] = (ar + br, None), (ar - br, None)
        elif 2 * p == half:
            even[p], odd[p] = (ar + ar, None), (-(ai + ai), None)
        else:
            c, s = math.cos(2 * math.pi * p / n), math.sin(2 * math.pi * p / n)
            dr, di = ar - br, ai + bi
            even[p], odd[p] = (ar + br, ai - bi), (dr * c - di * s, dr * s + di * c)
    out = [None] * n
    out[0::2], out[1::2] = real_inverse(even), real_inverse(odd)
    return out


def conv_kernel(twist_ref, ahead_ref, back_ref, x_ref, filter_ref, out_ref, first_ref, turned_ref):
    cycle, tokens, unit = x_ref.shape
    kept = filter_ref.shape[2] // 2
    per = max(1, 256 // unit)
    width = per * unit

    def twist(rows):
        block = twist_ref[rows, :]
        return [
            (block[:, p : p + 1], block[:, cycle + p : cycle + p + 1]) for p in range(cycle)
        ]

    def ahead(step, carry):
        start = pl.multiple_of(step * ROWS, ROWS)
        rows = pl.ds(start, ROWS)
        freqs = real_forward([x_ref[a, rows, :].astype(F32) for a in range(cycle)])
        for p, (c, s) in enumerate(twist(rows)):
            real, imaginary = freqs[min(p, cycle - p)]
            if imaginary is None:
                fr, fi = real * c, -(real * s)
            elif 2 * p > cycle:
                fr, fi = real * c - imaginary * s, -(imaginary * c + real * s)
            else:
                fr, fi = real * c + imaginary * s, imaginary * c - real * s
            lanes = slice(p * unit, (p + 1) * unit)
            first_ref[rows, lanes] = fr.astype(BF16)
            first_ref[pl.ds(tokens + start, ROWS), lanes] = fi.astype(BF16)
        return carry

    lax.fori_loop(0, tokens // ROWS, ahead, 0)

    def middle(step, carry):
        lanes = pl.ds(pl.multiple_of(step * width, width), width)
        spectrum = jnp.dot(ahead_ref[0], first_ref[:, lanes], preferred_element_type=F32)
        reals, imaginaries = [], []
        for u in range(per):
            part = filter_ref[step * per + u, 0].astype(F32)
            hr, hi = part[:kept], part[kept:]
            own = slice(u * unit, (u + 1) * unit)
            sr, si = spectrum[:kept, own], spectrum[kept:, own]
            reals.append(hr * sr - hi * si)
            imaginaries.append(hr * si + hi * sr)
        product = jnp.concatenate(
            [jnp.concatenate(reals, axis=1), jnp.concatenate(imaginaries, axis=1)], axis=0
        ).astype(BF16)
        turned_ref[:, lanes] = jnp.dot(back_ref[0], product, preferred_element_type=F32)
        return carry

    lax.fori_loop(0, cycle // per, middle, 0)

    def behind(step, carry):
        start = pl.multiple_of(step * ROWS, ROWS)
        rows = pl.ds(start, ROWS)
        parts = []
        for p, (c, s) in enumerate(twist(rows)):
            lanes = slice(p * unit, (p + 1) * unit)
            br = turned_ref[rows, lanes]
            bi = turned_ref[pl.ds(tokens + start, ROWS), lanes]
            parts.append(
                (
                    (br * c - bi * s).astype(BF16).astype(F32),
                    (br * s + bi * c).astype(BF16).astype(F32),
                )
            )
        half = cycle // 2
        freqs = [(parts[0][0] * 2.0, None)]
        for p in range(1, half):
            (ur, ui), (vr, vi) = parts[p], parts[cycle - p]
            freqs.append((ur + vr, ui - vi))
        freqs.append((parts[half][0] * 2.0, None))
        scale = 0.5 / (cycle * tokens)
        for a, value in enumerate(real_inverse(freqs)):
            out_ref[a, rows, :] = (value * scale).astype(BF16)
        return carry

    lax.fori_loop(0, tokens // ROWS, behind, 0)


def convolve(chunk, twist, ahead, back, signal, filters):
    cycle, tokens, unit = signal.shape
    kept = filters.shape[2] // 2
    flops = 4 * 2 * kept * 2 * tokens * cycle * unit
    return pl.pallas_call(
        conv_kernel,
        grid=(1,),
        out_shape=jax.ShapeDtypeStruct(signal.shape, BF16),
        in_specs=[
            pl.BlockSpec(twist.shape, lambda i: (0, 0)),
            pl.BlockSpec((1, *ahead.shape[1:]), lambda i: (chunk, 0, 0)),
            pl.BlockSpec((1, *back.shape[1:]), lambda i: (chunk, 0, 0)),
            pl.BlockSpec(signal.shape, lambda i: (0, 0, 0)),
            pl.BlockSpec((cycle, 1, 2 * kept, unit), lambda i: (0, chunk, 0, 0)),
        ],
        out_specs=pl.BlockSpec(signal.shape, lambda i: (0, 0, 0)),
        scratch_shapes=[
            pltpu.VMEM((2 * tokens, cycle * unit), BF16),
            pltpu.VMEM((2 * tokens, cycle * unit), F32),
        ],
        compiler_params=pltpu.CompilerParams(vmem_limit_bytes=VMEM),
        cost_estimate=pl.CostEstimate(
            flops=flops, bytes_accessed=16 * signal.size, transcendentals=0
        ),
        name="convolve",
    )(twist, ahead, back, signal, filters)


def pack_kernel(unit, x_ref, out_ref):
    for d in range(out_ref.shape[0]):
        out_ref[d] = x_ref[:, d * unit : (d + 1) * unit]


def pack_signal(keyval, chunk, cycle, unit):
    tokens = keyval.shape[0]
    wide = max(1, min(cycle, 512 // unit))
    steps = cycle // wide
    return pl.pallas_call(
        functools.partial(pack_kernel, unit),
        grid=(steps,),
        out_shape=jax.ShapeDtypeStruct((cycle, tokens, unit), BF16),
        in_specs=[pl.BlockSpec((tokens, wide * unit), lambda i: (0, chunk * steps + i))],
        out_specs=pl.BlockSpec((wide, tokens, unit), lambda i: (i, 0, 0)),
        compiler_params=pltpu.CompilerParams(vmem_limit_bytes=VMEM),
        cost_estimate=pl.CostEstimate(
            flops=0, bytes_accessed=4 * tokens * cycle * unit, transcendentals=0
        ),
        name="pack_signal",
    )(keyval)


def pack_filter_kernel(unit, f_ref, out_ref):
    for d in range(out_ref.shape[0]):
        out_ref[d, 0] = f_ref[:, 0, d * unit : (d + 1) * unit].astype(BF16)


def pack_filters(filter_values, cycle, chunks, unit):
    channels = filter_values.shape[-1]
    rows = filter_values.size // channels
    flat = filter_values.reshape(rows, 1, channels)
    wide = max(1, min(cycle, 512 // unit))
    steps = cycle // wide
    return pl.pallas_call(
        functools.partial(pack_filter_kernel, unit),
        grid=(chunks, steps),
        out_shape=jax.ShapeDtypeStruct((cycle, chunks, rows, unit), BF16),
        in_specs=[pl.BlockSpec((rows, 1, wide * unit), lambda g, i: (0, 0, g * steps + i))],
        out_specs=pl.BlockSpec((wide, 1, rows, unit), lambda g, i: (i, g, 0, 0)),
        compiler_params=pltpu.CompilerParams(vmem_limit_bytes=VMEM),
        cost_estimate=pl.CostEstimate(
            flops=0, bytes_accessed=6 * filter_values.size, transcendentals=0
        ),
        name="pack_filters",
    )(flat)


def gate_kernel(unit, c_ref, x_ref, g_ref, s_ref, out_ref):
    for d in range(c_ref.shape[0]):
        lanes = slice(d * unit, (d + 1) * unit)
        direct = s_ref[0:1, lanes] * x_ref[:, lanes].astype(F32)
        value = g_ref[:, lanes].astype(F32) * (c_ref[d].astype(F32) + direct)
        out_ref[:, lanes] = value.astype(BF16)


def gate(convolved, keyval, gating, skip_gain, chunk):
    cycle, tokens, unit = convolved.shape
    wide = max(1, min(cycle, 512 // unit))
    steps = cycle // wide
    lanes = wide * unit
    return pl.pallas_call(
        functools.partial(gate_kernel, unit),
        grid=(steps,),
        out_shape=jax.ShapeDtypeStruct((tokens, cycle * unit), BF16),
        in_specs=[
            pl.BlockSpec((wide, tokens, unit), lambda i: (i, 0, 0)),
            pl.BlockSpec((tokens, lanes), lambda i: (0, chunk * steps + i)),
            pl.BlockSpec((tokens, lanes), lambda i: (0, chunk * steps + i)),
            pl.BlockSpec((1, lanes), lambda i: (0, chunk * steps + i)),
        ],
        out_specs=pl.BlockSpec((tokens, lanes), lambda i: (0, i)),
        compiler_params=pltpu.CompilerParams(vmem_limit_bytes=VMEM),
        cost_estimate=pl.CostEstimate(
            flops=0, bytes_accessed=8 * convolved.size, transcendentals=0
        ),
        name="gate",
    )(convolved, keyval, gating, skip_gain.reshape(1, -1))


def mix_kernel(pieces, start_ref, *refs):
    w_ref, out_ref, total_ref = refs[pieces], refs[-2], refs[-1]
    step = pl.program_id(1)
    columns = w_ref.shape[1]
    tile = min(256, columns)
    for k in range(pieces):

        @pl.when(step == k)
        def _(k=k):
            for low in range(0, columns, tile):
                lanes = slice(low, low + tile)
                part = jnp.dot(refs[k][...], w_ref[:, lanes], preferred_element_type=F32)
                if k:
                    part = total_ref[:, lanes] + part
                if k < pieces - 1:
                    total_ref[:, lanes] = part
                else:
                    out_ref[:, lanes] = part.astype(BF16)


def mix(hidden, starts, weight, low, columns, result):
    tokens, width = hidden[0].shape
    depth, part = weight.shape
    tile = min(1024, part)
    first = low // tile
    pieces = len(hidden)
    before = [] if result is None else [result]
    return pl.pallas_call(
        functools.partial(mix_kernel, pieces),
        grid_spec=pltpu.PrefetchScalarGridSpec(
            num_scalar_prefetch=1,
            grid=(part // tile, pieces),
            in_specs=[pl.BlockSpec(h.shape, lambda i, k, s: (0, 0)) for h in hidden]
            + [pl.BlockSpec((width, tile), lambda i, k, s: (s[k], i))]
            + [pl.BlockSpec(memory_space=pl.ANY) for _ in before],
            out_specs=pl.BlockSpec((tokens, tile), lambda i, k, s: (0, first + i)),
            scratch_shapes=[pltpu.VMEM((tokens, tile), F32)],
        ),
        out_shape=jax.ShapeDtypeStruct((tokens, columns), BF16),
        input_output_aliases={pieces + 2: 0} if before else {},
        compiler_params=pltpu.CompilerParams(vmem_limit_bytes=VMEM),
        cost_estimate=pl.CostEstimate(
            flops=2 * tokens * depth * part, bytes_accessed=2 * depth * part, transcendentals=0
        ),
        name="mix",
    )(starts, *hidden, weight, *before)


def body(keyval, gating, skip_gain, filter_values, blocks, out_weight):
    cycle = lax.axis_size("seq")
    place = lax.axis_index("seq")
    peers = lax.axis_size("tensor")
    side = lax.axis_index("tensor")
    tokens, channels = keyval.shape
    repeat = BLOCK // cycle
    groups_local = blocks.shape[0]
    group_width = channels // groups_local
    narrow = channels // cycle
    unit = min(narrow, group_width)
    chunks = narrow // unit

    columns = out_weight.shape[1]
    eighth = columns // 8
    bounds = [0, 4 * eighth, columns] if eighth % 256 == 0 else [0, columns]
    weights = [
        lax.all_gather(out_weight[:, low:high], "seq", axis=0, tiled=True)
        for low, high in zip(bounds[:-1], bounds[1:])
    ]

    exchange = functools.partial(
        lax.all_to_all, axis_name="seq", split_axis=0, concat_axis=0, tiled=True
    )
    signals = [exchange(pack_signal(keyval, g, cycle, unit)) for g in range(chunks)]
    filters = exchange(pack_filters(filter_values, cycle, chunks, unit))

    group = (jnp.arange(chunks, dtype=jnp.int32) * cycle + place) * unit // group_width
    kept_blocks = jnp.take(blocks, group, axis=0)
    kept_rows = (
        kept_blocks[:, :, None] * repeat + jnp.arange(repeat, dtype=jnp.int32)
    ).reshape(chunks, -1)
    local_index = jnp.arange(tokens, dtype=jnp.int32)
    cosine, sine = tables(kept_rows[:, :, None], local_index[None, None, :], tokens)
    ahead = jnp.concatenate(
        [jnp.concatenate([cosine, sine], axis=2), jnp.concatenate([-sine, cosine], axis=2)],
        axis=1,
    ).astype(BF16)
    cosine, sine = tables(kept_rows[:, None, :], local_index[None, :, None], tokens)
    back = jnp.concatenate(
        [jnp.concatenate([cosine, -sine], axis=2), jnp.concatenate([sine, cosine], axis=2)],
        axis=1,
    ).astype(BF16)
    cycle_index = jnp.arange(cycle, dtype=jnp.int32)
    twist = jnp.concatenate(
        tables(local_index[:, None], cycle_index[None, :], cycle * tokens), axis=1
    )

    hidden, starts = [], []
    for g in range(chunks):
        done = exchange(convolve(g, twist, ahead, back, signals[g], filters))
        own = gate(done, keyval, gating, skip_gain, g)
        for shift in range(peers):
            if shift == 0:
                piece = own
            else:
                piece = lax.ppermute(
                    own, "tensor", [(t, (t + shift) % peers) for t in range(peers)]
                )
            hidden.append(piece)
            source = lax.rem(side + peers - shift, peers)
            starts.append(source * chunks + g)
    starts = jnp.stack(starts).astype(jnp.int32)
    result = None
    for low, weight in zip(bounds[:-1], weights):
        result = mix(hidden, starts, weight, low, columns, result)
    return result


def solution(mesh):
    placed = (
        P("seq", "tensor"),
        P("seq", "tensor"),
        P("tensor"),
        P(None, None, None, "seq", "tensor"),
        P("tensor", None),
        P("seq", "tensor"),
    )
    return jax.shard_map(
        body, mesh=mesh, in_specs=placed, out_specs=P("seq", "tensor"), check_vma=False
    )
```

```python
import functools
import math

import jax
import jax.numpy as jnp
from jax import lax
from jax.experimental import pallas as pl
from jax.experimental.pallas import tpu as pltpu
from jax.sharding import PartitionSpec as P

BLOCK = 64
ROWS = 16
VMEM = 48 * 2**20
F32 = jnp.float32
BF16 = jnp.bfloat16


def tables(first_index, second_index, length):
    phase = first_index * second_index % length
    angle = 2.0 * math.pi / length * phase.astype(F32)
    return (jnp.cos(angle), jnp.sin(angle))


def real_forward(values):
    n = len(values)
    if n == 2:
        return [(values[0] + values[1], None), (values[0] - values[1], None)]
    even, odd = real_forward(values[0::2]), real_forward(values[1::2])
    half = n // 2
    out = [None] * (half + 1)
    for p in range(half // 2 + 1):
        (er, ei), (dr, di) = even[p], odd[p]
        if p == 0:
            out[0], out[half] = (er + dr, None), (er - dr, None)
        elif 2 * p == half:
            out[p] = (er, -dr)
        else:
            c, s = math.cos(2 * math.pi * p / n), math.sin(2 * math.pi * p / n)
            tr, ti = dr * c + di * s, di * c - dr * s
            out[p], out[half - p] = (er + tr, ei + ti), (er - tr, ti - ei)
    return out


def real_inverse(freqs):
    half = len(freqs) - 1
    if half == 1:
        return [freqs[0][0] + freqs[1][0], freqs[0][0] - freqs[1][0]]
    n = 2 * half
    even, odd = [None] * (half // 2 + 1), [None] * (half // 2 + 1)
    for p in range(half // 2 + 1):
        (ar, ai), (br, bi) = freqs[p], freqs[half - p]
        if p == 0:
            even[0], odd[0] = (ar + br, None), (ar - br, None)
        elif 2 * p == half:
            even[p], odd[p] = (ar + ar, None), (-(ai + ai), None)
        else:
            c, s = math.cos(2 * math.pi * p / n), math.sin(2 * math.pi * p / n)
            dr, di = ar - br, ai + bi
            even[p], odd[p] = (ar + br, ai - bi), (dr * c - di * s, dr * s + di * c)
    out = [None] * n
    out[0::2], out[1::2] = real_inverse(even), real_inverse(odd)
    return out


def conv_kernel(twist_ref, ahead_ref, back_ref, x_ref, filter_ref, out_ref, first_ref, turned_ref):
    cycle, tokens, unit = x_ref.shape
    kept = filter_ref.shape[2] // 2
    per = max(1, 256 // unit)
    width = per * unit

    def twist(rows):
        block = twist_ref[rows, :]
        return [
            (block[:, p : p + 1], block[:, cycle + p : cycle + p + 1]) for p in range(cycle)
        ]

    def ahead(step, carry):
        start = pl.multiple_of(step * ROWS, ROWS)
        rows = pl.ds(start, ROWS)
        freqs = real_forward([x_ref[a, rows, :].astype(F32) for a in range(cycle)])
        for p, (c, s) in enumerate(twist(rows)):
            real, imaginary = freqs[min(p, cycle - p)]
            if imaginary is None:
                fr, fi = real * c, -(real * s)
            elif 2 * p > cycle:
                fr, fi = real * c - imaginary * s, -(imaginary * c + real * s)
            else:
                fr, fi = real * c + imaginary * s, imaginary * c - real * s
            lanes = slice(p * unit, (p + 1) * unit)
            first_ref[rows, lanes] = fr.astype(BF16)
            first_ref[pl.ds(tokens + start, ROWS), lanes] = fi.astype(BF16)
        return carry

    lax.fori_loop(0, tokens // ROWS, ahead, 0)

    def middle(step, carry):
        lanes = pl.ds(pl.multiple_of(step * width, width), width)
        spectrum = jnp.dot(ahead_ref[0], first_ref[:, lanes], preferred_element_type=F32)
        reals, imaginaries = [], []
        for u in range(per):
            part = filter_ref[step * per + u, 0].astype(F32)
            hr, hi = part[:kept], part[kept:]
            own = slice(u * unit, (u + 1) * unit)
            sr, si = spectrum[:kept, own], spectrum[kept:, own]
            reals.append(hr * sr - hi * si)
            imaginaries.append(hr * si + hi * sr)
        product = jnp.concatenate(
            [jnp.concatenate(reals, axis=1), jnp.concatenate(imaginaries, axis=1)], axis=0
        ).astype(BF16)
        turned_ref[:, lanes] = jnp.dot(back_ref[0], product, preferred_element_type=F32)
        return carry

    lax.fori_loop(0, cycle // per, middle, 0)

    def behind(step, carry):
        start = pl.multiple_of(step * ROWS, ROWS)
        rows = pl.ds(start, ROWS)
        parts = []
        for p, (c, s) in enumerate(twist(rows)):
            lanes = slice(p * unit, (p + 1) * unit)
            br = turned_ref[rows, lanes]
            bi = turned_ref[pl.ds(tokens + start, ROWS), lanes]
            parts.append(
                (
                    (br * c - bi * s).astype(BF16).astype(F32),
                    (br * s + bi * c).astype(BF16).astype(F32),
                )
            )
        half = cycle // 2
        freqs = [(parts[0][0] * 2.0, None)]
        for p in range(1, half):
            (ur, ui), (vr, vi) = parts[p], parts[cycle - p]
            freqs.append((ur + vr, ui - vi))
        freqs.append((parts[half][0] * 2.0, None))
        scale = 0.5 / (cycle * tokens)
        for a, value in enumerate(real_inverse(freqs)):
            out_ref[a, rows, :] = (value * scale).astype(BF16)
        return carry

    lax.fori_loop(0, tokens // ROWS, behind, 0)


def convolve(chunk, twist, ahead, back, signal, filters):
    cycle, tokens, unit = signal.shape
    kept = filters.shape[2] // 2
    flops = 4 * 2 * kept * 2 * tokens * cycle * unit
    return pl.pallas_call(
        conv_kernel,
        grid=(1,),
        out_shape=jax.ShapeDtypeStruct(signal.shape, BF16),
        in_specs=[
            pl.BlockSpec(twist.shape, lambda i: (0, 0)),
            pl.BlockSpec((1, *ahead.shape[1:]), lambda i: (chunk, 0, 0)),
            pl.BlockSpec((1, *back.shape[1:]), lambda i: (chunk, 0, 0)),
            pl.BlockSpec(signal.shape, lambda i: (0, 0, 0)),
            pl.BlockSpec((cycle, 1, 2 * kept, unit), lambda i: (0, chunk, 0, 0)),
        ],
        out_specs=pl.BlockSpec(signal.shape, lambda i: (0, 0, 0)),
        scratch_shapes=[
            pltpu.VMEM((2 * tokens, cycle * unit), BF16),
            pltpu.VMEM((2 * tokens, cycle * unit), F32),
        ],
        compiler_params=pltpu.CompilerParams(vmem_limit_bytes=VMEM),
        cost_estimate=pl.CostEstimate(
            flops=flops, bytes_accessed=16 * signal.size, transcendentals=0
        ),
        name="convolve",
    )(twist, ahead, back, signal, filters)


def pack_kernel(unit, x_ref, out_ref):
    for d in range(out_ref.shape[0]):
        out_ref[d] = x_ref[:, d * unit : (d + 1) * unit]


def pack_signal(keyval, chunk, cycle, unit):
    tokens = keyval.shape[0]
    wide = max(1, min(cycle, 512 // unit))
    steps = cycle // wide
    return pl.pallas_call(
        functools.partial(pack_kernel, unit),
        grid=(steps,),
        out_shape=jax.ShapeDtypeStruct((cycle, tokens, unit), BF16),
        in_specs=[pl.BlockSpec((tokens, wide * unit), lambda i: (0, chunk * steps + i))],
        out_specs=pl.BlockSpec((wide, tokens, unit), lambda i: (i, 0, 0)),
        compiler_params=pltpu.CompilerParams(vmem_limit_bytes=VMEM),
        cost_estimate=pl.CostEstimate(
            flops=0, bytes_accessed=4 * tokens * cycle * unit, transcendentals=0
        ),
        name="pack_signal",
    )(keyval)


def pack_filter_kernel(unit, f_ref, out_ref):
    for d in range(out_ref.shape[0]):
        out_ref[d, 0] = f_ref[:, 0, d * unit : (d + 1) * unit].astype(BF16)


def pack_filters(filter_values, cycle, chunks, unit):
    channels = filter_values.shape[-1]
    rows = filter_values.size // channels
    flat = filter_values.reshape(rows, 1, channels)
    wide = max(1, min(cycle, 512 // unit))
    steps = cycle // wide
    return pl.pallas_call(
        functools.partial(pack_filter_kernel, unit),
        grid=(chunks, steps),
        out_shape=jax.ShapeDtypeStruct((cycle, chunks, rows, unit), BF16),
        in_specs=[pl.BlockSpec((rows, 1, wide * unit), lambda g, i: (0, 0, g * steps + i))],
        out_specs=pl.BlockSpec((wide, 1, rows, unit), lambda g, i: (i, g, 0, 0)),
        compiler_params=pltpu.CompilerParams(vmem_limit_bytes=VMEM),
        cost_estimate=pl.CostEstimate(
            flops=0, bytes_accessed=6 * filter_values.size, transcendentals=0
        ),
        name="pack_filters",
    )(flat)


def gate_kernel(unit, c_ref, x_ref, g_ref, s_ref, out_ref):
    for d in range(c_ref.shape[0]):
        lanes = slice(d * unit, (d + 1) * unit)
        direct = s_ref[0:1, lanes] * x_ref[:, lanes].astype(F32)
        value = g_ref[:, lanes].astype(F32) * (c_ref[d].astype(F32) + direct)
        out_ref[:, lanes] = value.astype(BF16)


def gate(convolved, keyval, gating, skip_gain, chunk):
    cycle, tokens, unit = convolved.shape
    wide = max(1, min(cycle, 512 // unit))
    steps = cycle // wide
    lanes = wide * unit
    return pl.pallas_call(
        functools.partial(gate_kernel, unit),
        grid=(steps,),
        out_shape=jax.ShapeDtypeStruct((tokens, cycle * unit), BF16),
        in_specs=[
            pl.BlockSpec((wide, tokens, unit), lambda i: (i, 0, 0)),
            pl.BlockSpec((tokens, lanes), lambda i: (0, chunk * steps + i)),
            pl.BlockSpec((tokens, lanes), lambda i: (0, chunk * steps + i)),
            pl.BlockSpec((1, lanes), lambda i: (0, chunk * steps + i)),
        ],
        out_specs=pl.BlockSpec((tokens, lanes), lambda i: (0, i)),
        compiler_params=pltpu.CompilerParams(vmem_limit_bytes=VMEM),
        cost_estimate=pl.CostEstimate(
            flops=0, bytes_accessed=8 * convolved.size, transcendentals=0
        ),
        name="gate",
    )(convolved, keyval, gating, skip_gain.reshape(1, -1))


def mix_kernel(pieces, start_ref, *refs):
    w_ref, out_ref, total_ref = refs[pieces], refs[-2], refs[-1]
    step = pl.program_id(1)
    columns = w_ref.shape[1]
    tile = min(256, columns)
    for k in range(pieces):

        @pl.when(step == k)
        def _(k=k):
            for low in range(0, columns, tile):
                lanes = slice(low, low + tile)
                part = jnp.dot(refs[k][...], w_ref[:, lanes], preferred_element_type=F32)
                if k:
                    part = total_ref[:, lanes] + part
                if k < pieces - 1:
                    total_ref[:, lanes] = part
                else:
                    out_ref[:, lanes] = part.astype(BF16)


def mix(hidden, starts, weight, low, columns, result):
    tokens, width = hidden[0].shape
    depth, part = weight.shape
    tile = min(1024, part)
    first = low // tile
    pieces = len(hidden)
    before = [] if result is None else [result]
    return pl.pallas_call(
        functools.partial(mix_kernel, pieces),
        grid_spec=pltpu.PrefetchScalarGridSpec(
            num_scalar_prefetch=1,
            grid=(part // tile, pieces),
            in_specs=[pl.BlockSpec(h.shape, lambda i, k, s: (0, 0)) for h in hidden]
            + [pl.BlockSpec((width, tile), lambda i, k, s: (s[k], i))]
            + [pl.BlockSpec(memory_space=pl.ANY) for _ in before],
            out_specs=pl.BlockSpec((tokens, tile), lambda i, k, s: (0, first + i)),
            scratch_shapes=[pltpu.VMEM((tokens, tile), F32)],
        ),
        out_shape=jax.ShapeDtypeStruct((tokens, columns), BF16),
        input_output_aliases={pieces + 2: 0} if before else {},
        compiler_params=pltpu.CompilerParams(vmem_limit_bytes=VMEM),
        cost_estimate=pl.CostEstimate(
            flops=2 * tokens * depth * part, bytes_accessed=2 * depth * part, transcendentals=0
        ),
        name="mix",
    )(starts, *hidden, weight, *before)


def pair_kernel(pieces, place_ref, *refs):
    a_ref, b_ref, out_ref, total_ref = refs[pieces : pieces + 4]
    step = pl.program_id(1)
    columns = a_ref.shape[1]
    tile = min(256, columns)
    for k in range(pieces):
        for place, w_ref in enumerate((a_ref, b_ref)):

            @pl.when(jnp.logical_and(step == k, place_ref[2 * pieces + k] == place))
            def _(k=k, w_ref=w_ref):
                for low in range(0, columns, tile):
                    lanes = slice(low, low + tile)
                    part = jnp.dot(refs[k][...], w_ref[:, lanes], preferred_element_type=F32)
                    if k:
                        part = total_ref[:, lanes] + part
                    if k < pieces - 1:
                        total_ref[:, lanes] = part
                    else:
                        out_ref[:, lanes] = part.astype(BF16)


def mix_pair(hidden, places, weights, columns):
    tokens, width = hidden[0].shape
    depth, part = weights[0].shape
    tile = min(512, part)
    pieces = len(hidden)
    return pl.pallas_call(
        functools.partial(pair_kernel, pieces),
        grid_spec=pltpu.PrefetchScalarGridSpec(
            num_scalar_prefetch=1,
            grid=(part // tile, pieces),
            in_specs=[pl.BlockSpec(h.shape, lambda i, k, s: (0, 0)) for h in hidden]
            + [
                pl.BlockSpec((width, tile), lambda i, k, s: (s[k], i)),
                pl.BlockSpec((width, tile), lambda i, k, s: (s[pieces + k], i)),
            ],
            out_specs=pl.BlockSpec((tokens, tile), lambda i, k, s: (0, i)),
            scratch_shapes=[pltpu.VMEM((tokens, tile), F32)],
        ),
        out_shape=jax.ShapeDtypeStruct((tokens, columns), BF16),
        compiler_params=pltpu.CompilerParams(vmem_limit_bytes=VMEM),
        cost_estimate=pl.CostEstimate(
            flops=4 * tokens * depth * part, bytes_accessed=4 * depth * part, transcendentals=0
        ),
        name="mix_pair",
    )(places, *hidden, *weights)


def body(keyval, gating, skip_gain, filter_values, blocks, out_weight):
    cycle = lax.axis_size("seq")
    place = lax.axis_index("seq")
    peers = lax.axis_size("tensor")
    side = lax.axis_index("tensor")
    tokens, channels = keyval.shape
    repeat = BLOCK // cycle
    groups_local = blocks.shape[0]
    group_width = channels // groups_local
    narrow = channels // cycle
    unit = min(narrow, group_width)
    chunks = narrow // unit

    columns = out_weight.shape[1]
    half = cycle // 2
    width = cycle * unit
    paired = columns % 2048 == 0 and peers == 2 and half * out_weight.shape[0] == channels
    cut = columns // 2 if paired else 0
    if paired:
        sides = [list(range(half)), list(range(half, cycle))]
        gather = functools.partial(
            lax.all_gather, axis_name="seq", axis=0, tiled=True, axis_index_groups=sides
        )
        own = out_weight[:, :cut]
        other = lax.ppermute(own, "seq", [(i, (i + half) % cycle) for i in range(cycle)])
        pair = [gather(own), gather(other)]
    weight = lax.all_gather(out_weight[:, cut:], "seq", axis=0, tiled=True)

    exchange = functools.partial(
        lax.all_to_all, axis_name="seq", split_axis=0, concat_axis=0, tiled=True
    )
    signals = [exchange(pack_signal(keyval, g, cycle, unit)) for g in range(chunks)]
    filters = exchange(pack_filters(filter_values, cycle, chunks, unit))

    group = (jnp.arange(chunks, dtype=jnp.int32) * cycle + place) * unit // group_width
    kept_blocks = jnp.take(blocks, group, axis=0)
    kept_rows = (
        kept_blocks[:, :, None] * repeat + jnp.arange(repeat, dtype=jnp.int32)
    ).reshape(chunks, -1)
    local_index = jnp.arange(tokens, dtype=jnp.int32)
    cosine, sine = tables(kept_rows[:, :, None], local_index[None, None, :], tokens)
    ahead = jnp.concatenate(
        [jnp.concatenate([cosine, sine], axis=2), jnp.concatenate([-sine, cosine], axis=2)],
        axis=1,
    ).astype(BF16)
    cosine, sine = tables(kept_rows[:, None, :], local_index[None, :, None], tokens)
    back = jnp.concatenate(
        [jnp.concatenate([cosine, -sine], axis=2), jnp.concatenate([sine, cosine], axis=2)],
        axis=1,
    ).astype(BF16)
    cycle_index = jnp.arange(cycle, dtype=jnp.int32)
    twist = jnp.concatenate(
        tables(local_index[:, None], cycle_index[None, :], cycle * tokens), axis=1
    )

    hidden, starts = [], []
    for g in range(chunks):
        done = exchange(convolve(g, twist, ahead, back, signals[g], filters))
        own = gate(done, keyval, gating, skip_gain, g)
        for shift in range(peers):
            if shift == 0:
                piece = own
            else:
                piece = lax.ppermute(
                    own, "tensor", [(t, (t + shift) % peers) for t in range(peers)]
                )
            hidden.append(piece)
            source = lax.rem(side + peers - shift, peers)
            starts.append(source * chunks + g)
    result = None
    if paired:
        which = [(place // half + side + shift) % 2 for g in range(chunks) for shift in range(2)]
        rows = [jnp.full((), g, jnp.int32) for g in range(chunks) for shift in range(2)]
        places = jnp.stack(rows + rows + which).astype(jnp.int32)
        result = mix_pair(hidden, places, pair, columns)
    starts = jnp.stack(starts).astype(jnp.int32)
    return mix(hidden, starts, weight, cut, columns, result)


def solution(mesh):
    placed = (
        P("seq", "tensor"),
        P("seq", "tensor"),
        P("tensor"),
        P(None, None, None, "seq", "tensor"),
        P("tensor", None),
        P("seq", "tensor"),
    )
    return jax.shard_map(
        body, mesh=mesh, in_specs=placed, out_specs=P("seq", "tensor"), check_vma=False
    )
```

```python
import functools
import math

import jax
import jax.numpy as jnp
from jax import lax
from jax.experimental import pallas as pl
from jax.experimental.pallas import tpu as pltpu
from jax.sharding import PartitionSpec as P

BLOCK = 64
ROWS = 16
VMEM = 48 * 2**20
F32 = jnp.float32
BF16 = jnp.bfloat16


def tables(first_index, second_index, length):
    phase = first_index * second_index % length
    angle = 2.0 * math.pi / length * phase.astype(F32)
    return (jnp.cos(angle), jnp.sin(angle))


def real_forward(values):
    n = len(values)
    if n == 2:
        return [(values[0] + values[1], None), (values[0] - values[1], None)]
    even, odd = real_forward(values[0::2]), real_forward(values[1::2])
    half = n // 2
    out = [None] * (half + 1)
    for p in range(half // 2 + 1):
        (er, ei), (dr, di) = even[p], odd[p]
        if p == 0:
            out[0], out[half] = (er + dr, None), (er - dr, None)
        elif 2 * p == half:
            out[p] = (er, -dr)
        else:
            c, s = math.cos(2 * math.pi * p / n), math.sin(2 * math.pi * p / n)
            tr, ti = dr * c + di * s, di * c - dr * s
            out[p], out[half - p] = (er + tr, ei + ti), (er - tr, ti - ei)
    return out


def real_inverse(freqs):
    half = len(freqs) - 1
    if half == 1:
        return [freqs[0][0] + freqs[1][0], freqs[0][0] - freqs[1][0]]
    n = 2 * half
    even, odd = [None] * (half // 2 + 1), [None] * (half // 2 + 1)
    for p in range(half // 2 + 1):
        (ar, ai), (br, bi) = freqs[p], freqs[half - p]
        if p == 0:
            even[0], odd[0] = (ar + br, None), (ar - br, None)
        elif 2 * p == half:
            even[p], odd[p] = (ar + ar, None), (-(ai + ai), None)
        else:
            c, s = math.cos(2 * math.pi * p / n), math.sin(2 * math.pi * p / n)
            dr, di = ar - br, ai + bi
            even[p], odd[p] = (ar + br, ai - bi), (dr * c - di * s, dr * s + di * c)
    out = [None] * n
    out[0::2], out[1::2] = real_inverse(even), real_inverse(odd)
    return out


def conv_kernel(twist_ref, ahead_ref, back_ref, x_ref, filter_ref, out_ref, first_ref, turned_ref):
    cycle, tokens, unit = x_ref.shape
    kept = filter_ref.shape[2] // 2
    per = max(1, 256 // unit)
    width = per * unit

    def twist(rows):
        block = twist_ref[rows, :]
        return [
            (block[:, p : p + 1], block[:, cycle + p : cycle + p + 1]) for p in range(cycle)
        ]

    def ahead(step, carry):
        start = pl.multiple_of(step * ROWS, ROWS)
        rows = pl.ds(start, ROWS)
        freqs = real_forward([x_ref[a, rows, :].astype(F32) for a in range(cycle)])
        for p, (c, s) in enumerate(twist(rows)):
            real, imaginary = freqs[min(p, cycle - p)]
            if imaginary is None:
                fr, fi = real * c, -(real * s)
            elif 2 * p > cycle:
                fr, fi = real * c - imaginary * s, -(imaginary * c + real * s)
            else:
                fr, fi = real * c + imaginary * s, imaginary * c - real * s
            lanes = slice(p * unit, (p + 1) * unit)
            first_ref[rows, lanes] = fr.astype(BF16)
            first_ref[pl.ds(tokens + start, ROWS), lanes] = fi.astype(BF16)
        return carry

    lax.fori_loop(0, tokens // ROWS, ahead, 0)

    def middle(step, carry):
        lanes = pl.ds(pl.multiple_of(step * width, width), width)
        spectrum = jnp.dot(ahead_ref[0], first_ref[:, lanes], preferred_element_type=F32)
        reals, imaginaries = [], []
        for u in range(per):
            part = filter_ref[step * per + u, 0].astype(F32)
            hr, hi = part[:kept], part[kept:]
            own = slice(u * unit, (u + 1) * unit)
            sr, si = spectrum[:kept, own], spectrum[kept:, own]
            reals.append(hr * sr - hi * si)
            imaginaries.append(hr * si + hi * sr)
        product = jnp.concatenate(
            [jnp.concatenate(reals, axis=1), jnp.concatenate(imaginaries, axis=1)], axis=0
        ).astype(BF16)
        turned_ref[:, lanes] = jnp.dot(back_ref[0], product, preferred_element_type=F32)
        return carry

    lax.fori_loop(0, cycle // per, middle, 0)

    def behind(step, carry):
        start = pl.multiple_of(step * ROWS, ROWS)
        rows = pl.ds(start, ROWS)
        parts = []
        for p, (c, s) in enumerate(twist(rows)):
            lanes = slice(p * unit, (p + 1) * unit)
            br = turned_ref[rows, lanes]
            bi = turned_ref[pl.ds(tokens + start, ROWS), lanes]
            parts.append(
                (
                    (br * c - bi * s).astype(BF16).astype(F32),
                    (br * s + bi * c).astype(BF16).astype(F32),
                )
            )
        half = cycle // 2
        freqs = [(parts[0][0] * 2.0, None)]
        for p in range(1, half):
            (ur, ui), (vr, vi) = parts[p], parts[cycle - p]
            freqs.append((ur + vr, ui - vi))
        freqs.append((parts[half][0] * 2.0, None))
        scale = 0.5 / (cycle * tokens)
        for a, value in enumerate(real_inverse(freqs)):
            out_ref[a, rows, :] = (value * scale).astype(BF16)
        return carry

    lax.fori_loop(0, tokens // ROWS, behind, 0)


def convolve(chunk, twist, ahead, back, signal, filters):
    cycle, tokens, unit = signal.shape
    kept = filters.shape[2] // 2
    flops = 4 * 2 * kept * 2 * tokens * cycle * unit
    return pl.pallas_call(
        conv_kernel,
        grid=(1,),
        out_shape=jax.ShapeDtypeStruct(signal.shape, BF16),
        in_specs=[
            pl.BlockSpec(twist.shape, lambda i: (0, 0)),
            pl.BlockSpec((1, *ahead.shape[1:]), lambda i: (chunk, 0, 0)),
            pl.BlockSpec((1, *back.shape[1:]), lambda i: (chunk, 0, 0)),
            pl.BlockSpec(signal.shape, lambda i: (0, 0, 0)),
            pl.BlockSpec((cycle, 1, 2 * kept, unit), lambda i: (0, chunk, 0, 0)),
        ],
        out_specs=pl.BlockSpec(signal.shape, lambda i: (0, 0, 0)),
        scratch_shapes=[
            pltpu.VMEM((2 * tokens, cycle * unit), BF16),
            pltpu.VMEM((2 * tokens, cycle * unit), F32),
        ],
        compiler_params=pltpu.CompilerParams(vmem_limit_bytes=VMEM),
        cost_estimate=pl.CostEstimate(
            flops=flops, bytes_accessed=16 * signal.size, transcendentals=0
        ),
        name="convolve",
    )(twist, ahead, back, signal, filters)


def pack_kernel(unit, x_ref, out_ref):
    for d in range(out_ref.shape[0]):
        out_ref[d] = x_ref[:, d * unit : (d + 1) * unit]


def pack_signal(keyval, chunk, cycle, unit):
    tokens = keyval.shape[0]
    wide = max(1, min(cycle, 512 // unit))
    steps = cycle // wide
    return pl.pallas_call(
        functools.partial(pack_kernel, unit),
        grid=(steps,),
        out_shape=jax.ShapeDtypeStruct((cycle, tokens, unit), BF16),
        in_specs=[pl.BlockSpec((tokens, wide * unit), lambda i: (0, chunk * steps + i))],
        out_specs=pl.BlockSpec((wide, tokens, unit), lambda i: (i, 0, 0)),
        compiler_params=pltpu.CompilerParams(vmem_limit_bytes=VMEM),
        cost_estimate=pl.CostEstimate(
            flops=0, bytes_accessed=4 * tokens * cycle * unit, transcendentals=0
        ),
        name="pack_signal",
    )(keyval)


def pack_filter_kernel(unit, f_ref, out_ref):
    for d in range(out_ref.shape[0]):
        out_ref[d, 0] = f_ref[:, 0, d * unit : (d + 1) * unit].astype(BF16)


def pack_filters(filter_values, cycle, chunks, unit):
    channels = filter_values.shape[-1]
    rows = filter_values.size // channels
    flat = filter_values.reshape(rows, 1, channels)
    wide = max(1, min(cycle, 512 // unit))
    steps = cycle // wide
    return pl.pallas_call(
        functools.partial(pack_filter_kernel, unit),
        grid=(chunks, steps),
        out_shape=jax.ShapeDtypeStruct((cycle, chunks, rows, unit), BF16),
        in_specs=[pl.BlockSpec((rows, 1, wide * unit), lambda g, i: (0, 0, g * steps + i))],
        out_specs=pl.BlockSpec((wide, 1, rows, unit), lambda g, i: (i, g, 0, 0)),
        compiler_params=pltpu.CompilerParams(vmem_limit_bytes=VMEM),
        cost_estimate=pl.CostEstimate(
            flops=0, bytes_accessed=6 * filter_values.size, transcendentals=0
        ),
        name="pack_filters",
    )(flat)


def gate_kernel(unit, c_ref, x_ref, g_ref, s_ref, out_ref):
    for d in range(c_ref.shape[0]):
        lanes = slice(d * unit, (d + 1) * unit)
        direct = s_ref[0:1, lanes] * x_ref[:, lanes].astype(F32)
        value = g_ref[:, lanes].astype(F32) * (c_ref[d].astype(F32) + direct)
        out_ref[:, lanes] = value.astype(BF16)


def gate(convolved, keyval, gating, skip_gain, chunk):
    cycle, tokens, unit = convolved.shape
    wide = max(1, min(cycle, 512 // unit))
    steps = cycle // wide
    lanes = wide * unit
    return pl.pallas_call(
        functools.partial(gate_kernel, unit),
        grid=(steps,),
        out_shape=jax.ShapeDtypeStruct((tokens, cycle * unit), BF16),
        in_specs=[
            pl.BlockSpec((wide, tokens, unit), lambda i: (i, 0, 0)),
            pl.BlockSpec((tokens, lanes), lambda i: (0, chunk * steps + i)),
            pl.BlockSpec((tokens, lanes), lambda i: (0, chunk * steps + i)),
            pl.BlockSpec((1, lanes), lambda i: (0, chunk * steps + i)),
        ],
        out_specs=pl.BlockSpec((tokens, lanes), lambda i: (0, i)),
        compiler_params=pltpu.CompilerParams(vmem_limit_bytes=VMEM),
        cost_estimate=pl.CostEstimate(
            flops=0, bytes_accessed=8 * convolved.size, transcendentals=0
        ),
        name="gate",
    )(convolved, keyval, gating, skip_gain.reshape(1, -1))


def mix_kernel(pieces, start_ref, *refs):
    w_ref, out_ref, total_ref = refs[pieces], refs[-2], refs[-1]
    step = pl.program_id(1)
    columns = w_ref.shape[1]
    tile = min(256, columns)
    for k in range(pieces):

        @pl.when(step == k)
        def _(k=k):
            for low in range(0, columns, tile):
                lanes = slice(low, low + tile)
                part = jnp.dot(refs[k][...], w_ref[:, lanes], preferred_element_type=F32)
                if k:
                    part = total_ref[:, lanes] + part
                if k < pieces - 1:
                    total_ref[:, lanes] = part
                else:
                    out_ref[:, lanes] = part.astype(BF16)


def mix(hidden, starts, weight, low, columns, result):
    tokens, width = hidden[0].shape
    depth, part = weight.shape
    tile = min(1024, part)
    first = low // tile
    pieces = len(hidden)
    before = [] if result is None else [result]
    return pl.pallas_call(
        functools.partial(mix_kernel, pieces),
        grid_spec=pltpu.PrefetchScalarGridSpec(
            num_scalar_prefetch=1,
            grid=(part // tile, pieces),
            in_specs=[pl.BlockSpec(h.shape, lambda i, k, s: (0, 0)) for h in hidden]
            + [pl.BlockSpec((width, tile), lambda i, k, s: (s[k], i))]
            + [pl.BlockSpec(memory_space=pl.ANY) for _ in before],
            out_specs=pl.BlockSpec((tokens, tile), lambda i, k, s: (0, first + i)),
            scratch_shapes=[pltpu.VMEM((tokens, tile), F32)],
        ),
        out_shape=jax.ShapeDtypeStruct((tokens, columns), BF16),
        input_output_aliases={pieces + 2: 0} if before else {},
        compiler_params=pltpu.CompilerParams(vmem_limit_bytes=VMEM),
        cost_estimate=pl.CostEstimate(
            flops=2 * tokens * depth * part, bytes_accessed=2 * depth * part, transcendentals=0
        ),
        name="mix",
    )(starts, *hidden, weight, *before)


def pair_kernel(pieces, place_ref, *refs):
    a_ref, b_ref, out_ref, total_ref = refs[pieces : pieces + 4]
    step = pl.program_id(1)
    columns = a_ref.shape[1]
    tile = min(256, columns)
    for k in range(pieces):
        for place, w_ref in enumerate((a_ref, b_ref)):

            @pl.when(jnp.logical_and(step == k, place_ref[2 * pieces + k] == place))
            def _(k=k, w_ref=w_ref):
                for low in range(0, columns, tile):
                    lanes = slice(low, low + tile)
                    part = jnp.dot(refs[k][...], w_ref[:, lanes], preferred_element_type=F32)
                    if k:
                        part = total_ref[:, lanes] + part
                    if k < pieces - 1:
                        total_ref[:, lanes] = part
                    else:
                        out_ref[:, lanes] = part.astype(BF16)


def mix_pair(hidden, places, weights, columns):
    tokens, width = hidden[0].shape
    depth, part = weights[0].shape
    tile = min(1024, part)
    pieces = len(hidden)
    return pl.pallas_call(
        functools.partial(pair_kernel, pieces),
        grid_spec=pltpu.PrefetchScalarGridSpec(
            num_scalar_prefetch=1,
            grid=(part // tile, pieces),
            in_specs=[pl.BlockSpec(h.shape, lambda i, k, s: (0, 0)) for h in hidden]
            + [
                pl.BlockSpec((width, tile), lambda i, k, s: (s[k], i)),
                pl.BlockSpec((width, tile), lambda i, k, s: (s[pieces + k], i)),
            ],
            out_specs=pl.BlockSpec((tokens, tile), lambda i, k, s: (0, i)),
            scratch_shapes=[pltpu.VMEM((tokens, tile), F32)],
        ),
        out_shape=jax.ShapeDtypeStruct((tokens, columns), BF16),
        compiler_params=pltpu.CompilerParams(vmem_limit_bytes=VMEM),
        cost_estimate=pl.CostEstimate(
            flops=4 * tokens * depth * part, bytes_accessed=4 * depth * part, transcendentals=0
        ),
        name="mix_pair",
    )(places, *hidden, *weights)


def body(keyval, gating, skip_gain, filter_values, blocks, out_weight):
    cycle = lax.axis_size("seq")
    place = lax.axis_index("seq")
    peers = lax.axis_size("tensor")
    side = lax.axis_index("tensor")
    tokens, channels = keyval.shape
    repeat = BLOCK // cycle
    groups_local = blocks.shape[0]
    group_width = channels // groups_local
    narrow = channels // cycle
    unit = min(narrow, group_width)
    chunks = narrow // unit

    packed_filters = pack_filters(filter_values, cycle, chunks, unit)
    columns = out_weight.shape[1]
    half = cycle // 2
    width = cycle * unit
    paired = columns % 2048 == 0 and peers == 2 and half * out_weight.shape[0] == channels
    cut = columns // 2 if paired else 0
    if paired:
        sides = [list(range(half)), list(range(half, cycle))]
        gather = functools.partial(
            lax.all_gather, axis_name="seq", axis=0, tiled=True, axis_index_groups=sides
        )
        own = out_weight[:, :cut]
        sent, packed_filters = lax.optimization_barrier((own, packed_filters))
        other = lax.ppermute(sent, "seq", [(i, (i + half) % cycle) for i in range(cycle)])
        pair = [gather(own), gather(other)]
    weight = lax.all_gather(out_weight[:, cut:], "seq", axis=0, tiled=True)

    exchange = functools.partial(
        lax.all_to_all, axis_name="seq", split_axis=0, concat_axis=0, tiled=True
    )
    filters = exchange(packed_filters)
    signals = [exchange(pack_signal(keyval, g, cycle, unit)) for g in range(chunks)]

    group = (jnp.arange(chunks, dtype=jnp.int32) * cycle + place) * unit // group_width
    kept_blocks = jnp.take(blocks, group, axis=0)
    kept_rows = (
        kept_blocks[:, :, None] * repeat + jnp.arange(repeat, dtype=jnp.int32)
    ).reshape(chunks, -1)
    local_index = jnp.arange(tokens, dtype=jnp.int32)
    cosine, sine = tables(kept_rows[:, :, None], local_index[None, None, :], tokens)
    ahead = jnp.concatenate(
        [jnp.concatenate([cosine, sine], axis=2), jnp.concatenate([-sine, cosine], axis=2)],
        axis=1,
    ).astype(BF16)
    cosine, sine = tables(kept_rows[:, None, :], local_index[None, :, None], tokens)
    back = jnp.concatenate(
        [jnp.concatenate([cosine, -sine], axis=2), jnp.concatenate([sine, cosine], axis=2)],
        axis=1,
    ).astype(BF16)
    cycle_index = jnp.arange(cycle, dtype=jnp.int32)
    twist = jnp.concatenate(
        tables(local_index[:, None], cycle_index[None, :], cycle * tokens), axis=1
    )

    hidden, starts = [], []
    for g in range(chunks):
        done = exchange(convolve(g, twist, ahead, back, signals[g], filters))
        own = gate(done, keyval, gating, skip_gain, g)
        for shift in range(peers):
            if shift == 0:
                piece = own
            else:
                piece = lax.ppermute(
                    own, "tensor", [(t, (t + shift) % peers) for t in range(peers)]
                )
            hidden.append(piece)
            source = lax.rem(side + peers - shift, peers)
            starts.append(source * chunks + g)
    result = None
    if paired:
        which = [(place // half + side + shift) % 2 for g in range(chunks) for shift in range(2)]
        rows = [jnp.full((), g, jnp.int32) for g in range(chunks) for shift in range(2)]
        places = jnp.stack(rows + rows + which).astype(jnp.int32)
        result = mix_pair(hidden, places, pair, columns)
    starts = jnp.stack(starts).astype(jnp.int32)
    return mix(hidden, starts, weight, cut, columns, result)


def solution(mesh):
    placed = (
        P("seq", "tensor"),
        P("seq", "tensor"),
        P("tensor"),
        P(None, None, None, "seq", "tensor"),
        P("tensor", None),
        P("seq", "tensor"),
    )
    return jax.shard_map(
        body, mesh=mesh, in_specs=placed, out_specs=P("seq", "tensor"), check_vma=False
    )
```

```python
import functools
import math

import jax
import jax.numpy as jnp
from jax import lax
from jax.experimental import pallas as pl
from jax.experimental.pallas import tpu as pltpu
from jax.sharding import PartitionSpec as P

BLOCK = 64
ROWS = 16
VMEM = 48 * 2**20
F32 = jnp.float32
BF16 = jnp.bfloat16


def tables(first_index, second_index, length):
    phase = first_index * second_index % length
    angle = 2.0 * math.pi / length * phase.astype(F32)
    return (jnp.cos(angle), jnp.sin(angle))


def real_forward(values):
    n = len(values)
    if n == 2:
        return [(values[0] + values[1], None), (values[0] - values[1], None)]
    even, odd = real_forward(values[0::2]), real_forward(values[1::2])
    half = n // 2
    out = [None] * (half + 1)
    for p in range(half // 2 + 1):
        (er, ei), (dr, di) = even[p], odd[p]
        if p == 0:
            out[0], out[half] = (er + dr, None), (er - dr, None)
        elif 2 * p == half:
            out[p] = (er, -dr)
        else:
            c, s = math.cos(2 * math.pi * p / n), math.sin(2 * math.pi * p / n)
            tr, ti = dr * c + di * s, di * c - dr * s
            out[p], out[half - p] = (er + tr, ei + ti), (er - tr, ti - ei)
    return out


def real_inverse(freqs):
    half = len(freqs) - 1
    if half == 1:
        return [freqs[0][0] + freqs[1][0], freqs[0][0] - freqs[1][0]]
    n = 2 * half
    even, odd = [None] * (half // 2 + 1), [None] * (half // 2 + 1)
    for p in range(half // 2 + 1):
        (ar, ai), (br, bi) = freqs[p], freqs[half - p]
        if p == 0:
            even[0], odd[0] = (ar + br, None), (ar - br, None)
        elif 2 * p == half:
            even[p], odd[p] = (ar + ar, None), (-(ai + ai), None)
        else:
            c, s = math.cos(2 * math.pi * p / n), math.sin(2 * math.pi * p / n)
            dr, di = ar - br, ai + bi
            even[p], odd[p] = (ar + br, ai - bi), (dr * c - di * s, dr * s + di * c)
    out = [None] * n
    out[0::2], out[1::2] = real_inverse(even), real_inverse(odd)
    return out


def conv_kernel(twist_ref, ahead_ref, back_ref, x_ref, filter_ref, out_ref, first_ref, turned_ref):
    cycle, tokens, unit = x_ref.shape
    kept = filter_ref.shape[2] // 2
    per = max(1, 256 // unit)
    width = per * unit

    def twist(rows):
        block = twist_ref[rows, :]
        return [
            (block[:, p : p + 1], block[:, cycle + p : cycle + p + 1]) for p in range(cycle)
        ]

    def ahead(step, carry):
        start = pl.multiple_of(step * ROWS, ROWS)
        rows = pl.ds(start, ROWS)
        freqs = real_forward([x_ref[a, rows, :].astype(F32) for a in range(cycle)])
        for p, (c, s) in enumerate(twist(rows)):
            real, imaginary = freqs[min(p, cycle - p)]
            if imaginary is None:
                fr, fi = real * c, -(real * s)
            elif 2 * p > cycle:
                fr, fi = real * c - imaginary * s, -(imaginary * c + real * s)
            else:
                fr, fi = real * c + imaginary * s, imaginary * c - real * s
            lanes = slice(p * unit, (p + 1) * unit)
            first_ref[rows, lanes] = fr.astype(BF16)
            first_ref[pl.ds(tokens + start, ROWS), lanes] = fi.astype(BF16)
        return carry

    lax.fori_loop(0, tokens // ROWS, ahead, 0)

    def middle(step, carry):
        lanes = pl.ds(pl.multiple_of(step * width, width), width)
        spectrum = jnp.dot(ahead_ref[0], first_ref[:, lanes], preferred_element_type=F32)
        reals, imaginaries = [], []
        for u in range(per):
            part = filter_ref[step * per + u, 0].astype(F32)
            hr, hi = part[:kept], part[kept:]
            own = slice(u * unit, (u + 1) * unit)
            sr, si = spectrum[:kept, own], spectrum[kept:, own]
            reals.append(hr * sr - hi * si)
            imaginaries.append(hr * si + hi * sr)
        product = jnp.concatenate(
            [jnp.concatenate(reals, axis=1), jnp.concatenate(imaginaries, axis=1)], axis=0
        ).astype(BF16)
        turned_ref[:, lanes] = jnp.dot(back_ref[0], product, preferred_element_type=F32)
        return carry

    lax.fori_loop(0, cycle // per, middle, 0)

    def behind(step, carry):
        start = pl.multiple_of(step * ROWS, ROWS)
        rows = pl.ds(start, ROWS)
        parts = []
        for p, (c, s) in enumerate(twist(rows)):
            lanes = slice(p * unit, (p + 1) * unit)
            br = turned_ref[rows, lanes]
            bi = turned_ref[pl.ds(tokens + start, ROWS), lanes]
            parts.append(
                (
                    (br * c - bi * s).astype(BF16).astype(F32),
                    (br * s + bi * c).astype(BF16).astype(F32),
                )
            )
        half = cycle // 2
        freqs = [(parts[0][0] * 2.0, None)]
        for p in range(1, half):
            (ur, ui), (vr, vi) = parts[p], parts[cycle - p]
            freqs.append((ur + vr, ui - vi))
        freqs.append((parts[half][0] * 2.0, None))
        scale = 0.5 / (cycle * tokens)
        for a, value in enumerate(real_inverse(freqs)):
            out_ref[a, rows, :] = (value * scale).astype(BF16)
        return carry

    lax.fori_loop(0, tokens // ROWS, behind, 0)


def convolve(chunk, twist, ahead, back, signal, filters):
    cycle, tokens, unit = signal.shape
    kept = filters.shape[2] // 2
    flops = 4 * 2 * kept * 2 * tokens * cycle * unit
    return pl.pallas_call(
        conv_kernel,
        grid=(1,),
        out_shape=jax.ShapeDtypeStruct(signal.shape, BF16),
        in_specs=[
            pl.BlockSpec(twist.shape, lambda i: (0, 0)),
            pl.BlockSpec((1, *ahead.shape[1:]), lambda i: (chunk, 0, 0)),
            pl.BlockSpec((1, *back.shape[1:]), lambda i: (chunk, 0, 0)),
            pl.BlockSpec(signal.shape, lambda i: (0, 0, 0)),
            pl.BlockSpec((cycle, 1, 2 * kept, unit), lambda i: (0, chunk, 0, 0)),
        ],
        out_specs=pl.BlockSpec(signal.shape, lambda i: (0, 0, 0)),
        scratch_shapes=[
            pltpu.VMEM((2 * tokens, cycle * unit), BF16),
            pltpu.VMEM((2 * tokens, cycle * unit), F32),
        ],
        compiler_params=pltpu.CompilerParams(vmem_limit_bytes=VMEM),
        cost_estimate=pl.CostEstimate(
            flops=flops, bytes_accessed=16 * signal.size, transcendentals=0
        ),
        name="convolve",
    )(twist, ahead, back, signal, filters)


def pack_kernel(unit, x_ref, out_ref):
    for d in range(out_ref.shape[0]):
        out_ref[d] = x_ref[:, d * unit : (d + 1) * unit]


def pack_signal(keyval, chunk, cycle, unit):
    tokens = keyval.shape[0]
    wide = max(1, min(cycle, 512 // unit))
    steps = cycle // wide
    return pl.pallas_call(
        functools.partial(pack_kernel, unit),
        grid=(steps,),
        out_shape=jax.ShapeDtypeStruct((cycle, tokens, unit), BF16),
        in_specs=[pl.BlockSpec((tokens, wide * unit), lambda i: (0, chunk * steps + i))],
        out_specs=pl.BlockSpec((wide, tokens, unit), lambda i: (i, 0, 0)),
        compiler_params=pltpu.CompilerParams(vmem_limit_bytes=VMEM),
        cost_estimate=pl.CostEstimate(
            flops=0, bytes_accessed=4 * tokens * cycle * unit, transcendentals=0
        ),
        name="pack_signal",
    )(keyval)


def pack_filter_kernel(unit, f_ref, out_ref):
    for d in range(out_ref.shape[0]):
        out_ref[d, 0] = f_ref[:, 0, d * unit : (d + 1) * unit].astype(BF16)


def pack_filters(filter_values, cycle, chunks, unit):
    channels = filter_values.shape[-1]
    rows = filter_values.size // channels
    flat = filter_values.reshape(rows, 1, channels)
    wide = max(1, min(cycle, 512 // unit))
    steps = cycle // wide
    return pl.pallas_call(
        functools.partial(pack_filter_kernel, unit),
        grid=(chunks, steps),
        out_shape=jax.ShapeDtypeStruct((cycle, chunks, rows, unit), BF16),
        in_specs=[pl.BlockSpec((rows, 1, wide * unit), lambda g, i: (0, 0, g * steps + i))],
        out_specs=pl.BlockSpec((wide, 1, rows, unit), lambda g, i: (i, g, 0, 0)),
        compiler_params=pltpu.CompilerParams(vmem_limit_bytes=VMEM),
        cost_estimate=pl.CostEstimate(
            flops=0, bytes_accessed=6 * filter_values.size, transcendentals=0
        ),
        name="pack_filters",
    )(flat)


def gate_kernel(unit, c_ref, x_ref, g_ref, s_ref, out_ref):
    for d in range(c_ref.shape[0]):
        lanes = slice(d * unit, (d + 1) * unit)
        direct = s_ref[0:1, lanes] * x_ref[:, lanes].astype(F32)
        value = g_ref[:, lanes].astype(F32) * (c_ref[d].astype(F32) + direct)
        out_ref[:, lanes] = value.astype(BF16)


def gate(convolved, keyval, gating, skip_gain, chunk):
    cycle, tokens, unit = convolved.shape
    wide = max(1, min(cycle, 512 // unit))
    steps = cycle // wide
    lanes = wide * unit
    return pl.pallas_call(
        functools.partial(gate_kernel, unit),
        grid=(steps,),
        out_shape=jax.ShapeDtypeStruct((tokens, cycle * unit), BF16),
        in_specs=[
            pl.BlockSpec((wide, tokens, unit), lambda i: (i, 0, 0)),
            pl.BlockSpec((tokens, lanes), lambda i: (0, chunk * steps + i)),
            pl.BlockSpec((tokens, lanes), lambda i: (0, chunk * steps + i)),
            pl.BlockSpec((1, lanes), lambda i: (0, chunk * steps + i)),
        ],
        out_specs=pl.BlockSpec((tokens, lanes), lambda i: (0, i)),
        compiler_params=pltpu.CompilerParams(vmem_limit_bytes=VMEM),
        cost_estimate=pl.CostEstimate(
            flops=0, bytes_accessed=8 * convolved.size, transcendentals=0
        ),
        name="gate",
    )(convolved, keyval, gating, skip_gain.reshape(1, -1))


def mix_kernel(pieces, start_ref, *refs):
    w_ref, out_ref, total_ref = refs[pieces], refs[-2], refs[-1]
    step = pl.program_id(1)
    columns = w_ref.shape[1]
    tile = min(256, columns)
    for k in range(pieces):

        @pl.when(step == k)
        def _(k=k):
            for low in range(0, columns, tile):
                lanes = slice(low, low + tile)
                part = jnp.dot(refs[k][...], w_ref[:, lanes], preferred_element_type=F32)
                if k:
                    part = total_ref[:, lanes] + part
                if k < pieces - 1:
                    total_ref[:, lanes] = part
                else:
                    out_ref[:, lanes] = part.astype(BF16)


def mix(hidden, starts, weight, low, columns, result):
    tokens, width = hidden[0].shape
    depth, part = weight.shape
    tile = min(1024, part)
    first = low // tile
    pieces = len(hidden)
    before = [] if result is None else [result]
    return pl.pallas_call(
        functools.partial(mix_kernel, pieces),
        grid_spec=pltpu.PrefetchScalarGridSpec(
            num_scalar_prefetch=1,
            grid=(part // tile, pieces),
            in_specs=[pl.BlockSpec(h.shape, lambda i, k, s: (0, 0)) for h in hidden]
            + [pl.BlockSpec((width, tile), lambda i, k, s: (s[k], i))]
            + [pl.BlockSpec(memory_space=pl.ANY) for _ in before],
            out_specs=pl.BlockSpec((tokens, tile), lambda i, k, s: (0, first + i)),
            scratch_shapes=[pltpu.VMEM((tokens, tile), F32)],
        ),
        out_shape=jax.ShapeDtypeStruct((tokens, columns), BF16),
        input_output_aliases={pieces + 2: 0} if before else {},
        compiler_params=pltpu.CompilerParams(vmem_limit_bytes=VMEM),
        cost_estimate=pl.CostEstimate(
            flops=2 * tokens * depth * part, bytes_accessed=2 * depth * part, transcendentals=0
        ),
        name="mix",
    )(starts, *hidden, weight, *before)


def pair_kernel(pieces, place_ref, *refs):
    a_ref, b_ref, out_ref, total_ref = refs[pieces : pieces + 4]
    step = pl.program_id(1)
    columns = a_ref.shape[1]
    tile = min(256, columns)
    for k in range(pieces):
        for place, w_ref in enumerate((a_ref, b_ref)):

            @pl.when(jnp.logical_and(step == k, place_ref[2 * pieces + k] == place))
            def _(k=k, w_ref=w_ref):
                for low in range(0, columns, tile):
                    lanes = slice(low, low + tile)
                    part = jnp.dot(refs[k][...], w_ref[:, lanes], preferred_element_type=F32)
                    if k:
                        part = total_ref[:, lanes] + part
                    if k < pieces - 1:
                        total_ref[:, lanes] = part
                    else:
                        out_ref[:, lanes] = part.astype(BF16)


def mix_pair(hidden, places, weights, columns):
    tokens, width = hidden[0].shape
    depth, part = weights[0].shape
    tile = min(1024, part)
    pieces = len(hidden)
    return pl.pallas_call(
        functools.partial(pair_kernel, pieces),
        grid_spec=pltpu.PrefetchScalarGridSpec(
            num_scalar_prefetch=1,
            grid=(part // tile, pieces),
            in_specs=[pl.BlockSpec(h.shape, lambda i, k, s: (0, 0)) for h in hidden]
            + [
                pl.BlockSpec((width, tile), lambda i, k, s: (s[k], i)),
                pl.BlockSpec((width, tile), lambda i, k, s: (s[pieces + k], i)),
            ],
            out_specs=pl.BlockSpec((tokens, tile), lambda i, k, s: (0, i)),
            scratch_shapes=[pltpu.VMEM((tokens, tile), F32)],
        ),
        out_shape=jax.ShapeDtypeStruct((tokens, columns), BF16),
        compiler_params=pltpu.CompilerParams(vmem_limit_bytes=VMEM),
        cost_estimate=pl.CostEstimate(
            flops=4 * tokens * depth * part, bytes_accessed=4 * depth * part, transcendentals=0
        ),
        name="mix_pair",
    )(places, *hidden, *weights)


def body(keyval, gating, skip_gain, filter_values, blocks, out_weight):
    cycle = lax.axis_size("seq")
    place = lax.axis_index("seq")
    peers = lax.axis_size("tensor")
    side = lax.axis_index("tensor")
    tokens, channels = keyval.shape
    repeat = BLOCK // cycle
    groups_local = blocks.shape[0]
    group_width = channels // groups_local
    narrow = channels // cycle
    unit = min(narrow, group_width)
    chunks = narrow // unit

    packed_filters = pack_filters(filter_values, cycle, chunks, unit)
    columns = out_weight.shape[1]
    half = cycle // 2
    width = cycle * unit
    paired = columns % 2048 == 0 and peers == 2 and half * out_weight.shape[0] == channels
    cut = columns // 2 if paired else 0
    if paired:
        sides = [list(range(half)), list(range(half, cycle))]
        gather = functools.partial(
            lax.all_gather, axis_name="seq", axis=0, tiled=True, axis_index_groups=sides
        )
        own = out_weight[:, :cut]
        sent, packed_filters = lax.optimization_barrier((own, packed_filters))
        other = lax.ppermute(sent, "seq", [(i, (i + half) % cycle) for i in range(cycle)])
    exchange = functools.partial(
        lax.all_to_all, axis_name="seq", split_axis=0, concat_axis=0, tiled=True
    )
    filters = exchange(packed_filters)
    if paired:
        other, filters = lax.optimization_barrier((other, filters))
        pair = [gather(own), gather(other)]
    weight = lax.all_gather(out_weight[:, cut:], "seq", axis=0, tiled=True)
    signals = [exchange(pack_signal(keyval, g, cycle, unit)) for g in range(chunks)]

    group = (jnp.arange(chunks, dtype=jnp.int32) * cycle + place) * unit // group_width
    kept_blocks = jnp.take(blocks, group, axis=0)
    kept_rows = (
        kept_blocks[:, :, None] * repeat + jnp.arange(repeat, dtype=jnp.int32)
    ).reshape(chunks, -1)
    local_index = jnp.arange(tokens, dtype=jnp.int32)
    cosine, sine = tables(kept_rows[:, :, None], local_index[None, None, :], tokens)
    ahead = jnp.concatenate(
        [jnp.concatenate([cosine, sine], axis=2), jnp.concatenate([-sine, cosine], axis=2)],
        axis=1,
    ).astype(BF16)
    cosine, sine = tables(kept_rows[:, None, :], local_index[None, :, None], tokens)
    back = jnp.concatenate(
        [jnp.concatenate([cosine, -sine], axis=2), jnp.concatenate([sine, cosine], axis=2)],
        axis=1,
    ).astype(BF16)
    cycle_index = jnp.arange(cycle, dtype=jnp.int32)
    twist = jnp.concatenate(
        tables(local_index[:, None], cycle_index[None, :], cycle * tokens), axis=1
    )

    hidden, starts = [], []
    for g in range(chunks):
        done = exchange(convolve(g, twist, ahead, back, signals[g], filters))
        own = gate(done, keyval, gating, skip_gain, g)
        for shift in range(peers):
            if shift == 0:
                piece = own
            else:
                piece = lax.ppermute(
                    own, "tensor", [(t, (t + shift) % peers) for t in range(peers)]
                )
            hidden.append(piece)
            source = lax.rem(side + peers - shift, peers)
            starts.append(source * chunks + g)
    result = None
    if paired:
        which = [(place // half + side + shift) % 2 for g in range(chunks) for shift in range(2)]
        rows = [jnp.full((), g, jnp.int32) for g in range(chunks) for shift in range(2)]
        places = jnp.stack(rows + rows + which).astype(jnp.int32)
        result = mix_pair(hidden, places, pair, columns)
    starts = jnp.stack(starts).astype(jnp.int32)
    return mix(hidden, starts, weight, cut, columns, result)


def solution(mesh):
    placed = (
        P("seq", "tensor"),
        P("seq", "tensor"),
        P("tensor"),
        P(None, None, None, "seq", "tensor"),
        P("tensor", None),
        P("seq", "tensor"),
    )
    return jax.shard_map(
        body, mesh=mesh, in_specs=placed, out_specs=P("seq", "tensor"), check_vma=False
    )
```

```python
import functools
import math

import jax
import jax.numpy as jnp
from jax import lax
from jax.experimental import pallas as pl
from jax.experimental.pallas import tpu as pltpu
from jax.sharding import PartitionSpec as P

BLOCK = 64
ROWS = 16
VMEM = 48 * 2**20
F32 = jnp.float32
BF16 = jnp.bfloat16


def tables(first_index, second_index, length):
    phase = first_index * second_index % length
    angle = 2.0 * math.pi / length * phase.astype(F32)
    return (jnp.cos(angle), jnp.sin(angle))


def real_forward(values):
    n = len(values)
    if n == 2:
        return [(values[0] + values[1], None), (values[0] - values[1], None)]
    even, odd = real_forward(values[0::2]), real_forward(values[1::2])
    half = n // 2
    out = [None] * (half + 1)
    for p in range(half // 2 + 1):
        (er, ei), (dr, di) = even[p], odd[p]
        if p == 0:
            out[0], out[half] = (er + dr, None), (er - dr, None)
        elif 2 * p == half:
            out[p] = (er, -dr)
        else:
            c, s = math.cos(2 * math.pi * p / n), math.sin(2 * math.pi * p / n)
            tr, ti = dr * c + di * s, di * c - dr * s
            out[p], out[half - p] = (er + tr, ei + ti), (er - tr, ti - ei)
    return out


def real_inverse(freqs):
    half = len(freqs) - 1
    if half == 1:
        return [freqs[0][0] + freqs[1][0], freqs[0][0] - freqs[1][0]]
    n = 2 * half
    even, odd = [None] * (half // 2 + 1), [None] * (half // 2 + 1)
    for p in range(half // 2 + 1):
        (ar, ai), (br, bi) = freqs[p], freqs[half - p]
        if p == 0:
            even[0], odd[0] = (ar + br, None), (ar - br, None)
        elif 2 * p == half:
            even[p], odd[p] = (ar + ar, None), (-(ai + ai), None)
        else:
            c, s = math.cos(2 * math.pi * p / n), math.sin(2 * math.pi * p / n)
            dr, di = ar - br, ai + bi
            even[p], odd[p] = (ar + br, ai - bi), (dr * c - di * s, dr * s + di * c)
    out = [None] * n
    out[0::2], out[1::2] = real_inverse(even), real_inverse(odd)
    return out


def conv_kernel(twist_ref, ahead_ref, back_ref, x_ref, filter_ref, out_ref, first_ref, turned_ref):
    cycle, tokens, unit = x_ref.shape
    kept = filter_ref.shape[2] // 2
    per = max(1, 256 // unit)
    width = per * unit

    def twist(rows):
        block = twist_ref[rows, :]
        return [
            (block[:, p : p + 1], block[:, cycle + p : cycle + p + 1]) for p in range(cycle)
        ]

    def ahead(step, carry):
        start = pl.multiple_of(step * ROWS, ROWS)
        rows = pl.ds(start, ROWS)
        freqs = real_forward([x_ref[a, rows, :].astype(F32) for a in range(cycle)])
        for p, (c, s) in enumerate(twist(rows)):
            real, imaginary = freqs[min(p, cycle - p)]
            if imaginary is None:
                fr, fi = real * c, -(real * s)
            elif 2 * p > cycle:
                fr, fi = real * c - imaginary * s, -(imaginary * c + real * s)
            else:
                fr, fi = real * c + imaginary * s, imaginary * c - real * s
            lanes = slice(p * unit, (p + 1) * unit)
            first_ref[rows, lanes] = fr.astype(BF16)
            first_ref[pl.ds(tokens + start, ROWS), lanes] = fi.astype(BF16)
        return carry

    lax.fori_loop(0, tokens // ROWS, ahead, 0)

    def middle(step, carry):
        lanes = pl.ds(pl.multiple_of(step * width, width), width)
        spectrum = jnp.dot(ahead_ref[0], first_ref[:, lanes], preferred_element_type=F32)
        reals, imaginaries = [], []
        for u in range(per):
            part = filter_ref[step * per + u, 0].astype(F32)
            hr, hi = part[:kept], part[kept:]
            own = slice(u * unit, (u + 1) * unit)
            sr, si = spectrum[:kept, own], spectrum[kept:, own]
            reals.append(hr * sr - hi * si)
            imaginaries.append(hr * si + hi * sr)
        product = jnp.concatenate(
            [jnp.concatenate(reals, axis=1), jnp.concatenate(imaginaries, axis=1)], axis=0
        ).astype(BF16)
        turned_ref[:, lanes] = jnp.dot(back_ref[0], product, preferred_element_type=F32)
        return carry

    lax.fori_loop(0, cycle // per, middle, 0)

    def behind(step, carry):
        start = pl.multiple_of(step * ROWS, ROWS)
        rows = pl.ds(start, ROWS)
        parts = []
        for p, (c, s) in enumerate(twist(rows)):
            lanes = slice(p * unit, (p + 1) * unit)
            br = turned_ref[rows, lanes]
            bi = turned_ref[pl.ds(tokens + start, ROWS), lanes]
            parts.append(
                (
                    (br * c - bi * s).astype(BF16).astype(F32),
                    (br * s + bi * c).astype(BF16).astype(F32),
                )
            )
        half = cycle // 2
        freqs = [(parts[0][0] * 2.0, None)]
        for p in range(1, half):
            (ur, ui), (vr, vi) = parts[p], parts[cycle - p]
            freqs.append((ur + vr, ui - vi))
        freqs.append((parts[half][0] * 2.0, None))
        scale = 0.5 / (cycle * tokens)
        for a, value in enumerate(real_inverse(freqs)):
            out_ref[a, rows, :] = (value * scale).astype(BF16)
        return carry

    lax.fori_loop(0, tokens // ROWS, behind, 0)


def convolve(chunk, twist, ahead, back, signal, filters):
    cycle, tokens, unit = signal.shape
    kept = filters.shape[2] // 2
    flops = 4 * 2 * kept * 2 * tokens * cycle * unit
    return pl.pallas_call(
        conv_kernel,
        grid=(1,),
        out_shape=jax.ShapeDtypeStruct(signal.shape, BF16),
        in_specs=[
            pl.BlockSpec(twist.shape, lambda i: (0, 0)),
            pl.BlockSpec((1, *ahead.shape[1:]), lambda i: (chunk, 0, 0)),
            pl.BlockSpec((1, *back.shape[1:]), lambda i: (chunk, 0, 0)),
            pl.BlockSpec(signal.shape, lambda i: (0, 0, 0)),
            pl.BlockSpec((cycle, 1, 2 * kept, unit), lambda i: (0, chunk, 0, 0)),
        ],
        out_specs=pl.BlockSpec(signal.shape, lambda i: (0, 0, 0)),
        scratch_shapes=[
            pltpu.VMEM((2 * tokens, cycle * unit), BF16),
            pltpu.VMEM((2 * tokens, cycle * unit), F32),
        ],
        compiler_params=pltpu.CompilerParams(vmem_limit_bytes=VMEM),
        cost_estimate=pl.CostEstimate(
            flops=flops, bytes_accessed=16 * signal.size, transcendentals=0
        ),
        name="convolve",
    )(twist, ahead, back, signal, filters)


def pack_kernel(unit, x_ref, out_ref):
    for d in range(out_ref.shape[0]):
        out_ref[d] = x_ref[:, d * unit : (d + 1) * unit]


def pack_signal(keyval, chunk, cycle, unit):
    tokens = keyval.shape[0]
    wide = max(1, min(cycle, 512 // unit))
    steps = cycle // wide
    return pl.pallas_call(
        functools.partial(pack_kernel, unit),
        grid=(steps,),
        out_shape=jax.ShapeDtypeStruct((cycle, tokens, unit), BF16),
        in_specs=[pl.BlockSpec((tokens, wide * unit), lambda i: (0, chunk * steps + i))],
        out_specs=pl.BlockSpec((wide, tokens, unit), lambda i: (i, 0, 0)),
        compiler_params=pltpu.CompilerParams(vmem_limit_bytes=VMEM),
        cost_estimate=pl.CostEstimate(
            flops=0, bytes_accessed=4 * tokens * cycle * unit, transcendentals=0
        ),
        name="pack_signal",
    )(keyval)


def pack_filter_kernel(unit, f_ref, out_ref):
    for d in range(out_ref.shape[0]):
        out_ref[d, 0] = f_ref[:, 0, d * unit : (d + 1) * unit].astype(BF16)


def pack_filters(filter_values, cycle, chunks, unit):
    channels = filter_values.shape[-1]
    rows = filter_values.size // channels
    flat = filter_values.reshape(rows, 1, channels)
    wide = max(1, min(cycle, 512 // unit))
    steps = cycle // wide
    return pl.pallas_call(
        functools.partial(pack_filter_kernel, unit),
        grid=(chunks, steps),
        out_shape=jax.ShapeDtypeStruct((cycle, chunks, rows, unit), BF16),
        in_specs=[pl.BlockSpec((rows, 1, wide * unit), lambda g, i: (0, 0, g * steps + i))],
        out_specs=pl.BlockSpec((wide, 1, rows, unit), lambda g, i: (i, g, 0, 0)),
        compiler_params=pltpu.CompilerParams(vmem_limit_bytes=VMEM),
        cost_estimate=pl.CostEstimate(
            flops=0, bytes_accessed=6 * filter_values.size, transcendentals=0
        ),
        name="pack_filters",
    )(flat)


def gate_kernel(unit, c_ref, x_ref, g_ref, s_ref, out_ref):
    for d in range(c_ref.shape[0]):
        lanes = slice(d * unit, (d + 1) * unit)
        direct = s_ref[0:1, lanes] * x_ref[:, lanes].astype(F32)
        value = g_ref[:, lanes].astype(F32) * (c_ref[d].astype(F32) + direct)
        out_ref[:, lanes] = value.astype(BF16)


def gate(convolved, keyval, gating, skip_gain, chunk):
    cycle, tokens, unit = convolved.shape
    wide = max(1, min(cycle, 512 // unit))
    steps = cycle // wide
    lanes = wide * unit
    return pl.pallas_call(
        functools.partial(gate_kernel, unit),
        grid=(steps,),
        out_shape=jax.ShapeDtypeStruct((tokens, cycle * unit), BF16),
        in_specs=[
            pl.BlockSpec((wide, tokens, unit), lambda i: (i, 0, 0)),
            pl.BlockSpec((tokens, lanes), lambda i: (0, chunk * steps + i)),
            pl.BlockSpec((tokens, lanes), lambda i: (0, chunk * steps + i)),
            pl.BlockSpec((1, lanes), lambda i: (0, chunk * steps + i)),
        ],
        out_specs=pl.BlockSpec((tokens, lanes), lambda i: (0, i)),
        compiler_params=pltpu.CompilerParams(vmem_limit_bytes=VMEM),
        cost_estimate=pl.CostEstimate(
            flops=0, bytes_accessed=8 * convolved.size, transcendentals=0
        ),
        name="gate",
    )(convolved, keyval, gating, skip_gain.reshape(1, -1))


def mix_kernel(pieces, start_ref, *refs):
    w_ref, out_ref, total_ref = refs[pieces], refs[-2], refs[-1]
    step = pl.program_id(1)
    columns = w_ref.shape[1]
    tile = min(256, columns)
    for k in range(pieces):

        @pl.when(step == k)
        def _(k=k):
            for low in range(0, columns, tile):
                lanes = slice(low, low + tile)
                part = jnp.dot(refs[k][...], w_ref[:, lanes], preferred_element_type=F32)
                if k:
                    part = total_ref[:, lanes] + part
                if k < pieces - 1:
                    total_ref[:, lanes] = part
                else:
                    out_ref[:, lanes] = part.astype(BF16)


def mix(hidden, starts, weight, low, columns, result):
    tokens, width = hidden[0].shape
    depth, part = weight.shape
    tile = min(512, part)
    first = low // tile
    pieces = len(hidden)
    before = [] if result is None else [result]
    return pl.pallas_call(
        functools.partial(mix_kernel, pieces),
        grid_spec=pltpu.PrefetchScalarGridSpec(
            num_scalar_prefetch=1,
            grid=(part // tile, pieces),
            in_specs=[pl.BlockSpec(h.shape, lambda i, k, s: (0, 0)) for h in hidden]
            + [pl.BlockSpec((width, tile), lambda i, k, s: (s[k], i))]
            + [pl.BlockSpec(memory_space=pl.ANY) for _ in before],
            out_specs=pl.BlockSpec((tokens, tile), lambda i, k, s: (0, first + i)),
            scratch_shapes=[pltpu.VMEM((tokens, tile), F32)],
        ),
        out_shape=jax.ShapeDtypeStruct((tokens, columns), BF16),
        input_output_aliases={pieces + 2: 0} if before else {},
        compiler_params=pltpu.CompilerParams(vmem_limit_bytes=VMEM),
        cost_estimate=pl.CostEstimate(
            flops=2 * tokens * depth * part, bytes_accessed=2 * depth * part, transcendentals=0
        ),
        name="mix",
    )(starts, *hidden, weight, *before)


def pair_kernel(pieces, place_ref, *refs):
    a_ref, b_ref, out_ref, total_ref = refs[pieces : pieces + 4]
    step = pl.program_id(1)
    columns = a_ref.shape[1]
    tile = min(256, columns)
    for k in range(pieces):
        for place, w_ref in enumerate((a_ref, b_ref)):

            @pl.when(jnp.logical_and(step == k, place_ref[2 * pieces + k] == place))
            def _(k=k, w_ref=w_ref):
                for low in range(0, columns, tile):
                    lanes = slice(low, low + tile)
                    part = jnp.dot(refs[k][...], w_ref[:, lanes], preferred_element_type=F32)
                    if k:
                        part = total_ref[:, lanes] + part
                    if k < pieces - 1:
                        total_ref[:, lanes] = part
                    else:
                        out_ref[:, lanes] = part.astype(BF16)


def mix_pair(hidden, places, weights, columns):
    tokens, width = hidden[0].shape
    depth, part = weights[0].shape
    tile = min(1024, part)
    pieces = len(hidden)
    return pl.pallas_call(
        functools.partial(pair_kernel, pieces),
        grid_spec=pltpu.PrefetchScalarGridSpec(
            num_scalar_prefetch=1,
            grid=(part // tile, pieces),
            in_specs=[pl.BlockSpec(h.shape, lambda i, k, s: (0, 0)) for h in hidden]
            + [
                pl.BlockSpec((width, tile), lambda i, k, s: (s[k], i)),
                pl.BlockSpec((width, tile), lambda i, k, s: (s[pieces + k], i)),
            ],
            out_specs=pl.BlockSpec((tokens, tile), lambda i, k, s: (0, i)),
            scratch_shapes=[pltpu.VMEM((tokens, tile), F32)],
        ),
        out_shape=jax.ShapeDtypeStruct((tokens, columns), BF16),
        compiler_params=pltpu.CompilerParams(vmem_limit_bytes=VMEM),
        cost_estimate=pl.CostEstimate(
            flops=4 * tokens * depth * part, bytes_accessed=4 * depth * part, transcendentals=0
        ),
        name="mix_pair",
    )(places, *hidden, *weights)


def body(keyval, gating, skip_gain, filter_values, blocks, out_weight):
    cycle = lax.axis_size("seq")
    place = lax.axis_index("seq")
    peers = lax.axis_size("tensor")
    side = lax.axis_index("tensor")
    tokens, channels = keyval.shape
    repeat = BLOCK // cycle
    groups_local = blocks.shape[0]
    group_width = channels // groups_local
    narrow = channels // cycle
    unit = min(narrow, group_width)
    chunks = narrow // unit

    packed_filters = pack_filters(filter_values, cycle, chunks, unit)
    columns = out_weight.shape[1]
    half = cycle // 2
    width = cycle * unit
    paired = columns % 2048 == 0 and peers == 2 and half * out_weight.shape[0] == channels
    cut = columns // 4 if paired else 0
    bounds = [cut, cut + (columns - cut) // 2, columns] if paired else [0, columns]
    if paired:
        sides = [list(range(half)), list(range(half, cycle))]
        gather = functools.partial(
            lax.all_gather, axis_name="seq", axis=0, tiled=True, axis_index_groups=sides
        )
        own = out_weight[:, :cut]
        sent, packed_filters = lax.optimization_barrier((own, packed_filters))
        other = lax.ppermute(sent, "seq", [(i, (i + half) % cycle) for i in range(cycle)])
    exchange = functools.partial(
        lax.all_to_all, axis_name="seq", split_axis=0, concat_axis=0, tiled=True
    )
    filters = exchange(packed_filters)
    if paired:
        other, filters = lax.optimization_barrier((other, filters))
        pair = [gather(own), gather(other)]
    weights = [
        lax.all_gather(out_weight[:, low:high], "seq", axis=0, tiled=True)
        for low, high in zip(bounds[:-1], bounds[1:])
    ]
    signals = [exchange(pack_signal(keyval, g, cycle, unit)) for g in range(chunks)]

    group = (jnp.arange(chunks, dtype=jnp.int32) * cycle + place) * unit // group_width
    kept_blocks = jnp.take(blocks, group, axis=0)
    kept_rows = (
        kept_blocks[:, :, None] * repeat + jnp.arange(repeat, dtype=jnp.int32)
    ).reshape(chunks, -1)
    local_index = jnp.arange(tokens, dtype=jnp.int32)
    cosine, sine = tables(kept_rows[:, :, None], local_index[None, None, :], tokens)
    ahead = jnp.concatenate(
        [jnp.concatenate([cosine, sine], axis=2), jnp.concatenate([-sine, cosine], axis=2)],
        axis=1,
    ).astype(BF16)
    cosine, sine = tables(kept_rows[:, None, :], local_index[None, :, None], tokens)
    back = jnp.concatenate(
        [jnp.concatenate([cosine, -sine], axis=2), jnp.concatenate([sine, cosine], axis=2)],
        axis=1,
    ).astype(BF16)
    cycle_index = jnp.arange(cycle, dtype=jnp.int32)
    twist = jnp.concatenate(
        tables(local_index[:, None], cycle_index[None, :], cycle * tokens), axis=1
    )

    hidden, starts = [], []
    for g in range(chunks):
        done = exchange(convolve(g, twist, ahead, back, signals[g], filters))
        own = gate(done, keyval, gating, skip_gain, g)
        for shift in range(peers):
            if shift == 0:
                piece = own
            else:
                piece = lax.ppermute(
                    own, "tensor", [(t, (t + shift) % peers) for t in range(peers)]
                )
            hidden.append(piece)
            source = lax.rem(side + peers - shift, peers)
            starts.append(source * chunks + g)
    result = None
    if paired:
        which = [(place // half + side + shift) % 2 for g in range(chunks) for shift in range(2)]
        rows = [jnp.full((), g, jnp.int32) for g in range(chunks) for shift in range(2)]
        places = jnp.stack(rows + rows + which).astype(jnp.int32)
        result = mix_pair(hidden, places, pair, columns)
    starts = jnp.stack(starts).astype(jnp.int32)
    for low, weight in zip(bounds[:-1], weights):
        result = mix(hidden, starts, weight, low, columns, result)
    return result


def solution(mesh):
    placed = (
        P("seq", "tensor"),
        P("seq", "tensor"),
        P("tensor"),
        P(None, None, None, "seq", "tensor"),
        P("tensor", None),
        P("seq", "tensor"),
    )
    return jax.shard_map(
        body, mesh=mesh, in_specs=placed, out_specs=P("seq", "tensor"), check_vma=False
    )
```

```python
import functools
import math

import jax
import jax.numpy as jnp
from jax import lax
from jax.experimental import pallas as pl
from jax.experimental.pallas import tpu as pltpu
from jax.sharding import PartitionSpec as P

BLOCK = 64
ROWS = 16
VMEM = 48 * 2**20
F32 = jnp.float32
BF16 = jnp.bfloat16


def tables(first_index, second_index, length):
    phase = first_index * second_index % length
    angle = 2.0 * math.pi / length * phase.astype(F32)
    return (jnp.cos(angle), jnp.sin(angle))


def real_forward(values):
    n = len(values)
    if n == 2:
        return [(values[0] + values[1], None), (values[0] - values[1], None)]
    even, odd = real_forward(values[0::2]), real_forward(values[1::2])
    half = n // 2
    out = [None] * (half + 1)
    for p in range(half // 2 + 1):
        (er, ei), (dr, di) = even[p], odd[p]
        if p == 0:
            out[0], out[half] = (er + dr, None), (er - dr, None)
        elif 2 * p == half:
            out[p] = (er, -dr)
        else:
            c, s = math.cos(2 * math.pi * p / n), math.sin(2 * math.pi * p / n)
            tr, ti = dr * c + di * s, di * c - dr * s
            out[p], out[half - p] = (er + tr, ei + ti), (er - tr, ti - ei)
    return out


def real_inverse(freqs):
    half = len(freqs) - 1
    if half == 1:
        return [freqs[0][0] + freqs[1][0], freqs[0][0] - freqs[1][0]]
    n = 2 * half
    even, odd = [None] * (half // 2 + 1), [None] * (half // 2 + 1)
    for p in range(half // 2 + 1):
        (ar, ai), (br, bi) = freqs[p], freqs[half - p]
        if p == 0:
            even[0], odd[0] = (ar + br, None), (ar - br, None)
        elif 2 * p == half:
            even[p], odd[p] = (ar + ar, None), (-(ai + ai), None)
        else:
            c, s = math.cos(2 * math.pi * p / n), math.sin(2 * math.pi * p / n)
            dr, di = ar - br, ai + bi
            even[p], odd[p] = (ar + br, ai - bi), (dr * c - di * s, dr * s + di * c)
    out = [None] * n
    out[0::2], out[1::2] = real_inverse(even), real_inverse(odd)
    return out


def conv_kernel(twist_ref, ahead_ref, back_ref, x_ref, filter_ref, out_ref, first_ref, turned_ref):
    cycle, tokens, unit = x_ref.shape
    kept = filter_ref.shape[2] // 2
    per = max(1, 256 // unit)
    width = per * unit

    def twist(rows):
        block = twist_ref[rows, :]
        return [
            (block[:, p : p + 1], block[:, cycle + p : cycle + p + 1]) for p in range(cycle)
        ]

    def ahead(step, carry):
        start = pl.multiple_of(step * ROWS, ROWS)
        rows = pl.ds(start, ROWS)
        freqs = real_forward([x_ref[a, rows, :].astype(F32) for a in range(cycle)])
        for p, (c, s) in enumerate(twist(rows)):
            real, imaginary = freqs[min(p, cycle - p)]
            if imaginary is None:
                fr, fi = real * c, -(real * s)
            elif 2 * p > cycle:
                fr, fi = real * c - imaginary * s, -(imaginary * c + real * s)
            else:
                fr, fi = real * c + imaginary * s, imaginary * c - real * s
            lanes = slice(p * unit, (p + 1) * unit)
            first_ref[rows, lanes] = fr.astype(BF16)
            first_ref[pl.ds(tokens + start, ROWS), lanes] = fi.astype(BF16)
        return carry

    lax.fori_loop(0, tokens // ROWS, ahead, 0)

    def middle(step, carry):
        lanes = pl.ds(pl.multiple_of(step * width, width), width)
        spectrum = jnp.dot(ahead_ref[0], first_ref[:, lanes], preferred_element_type=F32)
        reals, imaginaries = [], []
        for u in range(per):
            part = filter_ref[step * per + u, 0].astype(F32)
            hr, hi = part[:kept], part[kept:]
            own = slice(u * unit, (u + 1) * unit)
            sr, si = spectrum[:kept, own], spectrum[kept:, own]
            reals.append(hr * sr - hi * si)
            imaginaries.append(hr * si + hi * sr)
        product = jnp.concatenate(
            [jnp.concatenate(reals, axis=1), jnp.concatenate(imaginaries, axis=1)], axis=0
        ).astype(BF16)
        turned_ref[:, lanes] = jnp.dot(back_ref[0], product, preferred_element_type=F32)
        return carry

    lax.fori_loop(0, cycle // per, middle, 0)

    def behind(step, carry):
        start = pl.multiple_of(step * ROWS, ROWS)
        rows = pl.ds(start, ROWS)
        parts = []
        for p, (c, s) in enumerate(twist(rows)):
            lanes = slice(p * unit, (p + 1) * unit)
            br = turned_ref[rows, lanes]
            bi = turned_ref[pl.ds(tokens + start, ROWS), lanes]
            parts.append(
                (
                    (br * c - bi * s).astype(BF16).astype(F32),
                    (br * s + bi * c).astype(BF16).astype(F32),
                )
            )
        half = cycle // 2
        freqs = [(parts[0][0] * 2.0, None)]
        for p in range(1, half):
            (ur, ui), (vr, vi) = parts[p], parts[cycle - p]
            freqs.append((ur + vr, ui - vi))
        freqs.append((parts[half][0] * 2.0, None))
        scale = 0.5 / (cycle * tokens)
        for a, value in enumerate(real_inverse(freqs)):
            out_ref[a, rows, :] = (value * scale).astype(BF16)
        return carry

    lax.fori_loop(0, tokens // ROWS, behind, 0)


def convolve(chunk, twist, ahead, back, signal, filters):
    cycle, tokens, unit = signal.shape
    kept = filters.shape[2] // 2
    flops = 4 * 2 * kept * 2 * tokens * cycle * unit
    return pl.pallas_call(
        conv_kernel,
        grid=(1,),
        out_shape=jax.ShapeDtypeStruct(signal.shape, BF16),
        in_specs=[
            pl.BlockSpec(twist.shape, lambda i: (0, 0)),
            pl.BlockSpec((1, *ahead.shape[1:]), lambda i: (chunk, 0, 0)),
            pl.BlockSpec((1, *back.shape[1:]), lambda i: (chunk, 0, 0)),
            pl.BlockSpec(signal.shape, lambda i: (0, 0, 0)),
            pl.BlockSpec((cycle, 1, 2 * kept, unit), lambda i: (0, chunk, 0, 0)),
        ],
        out_specs=pl.BlockSpec(signal.shape, lambda i: (0, 0, 0)),
        scratch_shapes=[
            pltpu.VMEM((2 * tokens, cycle * unit), BF16),
            pltpu.VMEM((2 * tokens, cycle * unit), F32),
        ],
        compiler_params=pltpu.CompilerParams(vmem_limit_bytes=VMEM),
        cost_estimate=pl.CostEstimate(
            flops=flops, bytes_accessed=16 * signal.size, transcendentals=0
        ),
        name="convolve",
    )(twist, ahead, back, signal, filters)


def pack_kernel(unit, x_ref, out_ref):
    for d in range(out_ref.shape[0]):
        out_ref[d] = x_ref[:, d * unit : (d + 1) * unit]


def pack_signal(keyval, chunk, cycle, unit):
    tokens = keyval.shape[0]
    wide = max(1, min(cycle, 512 // unit))
    steps = cycle // wide
    return pl.pallas_call(
        functools.partial(pack_kernel, unit),
        grid=(steps,),
        out_shape=jax.ShapeDtypeStruct((cycle, tokens, unit), BF16),
        in_specs=[pl.BlockSpec((tokens, wide * unit), lambda i: (0, chunk * steps + i))],
        out_specs=pl.BlockSpec((wide, tokens, unit), lambda i: (i, 0, 0)),
        compiler_params=pltpu.CompilerParams(vmem_limit_bytes=VMEM),
        cost_estimate=pl.CostEstimate(
            flops=0, bytes_accessed=4 * tokens * cycle * unit, transcendentals=0
        ),
        name="pack_signal",
    )(keyval)


def pack_filter_kernel(unit, f_ref, out_ref):
    for d in range(out_ref.shape[0]):
        out_ref[d, 0] = f_ref[:, 0, d * unit : (d + 1) * unit].astype(BF16)


def pack_filters(filter_values, cycle, chunks, unit):
    channels = filter_values.shape[-1]
    rows = filter_values.size // channels
    flat = filter_values.reshape(rows, 1, channels)
    wide = max(1, min(cycle, 512 // unit))
    steps = cycle // wide
    return pl.pallas_call(
        functools.partial(pack_filter_kernel, unit),
        grid=(chunks, steps),
        out_shape=jax.ShapeDtypeStruct((cycle, chunks, rows, unit), BF16),
        in_specs=[pl.BlockSpec((rows, 1, wide * unit), lambda g, i: (0, 0, g * steps + i))],
        out_specs=pl.BlockSpec((wide, 1, rows, unit), lambda g, i: (i, g, 0, 0)),
        compiler_params=pltpu.CompilerParams(vmem_limit_bytes=VMEM),
        cost_estimate=pl.CostEstimate(
            flops=0, bytes_accessed=6 * filter_values.size, transcendentals=0
        ),
        name="pack_filters",
    )(flat)


def gate_kernel(unit, c_ref, x_ref, g_ref, s_ref, out_ref):
    for d in range(c_ref.shape[0]):
        lanes = slice(d * unit, (d + 1) * unit)
        direct = s_ref[0:1, lanes] * x_ref[:, lanes].astype(F32)
        value = g_ref[:, lanes].astype(F32) * (c_ref[d].astype(F32) + direct)
        out_ref[:, lanes] = value.astype(BF16)


def gate(convolved, keyval, gating, skip_gain, chunk):
    cycle, tokens, unit = convolved.shape
    wide = max(1, min(cycle, 512 // unit))
    steps = cycle // wide
    lanes = wide * unit
    return pl.pallas_call(
        functools.partial(gate_kernel, unit),
        grid=(steps,),
        out_shape=jax.ShapeDtypeStruct((tokens, cycle * unit), BF16),
        in_specs=[
            pl.BlockSpec((wide, tokens, unit), lambda i: (i, 0, 0)),
            pl.BlockSpec((tokens, lanes), lambda i: (0, chunk * steps + i)),
            pl.BlockSpec((tokens, lanes), lambda i: (0, chunk * steps + i)),
            pl.BlockSpec((1, lanes), lambda i: (0, chunk * steps + i)),
        ],
        out_specs=pl.BlockSpec((tokens, lanes), lambda i: (0, i)),
        compiler_params=pltpu.CompilerParams(vmem_limit_bytes=VMEM),
        cost_estimate=pl.CostEstimate(
            flops=0, bytes_accessed=8 * convolved.size, transcendentals=0
        ),
        name="gate",
    )(convolved, keyval, gating, skip_gain.reshape(1, -1))


def mix_kernel(pieces, start_ref, *refs):
    w_ref, out_ref = refs[pieces], refs[-1]
    total = None
    for k in range(pieces):
        depth = refs[k].shape[1]
        start = pl.multiple_of(start_ref[k], depth)
        part = jnp.dot(
            refs[k][...], w_ref[pl.ds(start, depth), :], preferred_element_type=F32
        )
        total = part if total is None else total + part
    out_ref[...] = total.astype(BF16)


def mix(hidden, starts, weight, low, columns, result):
    tokens = hidden[0].shape[0]
    depth, part = weight.shape
    tile = min(256, part)
    first = low // tile
    pieces = len(hidden)
    before = [] if result is None else [result]
    return pl.pallas_call(
        functools.partial(mix_kernel, pieces),
        grid=(part // tile,),
        out_shape=jax.ShapeDtypeStruct((tokens, columns), BF16),
        in_specs=[pl.BlockSpec(memory_space=pltpu.SMEM)]
        + [pl.BlockSpec(h.shape, lambda i: (0, 0)) for h in hidden]
        + [pl.BlockSpec((depth, tile), lambda i: (0, i))]
        + [pl.BlockSpec(memory_space=pl.ANY) for _ in before],
        out_specs=pl.BlockSpec((tokens, tile), lambda i: (0, first + i)),
        input_output_aliases={pieces + 2: 0} if before else {},
        compiler_params=pltpu.CompilerParams(vmem_limit_bytes=VMEM),
        cost_estimate=pl.CostEstimate(
            flops=2 * tokens * depth * part, bytes_accessed=2 * depth * part, transcendentals=0
        ),
        name="mix",
    )(starts, *hidden, weight, *before)


def body(keyval, gating, skip_gain, filter_values, blocks, out_weight):
    cycle = lax.axis_size("seq")
    place = lax.axis_index("seq")
    peers = lax.axis_size("tensor")
    side = lax.axis_index("tensor")
    tokens, channels = keyval.shape
    repeat = BLOCK // cycle
    groups_local = blocks.shape[0]
    group_width = channels // groups_local
    narrow = channels // cycle
    unit = min(narrow, group_width)
    chunks = narrow // unit

    columns = out_weight.shape[1]
    eighth = columns // 8
    bounds = [0, 5 * eighth, columns] if eighth % 256 == 0 else [0, columns]
    weights = [
        lax.all_gather(out_weight[:, low:high], "seq", axis=0, tiled=True)
        for low, high in zip(bounds[:-1], bounds[1:])
    ]

    exchange = functools.partial(
        lax.all_to_all, axis_name="seq", split_axis=0, concat_axis=0, tiled=True
    )
    signals = [exchange(pack_signal(keyval, g, cycle, unit)) for g in range(chunks)]
    filters = exchange(pack_filters(filter_values, cycle, chunks, unit))

    group = (jnp.arange(chunks, dtype=jnp.int32) * cycle + place) * unit // group_width
    kept_blocks = jnp.take(blocks, group, axis=0)
    kept_rows = (
        kept_blocks[:, :, None] * repeat + jnp.arange(repeat, dtype=jnp.int32)
    ).reshape(chunks, -1)
    local_index = jnp.arange(tokens, dtype=jnp.int32)
    cosine, sine = tables(kept_rows[:, :, None], local_index[None, None, :], tokens)
    ahead = jnp.concatenate(
        [jnp.concatenate([cosine, sine], axis=2), jnp.concatenate([-sine, cosine], axis=2)],
        axis=1,
    ).astype(BF16)
    cosine, sine = tables(kept_rows[:, None, :], local_index[None, :, None], tokens)
    back = jnp.concatenate(
        [jnp.concatenate([cosine, -sine], axis=2), jnp.concatenate([sine, cosine], axis=2)],
        axis=1,
    ).astype(BF16)
    cycle_index = jnp.arange(cycle, dtype=jnp.int32)
    twist = jnp.concatenate(
        tables(local_index[:, None], cycle_index[None, :], cycle * tokens), axis=1
    )

    hidden, starts = [], []
    for g in range(chunks):
        done = exchange(convolve(g, twist, ahead, back, signals[g], filters))
        own = gate(done, keyval, gating, skip_gain, g)
        for shift in range(peers):
            if shift == 0:
                piece = own
            else:
                piece = lax.ppermute(
                    own, "tensor", [(t, (t + shift) % peers) for t in range(peers)]
                )
            hidden.append(piece)
            source = lax.rem(side + peers - shift, peers)
            starts.append(source * channels + g * cycle * unit)
    starts = jnp.stack(starts).astype(jnp.int32)
    result = None
    for low, weight in zip(bounds[:-1], weights):
        result = mix(hidden, starts, weight, low, columns, result)
    return result


def solution(mesh):
    placed = (
        P("seq", "tensor"),
        P("seq", "tensor"),
        P("tensor"),
        P(None, None, None, "seq", "tensor"),
        P("tensor", None),
        P("seq", "tensor"),
    )
    return jax.shard_map(
        body, mesh=mesh, in_specs=placed, out_specs=P("seq", "tensor"), check_vma=False
    )
```

```python
import functools
import math

import jax
import jax.numpy as jnp
from jax import lax
from jax.experimental import pallas as pl
from jax.experimental.pallas import tpu as pltpu
from jax.sharding import PartitionSpec as P

BLOCK = 64
ROWS = 16
VMEM = 48 * 2**20
F32 = jnp.float32
BF16 = jnp.bfloat16


def tables(first_index, second_index, length):
    phase = first_index * second_index % length
    angle = 2.0 * math.pi / length * phase.astype(F32)
    return (jnp.cos(angle), jnp.sin(angle))


def real_forward(values):
    n = len(values)
    if n == 2:
        return [(values[0] + values[1], None), (values[0] - values[1], None)]
    even, odd = real_forward(values[0::2]), real_forward(values[1::2])
    half = n // 2
    out = [None] * (half + 1)
    for p in range(half // 2 + 1):
        (er, ei), (dr, di) = even[p], odd[p]
        if p == 0:
            out[0], out[half] = (er + dr, None), (er - dr, None)
        elif 2 * p == half:
            out[p] = (er, -dr)
        else:
            c, s = math.cos(2 * math.pi * p / n), math.sin(2 * math.pi * p / n)
            tr, ti = dr * c + di * s, di * c - dr * s
            out[p], out[half - p] = (er + tr, ei + ti), (er - tr, ti - ei)
    return out


def real_inverse(freqs):
    half = len(freqs) - 1
    if half == 1:
        return [freqs[0][0] + freqs[1][0], freqs[0][0] - freqs[1][0]]
    n = 2 * half
    even, odd = [None] * (half // 2 + 1), [None] * (half // 2 + 1)
    for p in range(half // 2 + 1):
        (ar, ai), (br, bi) = freqs[p], freqs[half - p]
        if p == 0:
            even[0], odd[0] = (ar + br, None), (ar - br, None)
        elif 2 * p == half:
            even[p], odd[p] = (ar + ar, None), (-(ai + ai), None)
        else:
            c, s = math.cos(2 * math.pi * p / n), math.sin(2 * math.pi * p / n)
            dr, di = ar - br, ai + bi
            even[p], odd[p] = (ar + br, ai - bi), (dr * c - di * s, dr * s + di * c)
    out = [None] * n
    out[0::2], out[1::2] = real_inverse(even), real_inverse(odd)
    return out


def conv_kernel(twist_ref, ahead_ref, back_ref, x_ref, filter_ref, out_ref, first_ref, turned_ref):
    cycle, tokens, unit = x_ref.shape
    kept = filter_ref.shape[2] // 2
    per = max(1, 256 // unit)
    width = per * unit

    def twist(rows):
        block = twist_ref[rows, :]
        return [
            (block[:, p : p + 1], block[:, cycle + p : cycle + p + 1]) for p in range(cycle)
        ]

    def ahead(step, carry):
        start = pl.multiple_of(step * ROWS, ROWS)
        rows = pl.ds(start, ROWS)
        freqs = real_forward([x_ref[a, rows, :].astype(F32) for a in range(cycle)])
        for p, (c, s) in enumerate(twist(rows)):
            real, imaginary = freqs[min(p, cycle - p)]
            if imaginary is None:
                fr, fi = real * c, -(real * s)
            elif 2 * p > cycle:
                fr, fi = real * c - imaginary * s, -(imaginary * c + real * s)
            else:
                fr, fi = real * c + imaginary * s, imaginary * c - real * s
            lanes = slice(p * unit, (p + 1) * unit)
            first_ref[rows, lanes] = fr.astype(BF16)
            first_ref[pl.ds(tokens + start, ROWS), lanes] = fi.astype(BF16)
        return carry

    lax.fori_loop(0, tokens // ROWS, ahead, 0)

    def middle(step, carry):
        lanes = pl.ds(pl.multiple_of(step * width, width), width)
        spectrum = jnp.dot(ahead_ref[0], first_ref[:, lanes], preferred_element_type=F32)
        reals, imaginaries = [], []
        for u in range(per):
            part = filter_ref[step * per + u, 0].astype(F32)
            hr, hi = part[:kept], part[kept:]
            own = slice(u * unit, (u + 1) * unit)
            sr, si = spectrum[:kept, own], spectrum[kept:, own]
            reals.append(hr * sr - hi * si)
            imaginaries.append(hr * si + hi * sr)
        product = jnp.concatenate(
            [jnp.concatenate(reals, axis=1), jnp.concatenate(imaginaries, axis=1)], axis=0
        ).astype(BF16)
        turned_ref[:, lanes] = jnp.dot(back_ref[0], product, preferred_element_type=F32)
        return carry

    lax.fori_loop(0, cycle // per, middle, 0)

    def behind(step, carry):
        start = pl.multiple_of(step * ROWS, ROWS)
        rows = pl.ds(start, ROWS)
        parts = []
        for p, (c, s) in enumerate(twist(rows)):
            lanes = slice(p * unit, (p + 1) * unit)
            br = turned_ref[rows, lanes]
            bi = turned_ref[pl.ds(tokens + start, ROWS), lanes]
            parts.append(
                (
                    (br * c - bi * s).astype(BF16).astype(F32),
                    (br * s + bi * c).astype(BF16).astype(F32),
                )
            )
        half = cycle // 2
        freqs = [(parts[0][0] * 2.0, None)]
        for p in range(1, half):
            (ur, ui), (vr, vi) = parts[p], parts[cycle - p]
            freqs.append((ur + vr, ui - vi))
        freqs.append((parts[half][0] * 2.0, None))
        scale = 0.5 / (cycle * tokens)
        for a, value in enumerate(real_inverse(freqs)):
            out_ref[a, rows, :] = (value * scale).astype(BF16)
        return carry

    lax.fori_loop(0, tokens // ROWS, behind, 0)


def convolve(chunk, twist, ahead, back, signal, filters):
    cycle, tokens, unit = signal.shape
    kept = filters.shape[2] // 2
    flops = 4 * 2 * kept * 2 * tokens * cycle * unit
    return pl.pallas_call(
        conv_kernel,
        grid=(1,),
        out_shape=jax.ShapeDtypeStruct(signal.shape, BF16),
        in_specs=[
            pl.BlockSpec(twist.shape, lambda i: (0, 0)),
            pl.BlockSpec((1, *ahead.shape[1:]), lambda i: (chunk, 0, 0)),
            pl.BlockSpec((1, *back.shape[1:]), lambda i: (chunk, 0, 0)),
            pl.BlockSpec(signal.shape, lambda i: (0, 0, 0)),
            pl.BlockSpec((cycle, 1, 2 * kept, unit), lambda i: (0, chunk, 0, 0)),
        ],
        out_specs=pl.BlockSpec(signal.shape, lambda i: (0, 0, 0)),
        scratch_shapes=[
            pltpu.VMEM((2 * tokens, cycle * unit), BF16),
            pltpu.VMEM((2 * tokens, cycle * unit), F32),
        ],
        compiler_params=pltpu.CompilerParams(vmem_limit_bytes=VMEM),
        cost_estimate=pl.CostEstimate(
            flops=flops, bytes_accessed=16 * signal.size, transcendentals=0
        ),
        name="convolve",
    )(twist, ahead, back, signal, filters)


def pack_kernel(unit, x_ref, out_ref):
    for d in range(out_ref.shape[0]):
        out_ref[d] = x_ref[:, d * unit : (d + 1) * unit]


def pack_signal(keyval, chunk, cycle, unit):
    tokens = keyval.shape[0]
    wide = max(1, min(cycle, 512 // unit))
    steps = cycle // wide
    return pl.pallas_call(
        functools.partial(pack_kernel, unit),
        grid=(steps,),
        out_shape=jax.ShapeDtypeStruct((cycle, tokens, unit), BF16),
        in_specs=[pl.BlockSpec((tokens, wide * unit), lambda i: (0, chunk * steps + i))],
        out_specs=pl.BlockSpec((wide, tokens, unit), lambda i: (i, 0, 0)),
        compiler_params=pltpu.CompilerParams(vmem_limit_bytes=VMEM),
        cost_estimate=pl.CostEstimate(
            flops=0, bytes_accessed=4 * tokens * cycle * unit, transcendentals=0
        ),
        name="pack_signal",
    )(keyval)


def pack_filter_kernel(unit, f_ref, out_ref):
    for d in range(out_ref.shape[0]):
        out_ref[d, 0] = f_ref[:, 0, d * unit : (d + 1) * unit].astype(BF16)


def pack_filters(filter_values, cycle, chunks, unit):
    channels = filter_values.shape[-1]
    rows = filter_values.size // channels
    flat = filter_values.reshape(rows, 1, channels)
    wide = max(1, min(cycle, 512 // unit))
    steps = cycle // wide
    return pl.pallas_call(
        functools.partial(pack_filter_kernel, unit),
        grid=(chunks, steps),
        out_shape=jax.ShapeDtypeStruct((cycle, chunks, rows, unit), BF16),
        in_specs=[pl.BlockSpec((rows, 1, wide * unit), lambda g, i: (0, 0, g * steps + i))],
        out_specs=pl.BlockSpec((wide, 1, rows, unit), lambda g, i: (i, g, 0, 0)),
        compiler_params=pltpu.CompilerParams(vmem_limit_bytes=VMEM),
        cost_estimate=pl.CostEstimate(
            flops=0, bytes_accessed=6 * filter_values.size, transcendentals=0
        ),
        name="pack_filters",
    )(flat)


def gate_kernel(unit, c_ref, x_ref, g_ref, s_ref, out_ref):
    for d in range(c_ref.shape[0]):
        lanes = slice(d * unit, (d + 1) * unit)
        direct = s_ref[0:1, lanes] * x_ref[:, lanes].astype(F32)
        value = g_ref[:, lanes].astype(F32) * (c_ref[d].astype(F32) + direct)
        out_ref[:, lanes] = value.astype(BF16)


def gate(convolved, keyval, gating, skip_gain, chunk):
    cycle, tokens, unit = convolved.shape
    wide = max(1, min(cycle, 512 // unit))
    steps = cycle // wide
    lanes = wide * unit
    return pl.pallas_call(
        functools.partial(gate_kernel, unit),
        grid=(steps,),
        out_shape=jax.ShapeDtypeStruct((tokens, cycle * unit), BF16),
        in_specs=[
            pl.BlockSpec((wide, tokens, unit), lambda i: (i, 0, 0)),
            pl.BlockSpec((tokens, lanes), lambda i: (0, chunk * steps + i)),
            pl.BlockSpec((tokens, lanes), lambda i: (0, chunk * steps + i)),
            pl.BlockSpec((1, lanes), lambda i: (0, chunk * steps + i)),
        ],
        out_specs=pl.BlockSpec((tokens, lanes), lambda i: (0, i)),
        compiler_params=pltpu.CompilerParams(vmem_limit_bytes=VMEM),
        cost_estimate=pl.CostEstimate(
            flops=0, bytes_accessed=8 * convolved.size, transcendentals=0
        ),
        name="gate",
    )(convolved, keyval, gating, skip_gain.reshape(1, -1))


def mix_kernel(pieces, start_ref, *refs):
    w_ref, out_ref = refs[pieces], refs[-1]
    total = None
    for k in range(pieces):
        depth = refs[k].shape[1]
        start = pl.multiple_of(start_ref[k], depth)
        part = jnp.dot(
            refs[k][...], w_ref[pl.ds(start, depth), :], preferred_element_type=F32
        )
        total = part if total is None else total + part
    out_ref[...] = total.astype(BF16)


def mix(hidden, starts, weight, low, columns, result):
    tokens = hidden[0].shape[0]
    depth, part = weight.shape
    tile = min(256, part)
    first = low // tile
    pieces = len(hidden)
    before = [] if result is None else [result]
    return pl.pallas_call(
        functools.partial(mix_kernel, pieces),
        grid=(part // tile,),
        out_shape=jax.ShapeDtypeStruct((tokens, columns), BF16),
        in_specs=[pl.BlockSpec(memory_space=pltpu.SMEM)]
        + [pl.BlockSpec(memory_space=pltpu.VMEM) for h in hidden]
        + [pl.BlockSpec((depth, tile), lambda i: (0, i))]
        + [pl.BlockSpec(memory_space=pl.ANY) for _ in before],
        out_specs=pl.BlockSpec((tokens, tile), lambda i: (0, first + i)),
        input_output_aliases={pieces + 2: 0} if before else {},
        compiler_params=pltpu.CompilerParams(vmem_limit_bytes=32 * 2**20),
        cost_estimate=pl.CostEstimate(
            flops=2 * tokens * depth * part, bytes_accessed=2 * depth * part, transcendentals=0
        ),
        name="mix",
    )(starts, *hidden, weight, *before)


def body(keyval, gating, skip_gain, filter_values, blocks, out_weight):
    cycle = lax.axis_size("seq")
    place = lax.axis_index("seq")
    peers = lax.axis_size("tensor")
    side = lax.axis_index("tensor")
    tokens, channels = keyval.shape
    repeat = BLOCK // cycle
    groups_local = blocks.shape[0]
    group_width = channels // groups_local
    narrow = channels // cycle
    unit = min(narrow, group_width)
    chunks = narrow // unit

    columns = out_weight.shape[1]
    eighth = columns // 8
    bounds = [0, 5 * eighth, columns] if eighth % 256 == 0 else [0, columns]
    weights = [
        lax.all_gather(out_weight[:, low:high], "seq", axis=0, tiled=True)
        for low, high in zip(bounds[:-1], bounds[1:])
    ]

    exchange = functools.partial(
        lax.all_to_all, axis_name="seq", split_axis=0, concat_axis=0, tiled=True
    )
    signals = [exchange(pack_signal(keyval, g, cycle, unit)) for g in range(chunks)]
    filters = exchange(pack_filters(filter_values, cycle, chunks, unit))

    group = (jnp.arange(chunks, dtype=jnp.int32) * cycle + place) * unit // group_width
    kept_blocks = jnp.take(blocks, group, axis=0)
    kept_rows = (
        kept_blocks[:, :, None] * repeat + jnp.arange(repeat, dtype=jnp.int32)
    ).reshape(chunks, -1)
    local_index = jnp.arange(tokens, dtype=jnp.int32)
    cosine, sine = tables(kept_rows[:, :, None], local_index[None, None, :], tokens)
    ahead = jnp.concatenate(
        [jnp.concatenate([cosine, sine], axis=2), jnp.concatenate([-sine, cosine], axis=2)],
        axis=1,
    ).astype(BF16)
    cosine, sine = tables(kept_rows[:, None, :], local_index[None, :, None], tokens)
    back = jnp.concatenate(
        [jnp.concatenate([cosine, -sine], axis=2), jnp.concatenate([sine, cosine], axis=2)],
        axis=1,
    ).astype(BF16)
    cycle_index = jnp.arange(cycle, dtype=jnp.int32)
    twist = jnp.concatenate(
        tables(local_index[:, None], cycle_index[None, :], cycle * tokens), axis=1
    )

    hidden, starts = [], []
    for g in range(chunks):
        done = exchange(convolve(g, twist, ahead, back, signals[g], filters))
        own = gate(done, keyval, gating, skip_gain, g)
        for shift in range(peers):
            if shift == 0:
                piece = own
            else:
                piece = lax.ppermute(
                    own, "tensor", [(t, (t + shift) % peers) for t in range(peers)]
                )
            hidden.append(piece)
            source = lax.rem(side + peers - shift, peers)
            starts.append(source * channels + g * cycle * unit)
    starts = jnp.stack(starts).astype(jnp.int32)
    result = None
    for low, weight in zip(bounds[:-1], weights):
        result = mix(hidden, starts, weight, low, columns, result)
    return result


def solution(mesh):
    placed = (
        P("seq", "tensor"),
        P("seq", "tensor"),
        P("tensor"),
        P(None, None, None, "seq", "tensor"),
        P("tensor", None),
        P("seq", "tensor"),
    )
    return jax.shard_map(
        body, mesh=mesh, in_specs=placed, out_specs=P("seq", "tensor"), check_vma=False
    )
```

```python
import functools
import math

import jax
import jax.numpy as jnp
from jax import lax
from jax.experimental import pallas as pl
from jax.experimental.pallas import tpu as pltpu
from jax.sharding import PartitionSpec as P

BLOCK = 64
ROWS = 16
VMEM = 48 * 2**20
F32 = jnp.float32
BF16 = jnp.bfloat16


def tables(first_index, second_index, length):
    phase = first_index * second_index % length
    angle = 2.0 * math.pi / length * phase.astype(F32)
    return (jnp.cos(angle), jnp.sin(angle))


def real_forward(values):
    n = len(values)
    if n == 2:
        return [(values[0] + values[1], None), (values[0] - values[1], None)]
    even, odd = real_forward(values[0::2]), real_forward(values[1::2])
    half = n // 2
    out = [None] * (half + 1)
    for p in range(half // 2 + 1):
        (er, ei), (dr, di) = even[p], odd[p]
        if p == 0:
            out[0], out[half] = (er + dr, None), (er - dr, None)
        elif 2 * p == half:
            out[p] = (er, -dr)
        else:
            c, s = math.cos(2 * math.pi * p / n), math.sin(2 * math.pi * p / n)
            tr, ti = dr * c + di * s, di * c - dr * s
            out[p], out[half - p] = (er + tr, ei + ti), (er - tr, ti - ei)
    return out


def real_inverse(freqs):
    half = len(freqs) - 1
    if half == 1:
        return [freqs[0][0] + freqs[1][0], freqs[0][0] - freqs[1][0]]
    n = 2 * half
    even, odd = [None] * (half // 2 + 1), [None] * (half // 2 + 1)
    for p in range(half // 2 + 1):
        (ar, ai), (br, bi) = freqs[p], freqs[half - p]
        if p == 0:
            even[0], odd[0] = (ar + br, None), (ar - br, None)
        elif 2 * p == half:
            even[p], odd[p] = (ar + ar, None), (-(ai + ai), None)
        else:
            c, s = math.cos(2 * math.pi * p / n), math.sin(2 * math.pi * p / n)
            dr, di = ar - br, ai + bi
            even[p], odd[p] = (ar + br, ai - bi), (dr * c - di * s, dr * s + di * c)
    out = [None] * n
    out[0::2], out[1::2] = real_inverse(even), real_inverse(odd)
    return out


def conv_kernel(twist_ref, ahead_ref, back_ref, x_ref, filter_ref, out_ref, first_ref, turned_ref):
    cycle, tokens, unit = x_ref.shape
    kept = filter_ref.shape[2] // 2
    per = max(1, 256 // unit)
    width = per * unit

    def twist(rows):
        block = twist_ref[rows, :]
        return [
            (block[:, p : p + 1], block[:, cycle + p : cycle + p + 1]) for p in range(cycle)
        ]

    def ahead(step, carry):
        start = pl.multiple_of(step * ROWS, ROWS)
        rows = pl.ds(start, ROWS)
        freqs = real_forward([x_ref[a, rows, :].astype(F32) for a in range(cycle)])
        for p, (c, s) in enumerate(twist(rows)):
            real, imaginary = freqs[min(p, cycle - p)]
            if imaginary is None:
                fr, fi = real * c, -(real * s)
            elif 2 * p > cycle:
                fr, fi = real * c - imaginary * s, -(imaginary * c + real * s)
            else:
                fr, fi = real * c + imaginary * s, imaginary * c - real * s
            lanes = slice(p * unit, (p + 1) * unit)
            first_ref[rows, lanes] = fr.astype(BF16)
            first_ref[pl.ds(tokens + start, ROWS), lanes] = fi.astype(BF16)
        return carry

    lax.fori_loop(0, tokens // ROWS, ahead, 0)

    def middle(step, carry):
        lanes = pl.ds(pl.multiple_of(step * width, width), width)
        spectrum = jnp.dot(ahead_ref[0], first_ref[:, lanes], preferred_element_type=F32)
        reals, imaginaries = [], []
        for u in range(per):
            part = filter_ref[step * per + u, 0].astype(F32)
            hr, hi = part[:kept], part[kept:]
            own = slice(u * unit, (u + 1) * unit)
            sr, si = spectrum[:kept, own], spectrum[kept:, own]
            reals.append(hr * sr - hi * si)
            imaginaries.append(hr * si + hi * sr)
        product = jnp.concatenate(
            [jnp.concatenate(reals, axis=1), jnp.concatenate(imaginaries, axis=1)], axis=0
        ).astype(BF16)
        turned_ref[:, lanes] = jnp.dot(back_ref[0], product, preferred_element_type=F32)
        return carry

    lax.fori_loop(0, cycle // per, middle, 0)

    def behind(step, carry):
        start = pl.multiple_of(step * ROWS, ROWS)
        rows = pl.ds(start, ROWS)
        parts = []
        for p, (c, s) in enumerate(twist(rows)):
            lanes = slice(p * unit, (p + 1) * unit)
            br = turned_ref[rows, lanes]
            bi = turned_ref[pl.ds(tokens + start, ROWS), lanes]
            parts.append(
                (
                    (br * c - bi * s).astype(BF16).astype(F32),
                    (br * s + bi * c).astype(BF16).astype(F32),
                )
            )
        half = cycle // 2
        freqs = [(parts[0][0] * 2.0, None)]
        for p in range(1, half):
            (ur, ui), (vr, vi) = parts[p], parts[cycle - p]
            freqs.append((ur + vr, ui - vi))
        freqs.append((parts[half][0] * 2.0, None))
        scale = 0.5 / (cycle * tokens)
        for a, value in enumerate(real_inverse(freqs)):
            out_ref[a, rows, :] = (value * scale).astype(BF16)
        return carry

    lax.fori_loop(0, tokens // ROWS, behind, 0)


def convolve(chunk, twist, ahead, back, signal, filters):
    cycle, tokens, unit = signal.shape
    kept = filters.shape[2] // 2
    flops = 4 * 2 * kept * 2 * tokens * cycle * unit
    return pl.pallas_call(
        conv_kernel,
        grid=(1,),
        out_shape=jax.ShapeDtypeStruct(signal.shape, BF16),
        in_specs=[
            pl.BlockSpec(twist.shape, lambda i: (0, 0)),
            pl.BlockSpec((1, *ahead.shape[1:]), lambda i: (chunk, 0, 0)),
            pl.BlockSpec((1, *back.shape[1:]), lambda i: (chunk, 0, 0)),
            pl.BlockSpec(signal.shape, lambda i: (0, 0, 0)),
            pl.BlockSpec((cycle, 1, 2 * kept, unit), lambda i: (0, chunk, 0, 0)),
        ],
        out_specs=pl.BlockSpec(signal.shape, lambda i: (0, 0, 0)),
        scratch_shapes=[
            pltpu.VMEM((2 * tokens, cycle * unit), BF16),
            pltpu.VMEM((2 * tokens, cycle * unit), F32),
        ],
        compiler_params=pltpu.CompilerParams(vmem_limit_bytes=VMEM),
        cost_estimate=pl.CostEstimate(
            flops=flops, bytes_accessed=16 * signal.size, transcendentals=0
        ),
        name="convolve",
    )(twist, ahead, back, signal, filters)


def pack_kernel(unit, x_ref, out_ref):
    for d in range(out_ref.shape[0]):
        out_ref[d] = x_ref[:, d * unit : (d + 1) * unit]


def pack_signal(keyval, chunk, cycle, unit):
    tokens = keyval.shape[0]
    wide = max(1, min(cycle, 512 // unit))
    steps = cycle // wide
    return pl.pallas_call(
        functools.partial(pack_kernel, unit),
        grid=(steps,),
        out_shape=jax.ShapeDtypeStruct((cycle, tokens, unit), BF16),
        in_specs=[pl.BlockSpec((tokens, wide * unit), lambda i: (0, chunk * steps + i))],
        out_specs=pl.BlockSpec((wide, tokens, unit), lambda i: (i, 0, 0)),
        compiler_params=pltpu.CompilerParams(vmem_limit_bytes=VMEM),
        cost_estimate=pl.CostEstimate(
            flops=0, bytes_accessed=4 * tokens * cycle * unit, transcendentals=0
        ),
        name="pack_signal",
    )(keyval)


def pack_filter_kernel(unit, f_ref, out_ref):
    for d in range(out_ref.shape[0]):
        out_ref[d, 0] = f_ref[:, 0, d * unit : (d + 1) * unit].astype(BF16)


def pack_filters(filter_values, cycle, chunks, unit):
    channels = filter_values.shape[-1]
    rows = filter_values.size // channels
    flat = filter_values.reshape(rows, 1, channels)
    wide = max(1, min(cycle, 512 // unit))
    steps = cycle // wide
    return pl.pallas_call(
        functools.partial(pack_filter_kernel, unit),
        grid=(chunks, steps),
        out_shape=jax.ShapeDtypeStruct((cycle, chunks, rows, unit), BF16),
        in_specs=[pl.BlockSpec((rows, 1, wide * unit), lambda g, i: (0, 0, g * steps + i))],
        out_specs=pl.BlockSpec((wide, 1, rows, unit), lambda g, i: (i, g, 0, 0)),
        compiler_params=pltpu.CompilerParams(vmem_limit_bytes=VMEM),
        cost_estimate=pl.CostEstimate(
            flops=0, bytes_accessed=6 * filter_values.size, transcendentals=0
        ),
        name="pack_filters",
    )(flat)


def gate_kernel(unit, c_ref, x_ref, g_ref, s_ref, out_ref):
    for d in range(c_ref.shape[0]):
        lanes = slice(d * unit, (d + 1) * unit)
        direct = s_ref[0:1, lanes] * x_ref[:, lanes].astype(F32)
        value = g_ref[:, lanes].astype(F32) * (c_ref[d].astype(F32) + direct)
        out_ref[:, lanes] = value.astype(BF16)


def gate(convolved, keyval, gating, skip_gain, chunk):
    cycle, tokens, unit = convolved.shape
    wide = max(1, min(cycle, 512 // unit))
    steps = cycle // wide
    lanes = wide * unit
    return pl.pallas_call(
        functools.partial(gate_kernel, unit),
        grid=(steps,),
        out_shape=jax.ShapeDtypeStruct((tokens, cycle * unit), BF16),
        in_specs=[
            pl.BlockSpec((wide, tokens, unit), lambda i: (i, 0, 0)),
            pl.BlockSpec((tokens, lanes), lambda i: (0, chunk * steps + i)),
            pl.BlockSpec((tokens, lanes), lambda i: (0, chunk * steps + i)),
            pl.BlockSpec((1, lanes), lambda i: (0, chunk * steps + i)),
        ],
        out_specs=pl.BlockSpec((tokens, lanes), lambda i: (0, i)),
        compiler_params=pltpu.CompilerParams(vmem_limit_bytes=VMEM),
        cost_estimate=pl.CostEstimate(
            flops=0, bytes_accessed=8 * convolved.size, transcendentals=0
        ),
        name="gate",
    )(convolved, keyval, gating, skip_gain.reshape(1, -1))


def mix_kernel(pieces, start_ref, *refs):
    w_ref, out_ref = refs[pieces], refs[-1]
    total = None
    for k in range(pieces):
        depth = refs[k].shape[1]
        start = pl.multiple_of(start_ref[k], depth)
        part = jnp.dot(
            refs[k][...], w_ref[pl.ds(start, depth), :], preferred_element_type=F32
        )
        total = part if total is None else total + part
    out_ref[...] = total.astype(BF16)


def mix(hidden, starts, weight, low, columns, result):
    tokens = hidden[0].shape[0]
    depth, part = weight.shape
    tile = min(512, part)
    first = low // tile
    pieces = len(hidden)
    before = [] if result is None else [result]
    return pl.pallas_call(
        functools.partial(mix_kernel, pieces),
        grid=(part // tile,),
        out_shape=jax.ShapeDtypeStruct((tokens, columns), BF16),
        in_specs=[pl.BlockSpec(memory_space=pltpu.SMEM)]
        + [pl.BlockSpec(memory_space=pltpu.VMEM) for h in hidden]
        + [pl.BlockSpec((depth, tile), lambda i: (0, i))]
        + [pl.BlockSpec(memory_space=pl.ANY) for _ in before],
        out_specs=pl.BlockSpec((tokens, tile), lambda i: (0, first + i)),
        input_output_aliases={pieces + 2: 0} if before else {},
        compiler_params=pltpu.CompilerParams(vmem_limit_bytes=40 * 2**20),
        cost_estimate=pl.CostEstimate(
            flops=2 * tokens * depth * part, bytes_accessed=2 * depth * part, transcendentals=0
        ),
        name="mix",
    )(starts, *hidden, weight, *before)


def body(keyval, gating, skip_gain, filter_values, blocks, out_weight):
    cycle = lax.axis_size("seq")
    place = lax.axis_index("seq")
    peers = lax.axis_size("tensor")
    side = lax.axis_index("tensor")
    tokens, channels = keyval.shape
    repeat = BLOCK // cycle
    groups_local = blocks.shape[0]
    group_width = channels // groups_local
    narrow = channels // cycle
    unit = min(narrow, group_width)
    chunks = narrow // unit

    columns = out_weight.shape[1]
    eighth = columns // 8
    bounds = [0, 5 * eighth, columns] if eighth % 256 == 0 else [0, columns]
    weights = [
        lax.all_gather(out_weight[:, low:high], "seq", axis=0, tiled=True)
        for low, high in zip(bounds[:-1], bounds[1:])
    ]

    exchange = functools.partial(
        lax.all_to_all, axis_name="seq", split_axis=0, concat_axis=0, tiled=True
    )
    signals = [exchange(pack_signal(keyval, g, cycle, unit)) for g in range(chunks)]
    filters = exchange(pack_filters(filter_values, cycle, chunks, unit))

    group = (jnp.arange(chunks, dtype=jnp.int32) * cycle + place) * unit // group_width
    kept_blocks = jnp.take(blocks, group, axis=0)
    kept_rows = (
        kept_blocks[:, :, None] * repeat + jnp.arange(repeat, dtype=jnp.int32)
    ).reshape(chunks, -1)
    local_index = jnp.arange(tokens, dtype=jnp.int32)
    cosine, sine = tables(kept_rows[:, :, None], local_index[None, None, :], tokens)
    ahead = jnp.concatenate(
        [jnp.concatenate([cosine, sine], axis=2), jnp.concatenate([-sine, cosine], axis=2)],
        axis=1,
    ).astype(BF16)
    cosine, sine = tables(kept_rows[:, None, :], local_index[None, :, None], tokens)
    back = jnp.concatenate(
        [jnp.concatenate([cosine, -sine], axis=2), jnp.concatenate([sine, cosine], axis=2)],
        axis=1,
    ).astype(BF16)
    cycle_index = jnp.arange(cycle, dtype=jnp.int32)
    twist = jnp.concatenate(
        tables(local_index[:, None], cycle_index[None, :], cycle * tokens), axis=1
    )

    hidden, starts = [], []
    for g in range(chunks):
        done = exchange(convolve(g, twist, ahead, back, signals[g], filters))
        own = gate(done, keyval, gating, skip_gain, g)
        for shift in range(peers):
            if shift == 0:
                piece = own
            else:
                piece = lax.ppermute(
                    own, "tensor", [(t, (t + shift) % peers) for t in range(peers)]
                )
            hidden.append(piece)
            source = lax.rem(side + peers - shift, peers)
            starts.append(source * channels + g * cycle * unit)
    starts = jnp.stack(starts).astype(jnp.int32)
    result = None
    for low, weight in zip(bounds[:-1], weights):
        result = mix(hidden, starts, weight, low, columns, result)
    return result


def solution(mesh):
    placed = (
        P("seq", "tensor"),
        P("seq", "tensor"),
        P("tensor"),
        P(None, None, None, "seq", "tensor"),
        P("tensor", None),
        P("seq", "tensor"),
    )
    return jax.shard_map(
        body, mesh=mesh, in_specs=placed, out_specs=P("seq", "tensor"), check_vma=False
    )
```

```python
import functools
import math

import jax
import jax.numpy as jnp
from jax import lax
from jax.experimental import pallas as pl
from jax.experimental.pallas import tpu as pltpu
from jax.sharding import PartitionSpec as P

BLOCK = 64
ROWS = 16
VMEM = 48 * 2**20
F32 = jnp.float32
BF16 = jnp.bfloat16


def tables(first_index, second_index, length):
    phase = first_index * second_index % length
    angle = 2.0 * math.pi / length * phase.astype(F32)
    return (jnp.cos(angle), jnp.sin(angle))


def real_forward(values):
    n = len(values)
    if n == 2:
        return [(values[0] + values[1], None), (values[0] - values[1], None)]
    even, odd = real_forward(values[0::2]), real_forward(values[1::2])
    half = n // 2
    out = [None] * (half + 1)
    for p in range(half // 2 + 1):
        (er, ei), (dr, di) = even[p], odd[p]
        if p == 0:
            out[0], out[half] = (er + dr, None), (er - dr, None)
        elif 2 * p == half:
            out[p] = (er, -dr)
        else:
            c, s = math.cos(2 * math.pi * p / n), math.sin(2 * math.pi * p / n)
            tr, ti = dr * c + di * s, di * c - dr * s
            out[p], out[half - p] = (er + tr, ei + ti), (er - tr, ti - ei)
    return out


def real_inverse(freqs):
    half = len(freqs) - 1
    if half == 1:
        return [freqs[0][0] + freqs[1][0], freqs[0][0] - freqs[1][0]]
    n = 2 * half
    even, odd = [None] * (half // 2 + 1), [None] * (half // 2 + 1)
    for p in range(half // 2 + 1):
        (ar, ai), (br, bi) = freqs[p], freqs[half - p]
        if p == 0:
            even[0], odd[0] = (ar + br, None), (ar - br, None)
        elif 2 * p == half:
            even[p], odd[p] = (ar + ar, None), (-(ai + ai), None)
        else:
            c, s = math.cos(2 * math.pi * p / n), math.sin(2 * math.pi * p / n)
            dr, di = ar - br, ai + bi
            even[p], odd[p] = (ar + br, ai - bi), (dr * c - di * s, dr * s + di * c)
    out = [None] * n
    out[0::2], out[1::2] = real_inverse(even), real_inverse(odd)
    return out


def conv_kernel(twist_ref, ahead_ref, back_ref, x_ref, filter_ref, out_ref, first_ref, turned_ref):
    cycle, tokens, unit = x_ref.shape
    kept = filter_ref.shape[2] // 2
    per = max(1, 256 // unit)
    width = per * unit

    def twist(rows):
        block = twist_ref[rows, :]
        return [
            (block[:, p : p + 1], block[:, cycle + p : cycle + p + 1]) for p in range(cycle)
        ]

    def ahead(step, carry):
        start = pl.multiple_of(step * ROWS, ROWS)
        rows = pl.ds(start, ROWS)
        freqs = real_forward([x_ref[a, rows, :].astype(F32) for a in range(cycle)])
        for p, (c, s) in enumerate(twist(rows)):
            real, imaginary = freqs[min(p, cycle - p)]
            if imaginary is None:
                fr, fi = real * c, -(real * s)
            elif 2 * p > cycle:
                fr, fi = real * c - imaginary * s, -(imaginary * c + real * s)
            else:
                fr, fi = real * c + imaginary * s, imaginary * c - real * s
            lanes = slice(p * unit, (p + 1) * unit)
            first_ref[rows, lanes] = fr.astype(BF16)
            first_ref[pl.ds(tokens + start, ROWS), lanes] = fi.astype(BF16)
        return carry

    lax.fori_loop(0, tokens // ROWS, ahead, 0)

    def middle(step, carry):
        lanes = pl.ds(pl.multiple_of(step * width, width), width)
        spectrum = jnp.dot(ahead_ref[0], first_ref[:, lanes], preferred_element_type=F32)
        reals, imaginaries = [], []
        for u in range(per):
            part = filter_ref[step * per + u, 0].astype(F32)
            hr, hi = part[:kept], part[kept:]
            own = slice(u * unit, (u + 1) * unit)
            sr, si = spectrum[:kept, own], spectrum[kept:, own]
            reals.append(hr * sr - hi * si)
            imaginaries.append(hr * si + hi * sr)
        product = jnp.concatenate(
            [jnp.concatenate(reals, axis=1), jnp.concatenate(imaginaries, axis=1)], axis=0
        ).astype(BF16)
        turned_ref[:, lanes] = jnp.dot(back_ref[0], product, preferred_element_type=F32)
        return carry

    lax.fori_loop(0, cycle // per, middle, 0)

    def behind(step, carry):
        start = pl.multiple_of(step * ROWS, ROWS)
        rows = pl.ds(start, ROWS)
        parts = []
        for p, (c, s) in enumerate(twist(rows)):
            lanes = slice(p * unit, (p + 1) * unit)
            br = turned_ref[rows, lanes]
            bi = turned_ref[pl.ds(tokens + start, ROWS), lanes]
            parts.append(
                (
                    (br * c - bi * s).astype(BF16).astype(F32),
                    (br * s + bi * c).astype(BF16).astype(F32),
                )
            )
        half = cycle // 2
        freqs = [(parts[0][0] * 2.0, None)]
        for p in range(1, half):
            (ur, ui), (vr, vi) = parts[p], parts[cycle - p]
            freqs.append((ur + vr, ui - vi))
        freqs.append((parts[half][0] * 2.0, None))
        scale = 0.5 / (cycle * tokens)
        for a, value in enumerate(real_inverse(freqs)):
            out_ref[a, rows, :] = (value * scale).astype(BF16)
        return carry

    lax.fori_loop(0, tokens // ROWS, behind, 0)


def convolve(chunk, twist, ahead, back, signal, filters):
    cycle, tokens, unit = signal.shape
    kept = filters.shape[2] // 2
    flops = 4 * 2 * kept * 2 * tokens * cycle * unit
    return pl.pallas_call(
        conv_kernel,
        grid=(1,),
        out_shape=jax.ShapeDtypeStruct(signal.shape, BF16),
        in_specs=[
            pl.BlockSpec(twist.shape, lambda i: (0, 0)),
            pl.BlockSpec((1, *ahead.shape[1:]), lambda i: (chunk, 0, 0)),
            pl.BlockSpec((1, *back.shape[1:]), lambda i: (chunk, 0, 0)),
            pl.BlockSpec(signal.shape, lambda i: (0, 0, 0)),
            pl.BlockSpec((cycle, 1, 2 * kept, unit), lambda i: (0, chunk, 0, 0)),
        ],
        out_specs=pl.BlockSpec(signal.shape, lambda i: (0, 0, 0)),
        scratch_shapes=[
            pltpu.VMEM((2 * tokens, cycle * unit), BF16),
            pltpu.VMEM((2 * tokens, cycle * unit), F32),
        ],
        compiler_params=pltpu.CompilerParams(vmem_limit_bytes=VMEM),
        cost_estimate=pl.CostEstimate(
            flops=flops, bytes_accessed=16 * signal.size, transcendentals=0
        ),
        name="convolve",
    )(twist, ahead, back, signal, filters)


def pack_kernel(unit, x_ref, out_ref):
    for d in range(out_ref.shape[0]):
        out_ref[d] = x_ref[:, d * unit : (d + 1) * unit]


def pack_signal(keyval, chunk, cycle, unit):
    tokens = keyval.shape[0]
    wide = max(1, min(cycle, 512 // unit))
    steps = cycle // wide
    return pl.pallas_call(
        functools.partial(pack_kernel, unit),
        grid=(steps,),
        out_shape=jax.ShapeDtypeStruct((cycle, tokens, unit), BF16),
        in_specs=[pl.BlockSpec((tokens, wide * unit), lambda i: (0, chunk * steps + i))],
        out_specs=pl.BlockSpec((wide, tokens, unit), lambda i: (i, 0, 0)),
        compiler_params=pltpu.CompilerParams(vmem_limit_bytes=VMEM),
        cost_estimate=pl.CostEstimate(
            flops=0, bytes_accessed=4 * tokens * cycle * unit, transcendentals=0
        ),
        name="pack_signal",
    )(keyval)


def pack_filter_kernel(unit, f_ref, out_ref):
    for d in range(out_ref.shape[0]):
        out_ref[d, 0] = f_ref[:, 0, d * unit : (d + 1) * unit].astype(BF16)


def pack_filters(filter_values, cycle, chunks, unit):
    channels = filter_values.shape[-1]
    rows = filter_values.size // channels
    flat = filter_values.reshape(rows, 1, channels)
    wide = max(1, min(cycle, 512 // unit))
    steps = cycle // wide
    return pl.pallas_call(
        functools.partial(pack_filter_kernel, unit),
        grid=(chunks, steps),
        out_shape=jax.ShapeDtypeStruct((cycle, chunks, rows, unit), BF16),
        in_specs=[pl.BlockSpec((rows, 1, wide * unit), lambda g, i: (0, 0, g * steps + i))],
        out_specs=pl.BlockSpec((wide, 1, rows, unit), lambda g, i: (i, g, 0, 0)),
        compiler_params=pltpu.CompilerParams(vmem_limit_bytes=VMEM),
        cost_estimate=pl.CostEstimate(
            flops=0, bytes_accessed=6 * filter_values.size, transcendentals=0
        ),
        name="pack_filters",
    )(flat)


def gate_kernel(unit, c_ref, x_ref, g_ref, s_ref, out_ref):
    for d in range(c_ref.shape[0]):
        lanes = slice(d * unit, (d + 1) * unit)
        direct = s_ref[0:1, lanes] * x_ref[:, lanes].astype(F32)
        value = g_ref[:, lanes].astype(F32) * (c_ref[d].astype(F32) + direct)
        out_ref[:, lanes] = value.astype(BF16)


def gate(convolved, keyval, gating, skip_gain, chunk):
    cycle, tokens, unit = convolved.shape
    wide = max(1, min(cycle, 512 // unit))
    steps = cycle // wide
    lanes = wide * unit
    return pl.pallas_call(
        functools.partial(gate_kernel, unit),
        grid=(steps,),
        out_shape=jax.ShapeDtypeStruct((tokens, cycle * unit), BF16),
        in_specs=[
            pl.BlockSpec((wide, tokens, unit), lambda i: (i, 0, 0)),
            pl.BlockSpec((tokens, lanes), lambda i: (0, chunk * steps + i)),
            pl.BlockSpec((tokens, lanes), lambda i: (0, chunk * steps + i)),
            pl.BlockSpec((1, lanes), lambda i: (0, chunk * steps + i)),
        ],
        out_specs=pl.BlockSpec((tokens, lanes), lambda i: (0, i)),
        compiler_params=pltpu.CompilerParams(vmem_limit_bytes=VMEM),
        cost_estimate=pl.CostEstimate(
            flops=0, bytes_accessed=8 * convolved.size, transcendentals=0
        ),
        name="gate",
    )(convolved, keyval, gating, skip_gain.reshape(1, -1))


def mix_kernel(pieces, start_ref, *refs):
    w_ref, out_ref = refs[pieces], refs[-1]
    total = None
    for k in range(pieces):
        depth = refs[k].shape[1]
        start = pl.multiple_of(start_ref[k], depth)
        part = jnp.dot(
            refs[k][...], w_ref[pl.ds(start, depth), :], preferred_element_type=F32
        )
        total = part if total is None else total + part
    out_ref[...] = total.astype(BF16)


def mix(hidden, starts, weight, low, columns, result):
    tokens = hidden[0].shape[0]
    depth, part = weight.shape
    tile = min(256, part)
    first = low // tile
    pieces = len(hidden)
    before = [] if result is None else [result]
    return pl.pallas_call(
        functools.partial(mix_kernel, pieces),
        grid=(part // tile,),
        out_shape=jax.ShapeDtypeStruct((tokens, columns), BF16),
        in_specs=[pl.BlockSpec(memory_space=pltpu.SMEM)]
        + [pl.BlockSpec(h.shape, lambda i: (0, 0)) for h in hidden]
        + [pl.BlockSpec((depth, tile), lambda i: (0, i))]
        + [pl.BlockSpec(memory_space=pl.ANY) for _ in before],
        out_specs=pl.BlockSpec((tokens, tile), lambda i: (0, first + i)),
        input_output_aliases={pieces + 2: 0} if before else {},
        compiler_params=pltpu.CompilerParams(vmem_limit_bytes=VMEM),
        cost_estimate=pl.CostEstimate(
            flops=2 * tokens * depth * part, bytes_accessed=2 * depth * part, transcendentals=0
        ),
        name="mix",
    )(starts, *hidden, weight, *before)


def body(keyval, gating, skip_gain, filter_values, blocks, out_weight):
    cycle = lax.axis_size("seq")
    place = lax.axis_index("seq")
    peers = lax.axis_size("tensor")
    side = lax.axis_index("tensor")
    tokens, channels = keyval.shape
    repeat = BLOCK // cycle
    groups_local = blocks.shape[0]
    group_width = channels // groups_local
    narrow = channels // cycle
    unit = min(narrow, group_width)
    chunks = narrow // unit

    columns = out_weight.shape[1]
    eighth = columns // 8
    bounds = [0, eighth, 5 * eighth, columns] if eighth % 256 == 0 else [0, columns]
    weights = [
        lax.all_gather(out_weight[:, low:high], "seq", axis=0, tiled=True)
        for low, high in zip(bounds[:-1], bounds[1:])
    ]

    exchange = functools.partial(
        lax.all_to_all, axis_name="seq", split_axis=0, concat_axis=0, tiled=True
    )
    signals = [exchange(pack_signal(keyval, g, cycle, unit)) for g in range(chunks)]
    filters = exchange(pack_filters(filter_values, cycle, chunks, unit))

    group = (jnp.arange(chunks, dtype=jnp.int32) * cycle + place) * unit // group_width
    kept_blocks = jnp.take(blocks, group, axis=0)
    kept_rows = (
        kept_blocks[:, :, None] * repeat + jnp.arange(repeat, dtype=jnp.int32)
    ).reshape(chunks, -1)
    local_index = jnp.arange(tokens, dtype=jnp.int32)
    cosine, sine = tables(kept_rows[:, :, None], local_index[None, None, :], tokens)
    ahead = jnp.concatenate(
        [jnp.concatenate([cosine, sine], axis=2), jnp.concatenate([-sine, cosine], axis=2)],
        axis=1,
    ).astype(BF16)
    cosine, sine = tables(kept_rows[:, None, :], local_index[None, :, None], tokens)
    back = jnp.concatenate(
        [jnp.concatenate([cosine, -sine], axis=2), jnp.concatenate([sine, cosine], axis=2)],
        axis=1,
    ).astype(BF16)
    cycle_index = jnp.arange(cycle, dtype=jnp.int32)
    twist = jnp.concatenate(
        tables(local_index[:, None], cycle_index[None, :], cycle * tokens), axis=1
    )

    hidden, starts = [], []
    for g in range(chunks):
        done = exchange(convolve(g, twist, ahead, back, signals[g], filters))
        own = gate(done, keyval, gating, skip_gain, g)
        for shift in range(peers):
            if shift == 0:
                piece = own
            else:
                piece = lax.ppermute(
                    own, "tensor", [(t, (t + shift) % peers) for t in range(peers)]
                )
            hidden.append(piece)
            source = lax.rem(side + peers - shift, peers)
            starts.append(source * channels + g * cycle * unit)
    starts = jnp.stack(starts).astype(jnp.int32)
    result = None
    for low, weight in zip(bounds[:-1], weights):
        result = mix(hidden, starts, weight, low, columns, result)
    return result


def solution(mesh):
    placed = (
        P("seq", "tensor"),
        P("seq", "tensor"),
        P("tensor"),
        P(None, None, None, "seq", "tensor"),
        P("tensor", None),
        P("seq", "tensor"),
    )
    return jax.shard_map(
        body, mesh=mesh, in_specs=placed, out_specs=P("seq", "tensor"), check_vma=False
    )
```

```python
import functools
import math

import jax
import jax.numpy as jnp
from jax import lax
from jax.experimental import pallas as pl
from jax.experimental.pallas import tpu as pltpu
from jax.sharding import PartitionSpec as P

BLOCK = 64
ROWS = 16
VMEM = 48 * 2**20
F32 = jnp.float32
BF16 = jnp.bfloat16


def tables(first_index, second_index, length):
    phase = first_index * second_index % length
    angle = 2.0 * math.pi / length * phase.astype(F32)
    return (jnp.cos(angle), jnp.sin(angle))


def real_forward(values):
    n = len(values)
    if n == 2:
        return [(values[0] + values[1], None), (values[0] - values[1], None)]
    even, odd = real_forward(values[0::2]), real_forward(values[1::2])
    half = n // 2
    out = [None] * (half + 1)
    for p in range(half // 2 + 1):
        (er, ei), (dr, di) = even[p], odd[p]
        if p == 0:
            out[0], out[half] = (er + dr, None), (er - dr, None)
        elif 2 * p == half:
            out[p] = (er, -dr)
        else:
            c, s = math.cos(2 * math.pi * p / n), math.sin(2 * math.pi * p / n)
            tr, ti = dr * c + di * s, di * c - dr * s
            out[p], out[half - p] = (er + tr, ei + ti), (er - tr, ti - ei)
    return out


def real_inverse(freqs):
    half = len(freqs) - 1
    if half == 1:
        return [freqs[0][0] + freqs[1][0], freqs[0][0] - freqs[1][0]]
    n = 2 * half
    even, odd = [None] * (half // 2 + 1), [None] * (half // 2 + 1)
    for p in range(half // 2 + 1):
        (ar, ai), (br, bi) = freqs[p], freqs[half - p]
        if p == 0:
            even[0], odd[0] = (ar + br, None), (ar - br, None)
        elif 2 * p == half:
            even[p], odd[p] = (ar + ar, None), (-(ai + ai), None)
        else:
            c, s = math.cos(2 * math.pi * p / n), math.sin(2 * math.pi * p / n)
            dr, di = ar - br, ai + bi
            even[p], odd[p] = (ar + br, ai - bi), (dr * c - di * s, dr * s + di * c)
    out = [None] * n
    out[0::2], out[1::2] = real_inverse(even), real_inverse(odd)
    return out


def conv_kernel(twist_ref, ahead_ref, back_ref, x_ref, filter_ref, out_ref, first_ref, turned_ref):
    cycle, tokens, unit = x_ref.shape
    kept = filter_ref.shape[2] // 2
    per = max(1, 256 // unit)
    width = per * unit

    def twist(rows):
        block = twist_ref[rows, :]
        return [
            (block[:, p : p + 1], block[:, cycle + p : cycle + p + 1]) for p in range(cycle)
        ]

    def ahead(step, carry):
        start = pl.multiple_of(step * ROWS, ROWS)
        rows = pl.ds(start, ROWS)
        freqs = real_forward([x_ref[a, rows, :].astype(F32) for a in range(cycle)])
        for p, (c, s) in enumerate(twist(rows)):
            real, imaginary = freqs[min(p, cycle - p)]
            if imaginary is None:
                fr, fi = real * c, -(real * s)
            elif 2 * p > cycle:
                fr, fi = real * c - imaginary * s, -(imaginary * c + real * s)
            else:
                fr, fi = real * c + imaginary * s, imaginary * c - real * s
            lanes = slice(p * unit, (p + 1) * unit)
            first_ref[rows, lanes] = fr.astype(BF16)
            first_ref[pl.ds(tokens + start, ROWS), lanes] = fi.astype(BF16)
        return carry

    lax.fori_loop(0, tokens // ROWS, ahead, 0)

    def middle(step, carry):
        lanes = pl.ds(pl.multiple_of(step * width, width), width)
        spectrum = jnp.dot(ahead_ref[0], first_ref[:, lanes], preferred_element_type=F32)
        reals, imaginaries = [], []
        for u in range(per):
            part = filter_ref[step * per + u, 0].astype(F32)
            hr, hi = part[:kept], part[kept:]
            own = slice(u * unit, (u + 1) * unit)
            sr, si = spectrum[:kept, own], spectrum[kept:, own]
            reals.append(hr * sr - hi * si)
            imaginaries.append(hr * si + hi * sr)
        product = jnp.concatenate(
            [jnp.concatenate(reals, axis=1), jnp.concatenate(imaginaries, axis=1)], axis=0
        ).astype(BF16)
        turned_ref[:, lanes] = jnp.dot(back_ref[0], product, preferred_element_type=F32)
        return carry

    lax.fori_loop(0, cycle // per, middle, 0)

    def behind(step, carry):
        start = pl.multiple_of(step * ROWS, ROWS)
        rows = pl.ds(start, ROWS)
        parts = []
        for p, (c, s) in enumerate(twist(rows)):
            lanes = slice(p * unit, (p + 1) * unit)
            br = turned_ref[rows, lanes]
            bi = turned_ref[pl.ds(tokens + start, ROWS), lanes]
            parts.append(
                (
                    (br * c - bi * s).astype(BF16).astype(F32),
                    (br * s + bi * c).astype(BF16).astype(F32),
                )
            )
        half = cycle // 2
        freqs = [(parts[0][0] * 2.0, None)]
        for p in range(1, half):
            (ur, ui), (vr, vi) = parts[p], parts[cycle - p]
            freqs.append((ur + vr, ui - vi))
        freqs.append((parts[half][0] * 2.0, None))
        scale = 0.5 / (cycle * tokens)
        for a, value in enumerate(real_inverse(freqs)):
            out_ref[a, rows, :] = (value * scale).astype(BF16)
        return carry

    lax.fori_loop(0, tokens // ROWS, behind, 0)


def convolve(chunk, twist, ahead, back, signal, filters):
    cycle, tokens, unit = signal.shape
    kept = filters.shape[2] // 2
    flops = 4 * 2 * kept * 2 * tokens * cycle * unit
    return pl.pallas_call(
        conv_kernel,
        grid=(1,),
        out_shape=jax.ShapeDtypeStruct(signal.shape, BF16),
        in_specs=[
            pl.BlockSpec(twist.shape, lambda i: (0, 0)),
            pl.BlockSpec((1, *ahead.shape[1:]), lambda i: (chunk, 0, 0)),
            pl.BlockSpec((1, *back.shape[1:]), lambda i: (chunk, 0, 0)),
            pl.BlockSpec(signal.shape, lambda i: (0, 0, 0)),
            pl.BlockSpec((cycle, 1, 2 * kept, unit), lambda i: (0, chunk, 0, 0)),
        ],
        out_specs=pl.BlockSpec(signal.shape, lambda i: (0, 0, 0)),
        scratch_shapes=[
            pltpu.VMEM((2 * tokens, cycle * unit), BF16),
            pltpu.VMEM((2 * tokens, cycle * unit), F32),
        ],
        compiler_params=pltpu.CompilerParams(vmem_limit_bytes=VMEM),
        cost_estimate=pl.CostEstimate(
            flops=flops, bytes_accessed=16 * signal.size, transcendentals=0
        ),
        name="convolve",
    )(twist, ahead, back, signal, filters)


def pack_kernel(unit, x_ref, out_ref):
    for d in range(out_ref.shape[0]):
        out_ref[d] = x_ref[:, d * unit : (d + 1) * unit]


def pack_signal(keyval, chunk, cycle, unit):
    tokens = keyval.shape[0]
    wide = max(1, min(cycle, 512 // unit))
    steps = cycle // wide
    return pl.pallas_call(
        functools.partial(pack_kernel, unit),
        grid=(steps,),
        out_shape=jax.ShapeDtypeStruct((cycle, tokens, unit), BF16),
        in_specs=[pl.BlockSpec((tokens, wide * unit), lambda i: (0, chunk * steps + i))],
        out_specs=pl.BlockSpec((wide, tokens, unit), lambda i: (i, 0, 0)),
        compiler_params=pltpu.CompilerParams(vmem_limit_bytes=VMEM),
        cost_estimate=pl.CostEstimate(
            flops=0, bytes_accessed=4 * tokens * cycle * unit, transcendentals=0
        ),
        name="pack_signal",
    )(keyval)


def pack_filter_kernel(unit, f_ref, out_ref):
    for d in range(out_ref.shape[0]):
        out_ref[d, 0] = f_ref[:, 0, d * unit : (d + 1) * unit].astype(BF16)


def pack_filters(filter_values, cycle, chunks, unit):
    channels = filter_values.shape[-1]
    rows = filter_values.size // channels
    flat = filter_values.reshape(rows, 1, channels)
    wide = max(1, min(cycle, 512 // unit))
    steps = cycle // wide
    return pl.pallas_call(
        functools.partial(pack_filter_kernel, unit),
        grid=(chunks, steps),
        out_shape=jax.ShapeDtypeStruct((cycle, chunks, rows, unit), BF16),
        in_specs=[pl.BlockSpec((rows, 1, wide * unit), lambda g, i: (0, 0, g * steps + i))],
        out_specs=pl.BlockSpec((wide, 1, rows, unit), lambda g, i: (i, g, 0, 0)),
        compiler_params=pltpu.CompilerParams(vmem_limit_bytes=VMEM),
        cost_estimate=pl.CostEstimate(
            flops=0, bytes_accessed=6 * filter_values.size, transcendentals=0
        ),
        name="pack_filters",
    )(flat)


def gate_kernel(unit, c_ref, x_ref, g_ref, s_ref, out_ref):
    for d in range(c_ref.shape[0]):
        lanes = slice(d * unit, (d + 1) * unit)
        direct = s_ref[0:1, lanes] * x_ref[:, lanes].astype(F32)
        value = g_ref[:, lanes].astype(F32) * (c_ref[d].astype(F32) + direct)
        out_ref[:, lanes] = value.astype(BF16)


def gate(convolved, keyval, gating, skip_gain, chunk):
    cycle, tokens, unit = convolved.shape
    wide = max(1, min(cycle, 512 // unit))
    steps = cycle // wide
    lanes = wide * unit
    return pl.pallas_call(
        functools.partial(gate_kernel, unit),
        grid=(steps,),
        out_shape=jax.ShapeDtypeStruct((tokens, cycle * unit), BF16),
        in_specs=[
            pl.BlockSpec((wide, tokens, unit), lambda i: (i, 0, 0)),
            pl.BlockSpec((tokens, lanes), lambda i: (0, chunk * steps + i)),
            pl.BlockSpec((tokens, lanes), lambda i: (0, chunk * steps + i)),
            pl.BlockSpec((1, lanes), lambda i: (0, chunk * steps + i)),
        ],
        out_specs=pl.BlockSpec((tokens, lanes), lambda i: (0, i)),
        compiler_params=pltpu.CompilerParams(vmem_limit_bytes=VMEM),
        cost_estimate=pl.CostEstimate(
            flops=0, bytes_accessed=8 * convolved.size, transcendentals=0
        ),
        name="gate",
    )(convolved, keyval, gating, skip_gain.reshape(1, -1))


def mix_kernel(pieces, start_ref, *refs):
    w_ref, out_ref = refs[pieces], refs[-1]
    total = None
    for k in range(pieces):
        depth = refs[k].shape[1]
        start = pl.multiple_of(start_ref[k], depth)
        part = jnp.dot(
            refs[k][...], w_ref[pl.ds(start, depth), :], preferred_element_type=F32
        )
        total = part if total is None else total + part
    out_ref[...] = total.astype(BF16)


def mix(hidden, starts, weight, low, columns, result):
    tokens = hidden[0].shape[0]
    depth, part = weight.shape
    tile = min(256, part)
    first = low // tile
    pieces = len(hidden)
    before = [] if result is None else [result]
    return pl.pallas_call(
        functools.partial(mix_kernel, pieces),
        grid=(part // tile,),
        out_shape=jax.ShapeDtypeStruct((tokens, columns), BF16),
        in_specs=[pl.BlockSpec(memory_space=pltpu.SMEM)]
        + [pl.BlockSpec(h.shape, lambda i: (0, 0)) for h in hidden]
        + [pl.BlockSpec((depth, tile), lambda i: (0, i))]
        + [pl.BlockSpec(memory_space=pl.ANY) for _ in before],
        out_specs=pl.BlockSpec((tokens, tile), lambda i: (0, first + i)),
        input_output_aliases={pieces + 2: 0} if before else {},
        compiler_params=pltpu.CompilerParams(vmem_limit_bytes=VMEM),
        cost_estimate=pl.CostEstimate(
            flops=2 * tokens * depth * part, bytes_accessed=2 * depth * part, transcendentals=0
        ),
        name="mix",
    )(starts, *hidden, weight, *before)


def body(keyval, gating, skip_gain, filter_values, blocks, out_weight):
    cycle = lax.axis_size("seq")
    place = lax.axis_index("seq")
    peers = lax.axis_size("tensor")
    side = lax.axis_index("tensor")
    tokens, channels = keyval.shape
    repeat = BLOCK // cycle
    groups_local = blocks.shape[0]
    group_width = channels // groups_local
    narrow = channels // cycle
    unit = min(narrow, group_width)
    chunks = narrow // unit

    columns = out_weight.shape[1]
    eighth = columns // 8
    bounds = [0, 9 * (eighth // 2), columns] if eighth % 512 == 0 else [0, columns]
    weights = [
        lax.all_gather(out_weight[:, low:high], "seq", axis=0, tiled=True)
        for low, high in zip(bounds[:-1], bounds[1:])
    ]

    exchange = functools.partial(
        lax.all_to_all, axis_name="seq", split_axis=0, concat_axis=0, tiled=True
    )
    signals = [exchange(pack_signal(keyval, g, cycle, unit)) for g in range(chunks)]
    filters = exchange(pack_filters(filter_values, cycle, chunks, unit))

    group = (jnp.arange(chunks, dtype=jnp.int32) * cycle + place) * unit // group_width
    kept_blocks = jnp.take(blocks, group, axis=0)
    kept_rows = (
        kept_blocks[:, :, None] * repeat + jnp.arange(repeat, dtype=jnp.int32)
    ).reshape(chunks, -1)
    local_index = jnp.arange(tokens, dtype=jnp.int32)
    cosine, sine = tables(kept_rows[:, :, None], local_index[None, None, :], tokens)
    ahead = jnp.concatenate(
        [jnp.concatenate([cosine, sine], axis=2), jnp.concatenate([-sine, cosine], axis=2)],
        axis=1,
    ).astype(BF16)
    cosine, sine = tables(kept_rows[:, None, :], local_index[None, :, None], tokens)
    back = jnp.concatenate(
        [jnp.concatenate([cosine, -sine], axis=2), jnp.concatenate([sine, cosine], axis=2)],
        axis=1,
    ).astype(BF16)
    cycle_index = jnp.arange(cycle, dtype=jnp.int32)
    twist = jnp.concatenate(
        tables(local_index[:, None], cycle_index[None, :], cycle * tokens), axis=1
    )

    hidden, starts = [], []
    for g in range(chunks):
        done = exchange(convolve(g, twist, ahead, back, signals[g], filters))
        own = gate(done, keyval, gating, skip_gain, g)
        for shift in range(peers):
            if shift == 0:
                piece = own
            else:
                piece = lax.ppermute(
                    own, "tensor", [(t, (t + shift) % peers) for t in range(peers)]
                )
            hidden.append(piece)
            source = lax.rem(side + peers - shift, peers)
            starts.append(source * channels + g * cycle * unit)
    starts = jnp.stack(starts).astype(jnp.int32)
    result = None
    for low, weight in zip(bounds[:-1], weights):
        result = mix(hidden, starts, weight, low, columns, result)
    return result


def solution(mesh):
    placed = (
        P("seq", "tensor"),
        P("seq", "tensor"),
        P("tensor"),
        P(None, None, None, "seq", "tensor"),
        P("tensor", None),
        P("seq", "tensor"),
    )
    return jax.shard_map(
        body, mesh=mesh, in_specs=placed, out_specs=P("seq", "tensor"), check_vma=False
    )
```
